256 devices in a mesh: ctx: 64 (over y, z, core), head: 4 (over x).
Axes of the slice: x: 4, y: 4, z: 8, core: 2. Of those that a mesh axis runs over, the one named last changes fastest.
Arguments:
- normed_layer_input: bfloat16 [8192, 4096], P('ctx', 'head'), may hold values from -6 to 6
- mix: float32 [4096], P('head'), may hold values from 0.1 to 0.9
- paired_down_weight: bfloat16 [4096, 256], P('head'), may hold values from -0.09375 to 0.09375
- decay_up_weight: bfloat16 [128, 4096], P(None, 'head'), may hold values from -2 to 2
- rate_up_weight: bfloat16 [128, 4096], P(None, 'head'), may hold values from -1 to 1
- decay_bias: float32 [4096], P('head'), may hold values from -13 to -2.5
- rate_bias: float32 [4096], P('head'), may hold values from -11 to 1
- recept: bfloat16 [8192, 4096], P('ctx', 'head'), may hold values from -6 to 6
- key: bfloat16 [8192, 4096], P('ctx', 'head'), may hold values from -6 to 6
- value: bfloat16 [8192, 4096], P('ctx', 'head'), may hold values from -6 to 6
- window_state_start: float32 [64, 64, 64], P('head'), may hold values from -160 to 160
Outputs:
- mixed_out: bfloat16 [8192, 4096], P('ctx', 'head')
The draws below stay inside these ranges and needn't reach their ends.
All inputs are finite; a program needn't handle non-finite values.
Results may differ from the reference program's by a relative error of at most 0.0025.
Values may be sent and summed in bfloat16 or wider, within the bound.
A program may use at most 192 MiB of HBM per device.

```python
import jax
import jax.numpy as jnp
from jax import lax

MODEL_WIDTH = 4096
HEADS = 64
LOW_RANK_SIZE = 128
HEAD_SIZE = 64
TOK_DEV = 128
TOKENS = 8192
N_CTX = 64


def pick_slow(key, count):
    order = jax.random.permutation(key, HEADS)
    return jnp.repeat(order < count, HEAD_SIZE)


def draw_decay_bias(key, part):
    count = HEADS // 2
    slow = pick_slow(key, count)
    key = jax.random.fold_in(key, 11)
    low = jax.random.uniform(key, (MODEL_WIDTH,), jnp.float32, -13.0, -11.5)
    high = jax.random.uniform(jax.random.fold_in(key, 1), (MODEL_WIDTH,), jnp.float32, -4.0, -2.5)
    return jnp.where(slow, low, high)


def draw_rate_bias(key, part):
    count = HEADS // 2
    slow = pick_slow(key, count)
    key = jax.random.fold_in(key, 17)
    low = jax.random.uniform(key, (MODEL_WIDTH,), jnp.float32, -11.0, -9.0)
    high = jax.random.uniform(jax.random.fold_in(key, 1), (MODEL_WIDTH,), jnp.float32, -1.0, 1.0)
    return jnp.where(slow, low, high)


def draw_window_state_start(key, part):
    key = jax.random.fold_in(key, 23)
    scale = TOKENS // 256 + 8
    values = jnp.clip(jax.random.normal(key, (HEADS, HEAD_SIZE, HEAD_SIZE), jnp.float32), -4.0, 4.0)
    return values * scale


def shard_levels(stream_key, dims, pieces, low, top_value):
    gain = 1.0
    for axis_at, parts in pieces:
        steps = jax.random.uniform(jax.random.fold_in(jax.random.fold_in(stream_key, 6), axis_at), (parts,), jnp.float32, low / len(pieces), top_value / len(pieces))
        gain = gain * jnp.repeat(jnp.exp(steps), dims[axis_at] // parts).reshape((-1,) + (1,) * (len(dims) - 1 - axis_at))
    return gain


def noise(key, extent, width, reach, pieces=(), dtype=jnp.bfloat16):
    array = width * jax.random.normal(key, extent, jnp.float32)
    if pieces:
        array = array * shard_levels(key, extent, pieces, -0.22, 0.18)
    return jnp.clip(array, -reach, reach).astype(dtype)


def setup_inputs(seed: int = 0) -> dict:
    streams_of = jax.random.split(jax.random.key(seed), 12)
    return {
        "normed_layer_input": noise(streams_of[0], (TOKENS, MODEL_WIDTH), 1.0, 6.0, ((0, 64), (1, 4))),
        "mix": jnp.clip(0.1 + 0.79999997 * jax.random.uniform(streams_of[1], (MODEL_WIDTH,), jnp.float32) ** shard_levels(streams_of[1], (MODEL_WIDTH,), ((0, 4),), -0.2, 0.2), 0.1, 0.9),
        "paired_down_weight": noise(streams_of[2], (MODEL_WIDTH, 2 * LOW_RANK_SIZE), MODEL_WIDTH ** -0.5, 0.09375, ((0, 4),)),
        "decay_up_weight": noise(streams_of[3], (LOW_RANK_SIZE, MODEL_WIDTH), (LOW_RANK_SIZE // 16) ** -0.5, 2.0, ((1, 4),)),
        "rate_up_weight": noise(streams_of[4], (LOW_RANK_SIZE, MODEL_WIDTH), (LOW_RANK_SIZE // 4) ** -0.5, 1.0, ((1, 4),)),
        "decay_bias": draw_decay_bias(jax.random.fold_in(streams_of[11], 71), 0),
        "rate_bias": draw_rate_bias(jax.random.fold_in(streams_of[11], 71), 0),
        "recept": noise(streams_of[7], (TOKENS, MODEL_WIDTH), 1.0, 6.0, ((0, 64), (1, 4))),
        "key": noise(streams_of[8], (TOKENS, MODEL_WIDTH), 1.0, 6.0, ((0, 64), (1, 4))),
        "value": noise(streams_of[9], (TOKENS, MODEL_WIDTH), 1.0, 6.0, ((0, 64), (1, 4))),
        "window_state_start": draw_window_state_start(jax.random.fold_in(streams_of[11], 71), 0),
    }


def reduced_projection(token_shifted, paired_down_weight, decay_up_weight, rate_up_weight, decay_bias, rate_bias):
    grand_total = jnp.dot(token_shifted, paired_down_weight, preferred_element_type=jnp.float32)
    hidden = jnp.concatenate([jnp.tanh(grand_total[:, :LOW_RANK_SIZE]), grand_total[:, LOW_RANK_SIZE:]], axis=1).astype(jnp.bfloat16)
    decay_logarithm = -0.606531 * jax.nn.sigmoid(decay_bias + jnp.dot(hidden[:, :LOW_RANK_SIZE], decay_up_weight, preferred_element_type=jnp.float32))
    learning_rate_value = jax.nn.sigmoid(rate_bias + jnp.dot(hidden[:, LOW_RANK_SIZE:], rate_up_weight, preferred_element_type=jnp.float32))
    return (decay_logarithm, learning_rate_value)

def token_step(state, inputs):
    decay_logarithm, removal, direction, keys, values, queries = inputs
    along = jnp.einsum('hj,hji->hi', direction, state, precision=lax.Precision.HIGHEST)
    state = jnp.exp(decay_logarithm)[:, :, None] * state - removal[:, :, None] * along[:, None, :] + keys[:, :, None] * values[:, None, :]
    output = jnp.einsum('hj,hji->hi', queries, state, precision=lax.Precision.HIGHEST)
    return (state, output)

def group_norm(read):
    mean = lax.optimization_barrier(jnp.mean(read, axis=-1, keepdims=True))
    centered = read - mean
    var = lax.optimization_barrier(jnp.mean(centered * centered, axis=-1, keepdims=True))
    return (centered / jnp.sqrt(var + 0.00064)).astype(jnp.bfloat16)

def reference(normed_layer_input, mix, paired_down_weight, decay_up_weight, rate_up_weight, decay_bias, rate_bias, recept, key, value, window_state_start):

    def block_step(carry, inputs):
        state, last = carry
        x_blk, r_blk, k_blk, v_blk = inputs
        rows = x_blk.shape[0]
        before = jnp.concatenate([last[None, :], x_blk[:-1]], axis=0)
        xf = x_blk.astype(jnp.float32)
        token_shifted = (xf + (before.astype(jnp.float32) - xf) * mix).astype(jnp.bfloat16)
        decay_logarithm, learning_rate_value = reduced_projection(token_shifted, paired_down_weight, decay_up_weight, rate_up_weight, decay_bias, rate_bias)
        shape3 = (rows, HEADS, HEAD_SIZE)
        kf = k_blk.astype(jnp.float32).reshape(shape3)
        direction = kf / jnp.sqrt(lax.optimization_barrier(jnp.sum(kf * kf, axis=-1, keepdims=True)) + 1e-06)
        removal = learning_rate_value.reshape(shape3) * direction
        seq = (decay_logarithm.reshape(shape3), removal, direction, kf, v_blk.astype(jnp.float32).reshape(shape3), r_blk.astype(jnp.float32).reshape(shape3))
        state, reads = lax.scan(token_step, state, seq)
        return ((state, x_blk[rows - 1]), group_norm(reads).reshape(rows, MODEL_WIDTH))
    inputs = (normed_layer_input.reshape(N_CTX, TOK_DEV, MODEL_WIDTH), recept.reshape(N_CTX, TOK_DEV, MODEL_WIDTH), key.reshape(N_CTX, TOK_DEV, MODEL_WIDTH), value.reshape(N_CTX, TOK_DEV, MODEL_WIDTH))
    start = (window_state_start.astype(jnp.float32), jnp.zeros((MODEL_WIDTH,), jnp.bfloat16))
    final, outs = lax.scan(block_step, start, inputs)
    return outs.reshape(TOKENS, MODEL_WIDTH)
```

```python
import functools
import jax
import jax.numpy as jnp
from jax import lax
from jax.experimental import pallas as pl
from jax.experimental.pallas import tpu as pltpu

F32 = jnp.float32
BF16 = jnp.bfloat16
NN = (((1,), (0,)), ((), ()))
NT = (((1,), (1,)), ((), ()))


def dot(a, b, dims=NN):
    return lax.dot_general(a, b, dims, preferred_element_type=F32)


def split(x):
    high = x.astype(BF16)
    return high, (x - high.astype(F32)).astype(BF16)


def cat(parts, axis):
    return jnp.concatenate(parts, axis=axis)


def mm(a, b):
    ah, al = split(a)
    bh, bl = split(b)
    side = cat([bh, bl], 1)
    both = dot(cat([ah, al], 1), cat([side, side], 0))
    n = b.shape[1]
    return both[:, :n] + both[:, n:]


def mm3(a, b):
    ah, al = split(a)
    bh, bl = split(b)
    return dot(cat([ah, al], 1), cat([bh, bh], 0)) + dot(ah, bl)


def iota(shape, axis):
    return lax.broadcasted_iota(jnp.int32, shape, axis)


def chunk_kernel(hid, du, ru, db, rb, rec, key, val, mu_out, reff_out, base_out, *, pairs):
    T = hid.shape[0]
    row, col = iota((T, T), 0), iota((T, T), 1)
    tri = (row >= col).astype(BF16)
    half = (row // 64 == col // 64).astype(BF16)
    eye = (row == col).astype(F32)
    first = iota((T, 128), 1) < 64
    first2 = cat([first, first], 1)
    hd, hr = hid[:, :128], hid[:, 128:]
    tri2, half2 = cat([tri, tri], 1), cat([half, half], 0)
    P = range(pairs)
    H = range(2 * pairs)
    at = [slice(128 * p, 128 * p + 128) for p in P]

    logd = [-0.606531 * jax.nn.sigmoid(dot(hd, du[:, at[p]]) + db[:, at[p]]) for p in P]
    rate = [jax.nn.sigmoid(dot(hr, ru[:, at[p]]) + rb[:, at[p]]) for p in P]
    cum = []
    for p in P:
        l1, rest = split(logd[p])
        r1 = logd[p] - l1.astype(F32)
        l3 = (r1 - rest.astype(F32)).astype(BF16)
        cum.append(dot(tri2, cat([l1, rest], 0)) + dot(tri, l3))
    kf = [key[:, at[p]].astype(F32) for p in P]
    square = [dot(cat(split(kf[p] * kf[p]), 1), half2) for p in P]
    direction = [kf[p] * lax.rsqrt(square[p] + 1e-06) for p in P]
    mid = [cum[p][63:64] for p in P]
    last = [cum[p][T - 1 :] for p in P]
    e_in = [jnp.exp(cum[p] - mid[p]) for p in P]
    e_prior = [jnp.exp(cum[p] - logd[p] - mid[p]) for p in P]
    e_out = [jnp.exp(mid[p] - cum[p]) for p in P]
    dir_in = [direction[p] * e_prior[p] for p in P]
    read_in = [rec[:, at[p]].astype(F32) * e_in[p] for p in P]
    key_out = [kf[p] * e_out[p] for p in P]
    rem_out = [rate[p] * direction[p] * e_out[p] for p in P]
    e_mid = [jnp.exp(mid[p]) for p in P]
    e_end = [jnp.exp(last[p] - mid[p]) for p in P]
    e_all = [jnp.exp(last[p]) for p in P]

    scores = []
    zero = jnp.zeros((2 * T, 128), BF16)
    keep = cat([first, first], 0)
    for p in P:
        xh, xl = split(cat([dir_in[p], read_in[p]], 0))
        yh, yl = split(cat([key_out[p], rem_out[p]], 0))
        yhh = cat([yh, yh], 1)
        for side in (0, 1):
            pick = keep if side == 0 else jnp.logical_not(keep)
            xhs, xls = jnp.where(pick, xh, zero), jnp.where(pick, xl, zero)
            scores.append(dot(cat([xhs, xls], 1), yhh, NT) + dot(xhs, yl, NT))
    strict = row > col
    upto = row >= col
    a_kk = [jnp.where(strict, scores[h][:T, :T], 0.0) for h in H]
    low = [jnp.where(strict, scores[h][:T, T:], 0.0) for h in H]
    a_rk = [jnp.where(upto, scores[h][T:, :T], 0.0) for h in H]
    a_rb = [jnp.where(upto, scores[h][T:, T:], 0.0) for h in H]

    block = row // 8 == col // 8
    d = [jnp.where(block, low[h], 0.0) for h in H]
    d2 = [mm(d[h], d[h]) for h in H]
    dd = [mm(cat([d[h], d2[h]], 0), d2[h]) for h in H]
    poly = [eye - d[h] + d2[h] - dd[h][:T] for h in H]
    inv = [poly[h] + mm(poly[h], dd[h][T:]) for h in H]
    size = 8
    while size < T:
        pair_mask = (row // (2 * size) == col // (2 * size)) & (row // size > col // size)
        step = [mm(jnp.where(pair_mask, low[h], 0.0), inv[h]) for h in H]
        inv = [inv[h] - mm(inv[h], step[h]) for h in H]
        size *= 2

    vals = [val[:, at[p]] for p in P]
    kv = [dot(cat(split(a_kk[h]), 1), cat([vals[h // 2]] * 2, 0)) for h in H]
    right = [
        cat([dir_in[p] * e_mid[p], jnp.where(first, kv[2 * p], kv[2 * p + 1])], 1) for p in P
    ]
    sol = [mm3(inv[h], right[h // 2]) for h in H]
    solved = [jnp.where(first2, sol[2 * p], sol[2 * p + 1]) for p in P]
    for p in P:
        wide = cat([solved[p], cat([jnp.zeros((T, 128), F32), vals[p].astype(F32)], 1)], 0)
        ends = cat([-rem_out[p] * e_end[p], key_out[p] * e_end[p]], 0).T
        left = cat(
            [ends] + [cat([-a_rb[2 * p + s], a_rk[2 * p + s]], 1) for s in (0, 1)], 0
        )
        lh, ll = split(left)
        wh, wl = split(wide)
        out = dot(lh, wh) + dot(lh, wl) + dot(ll, wh)
        maps = out[:T]
        trans = maps[:, :128] + eye * e_all[p]
        added = maps[:, 128:]
        low_lane = iota((64, 128), 1) < 64
        mu_out[2 * p] = jnp.where(low_lane, trans[:64], pltpu.roll(added[:64], 64, 1))
        mu_out[2 * p + 1] = jnp.where(low_lane, pltpu.roll(trans[64:], 64, 1), added[64:])
        reads = jnp.where(first2, out[T : 2 * T], out[2 * T :])
        reff_out[:, at[p]] = read_in[p] * e_mid[p] + reads[:, :128]
        base_out[:, at[p]] = reads[:, 128:]


def chunk(hid, du, ru, db, rb, rec, key, val, pairs=2):
    T, width = rec.shape
    heads = width // 64
    w = 128 * pairs
    grid = (width // w,)
    cols = lambda i: (0, i)
    return pl.pallas_call(
        functools.partial(chunk_kernel, pairs=pairs),
        grid=grid,
        in_specs=[
            pl.BlockSpec((T, 256), lambda i: (0, 0)),
            pl.BlockSpec((128, w), cols),
            pl.BlockSpec((128, w), cols),
            pl.BlockSpec((1, w), cols),
            pl.BlockSpec((1, w), cols),
            pl.BlockSpec((T, w), cols),
            pl.BlockSpec((T, w), cols),
            pl.BlockSpec((T, w), cols),
        ],
        out_specs=[
            pl.BlockSpec((2 * pairs, 64, 128), lambda i: (i, 0, 0)),
            pl.BlockSpec((T, w), cols),
            pl.BlockSpec((T, w), cols),
        ],
        out_shape=[
            jax.ShapeDtypeStruct((heads, 64, 128), F32),
            jax.ShapeDtypeStruct((T, width), F32),
            jax.ShapeDtypeStruct((T, width), F32),
        ],
        compiler_params=pltpu.CompilerParams(vmem_limit_bytes=48 * 1024 * 1024),
    )(hid, du, ru, db, rb, rec, key, val)


MESH = pl.DeviceIdType.MESH


def hidden_kernel(
    x_ref, mix_ref, down_ref, out_ref,
    tail, total, shares, hidden, sends, recvs, *, nctx, nhead,
):
    ctx, head = lax.axis_index("ctx"), lax.axis_index("head")
    after, behind = lax.rem(ctx + 1, nctx), lax.rem(ctx + nctx - 1, nctx)
    T, width = x_ref.shape
    share = T // nhead
    barrier = pltpu.get_barrier_semaphore()
    for other in (after, behind):
        pl.semaphore_signal(barrier, inc=1, device_id={"ctx": other}, device_id_type=MESH)
    mates = [lax.rem(head + step, nhead) for step in range(1, nhead)]
    for mate in mates:
        pl.semaphore_signal(barrier, inc=1, device_id={"head": mate}, device_id_type=MESH)
    pl.semaphore_wait(barrier, 1 + nhead)

    shift = pltpu.make_async_remote_copy(
        src_ref=x_ref.at[pl.ds(T - 16, 16)],
        dst_ref=tail,
        send_sem=sends.at[0],
        recv_sem=recvs.at[0],
        device_id={"ctx": after},
        device_id_type=MESH,
    )
    shift.start()
    mix = mix_ref[...]
    xf = x_ref[...].astype(F32)
    before = pltpu.roll(xf, 1, 0)
    shifted = (xf + (before - xf) * mix).astype(BF16)
    total[...] = dot(shifted, down_ref[...])
    shift.wait()
    xt = x_ref[0:16, :].astype(F32)
    edge = jnp.where(ctx > 0, tail[...].astype(F32)[15:16], 0.0)
    before = jnp.where(iota((16, width), 0) == 0, edge, pltpu.roll(xt, 1, 0))
    shifted = (xt + (before - xt) * mix).astype(BF16)
    total[0:16, :] = dot(shifted, down_ref[...])

    copies = []
    for step, mate in enumerate(mates):
        copy = pltpu.make_async_remote_copy(
            src_ref=total.at[pl.ds(pl.multiple_of(mate * share, share), share)],
            dst_ref=shares.at[step],
            send_sem=sends.at[1 + step],
            recv_sem=recvs.at[1 + step],
            device_id={"head": mate},
            device_id_type=MESH,
        )
        copy.start()
        copies.append(copy)
    mine = pl.ds(pl.multiple_of(head * share, share), share)
    grand = total[mine, :]
    for step, copy in enumerate(copies):
        copy.wait_recv()
        grand = grand + shares[step]
    hidden[mine, :] = cat([jnp.tanh(grand[:, :128]), grand[:, 128:]], 1).astype(BF16)
    spread = []
    for step, mate in enumerate(mates):
        copy = pltpu.make_async_remote_copy(
            src_ref=hidden.at[mine],
            dst_ref=hidden.at[mine],
            send_sem=sends.at[nhead + step],
            recv_sem=recvs.at[nhead + step],
            device_id={"head": mate},
            device_id_type=MESH,
        )
        copy.start()
        spread.append(copy)
    for copy in copies:
        copy.wait_send()
    for copy in spread:
        copy.wait()
    out_ref[...] = hidden[...]


def hidden_of(x, mix, down, nctx, nhead):
    T, width = x.shape
    vmem = pl.BlockSpec(memory_space=pltpu.VMEM)
    return pl.pallas_call(
        functools.partial(hidden_kernel, nctx=nctx, nhead=nhead),
        in_specs=[vmem] * 3,
        out_specs=vmem,
        out_shape=jax.ShapeDtypeStruct((T, 256), BF16),
        scratch_shapes=[
            pltpu.VMEM((16, width), BF16),
            pltpu.VMEM((T, 256), F32),
            pltpu.VMEM((nhead - 1, T // nhead, 256), F32),
            pltpu.VMEM((T, 256), BF16),
            pltpu.SemaphoreType.DMA((2 * nhead,)),
            pltpu.SemaphoreType.DMA((2 * nhead,)),
        ],
        compiler_params=pltpu.CompilerParams(
            collective_id=0, has_side_effects=True, vmem_limit_bytes=32 * 1024 * 1024
        ),
    )(x, mix, down)


def later_of(map_later, earlier):
    wide = cat([earlier, jnp.zeros_like(earlier)], 0)
    lane = iota(map_later.shape, 1) < 64
    return mm(map_later, wide) + jnp.where(lane, 0.0, map_later)


def scan_kernel(
    mu_ref, start_ref, out_ref,
    maps, row_total, row_totals, states, got, s1, r1, s2, r2, s3, r3, *, nrow,
):
    ctx = lax.axis_index("ctx")
    n = mu_ref.shape[0]
    y, me = ctx // n, lax.rem(ctx, n)
    base = y * n
    mates = [lax.rem(me + step, n) for step in range(1, n)]
    rows = [lax.rem(y + step, nrow) for step in range(1, nrow)]
    barrier = pltpu.get_barrier_semaphore()
    for mate in mates:
        pl.semaphore_signal(barrier, inc=1, device_id={"ctx": base + mate}, device_id_type=MESH)
    for row in rows:
        pl.semaphore_signal(barrier, inc=1, device_id={"ctx": row * n + me}, device_id_type=MESH)
    pl.semaphore_wait(barrier, n + nrow - 2)

    first = []
    for step, mate in enumerate(mates):
        copy = pltpu.make_async_remote_copy(
            src_ref=mu_ref.at[mate],
            dst_ref=maps.at[me],
            send_sem=s1.at[step],
            recv_sem=r1.at[step],
            device_id={"ctx": base + mate},
            device_id_type=MESH,
        )
        copy.start()
        first.append(copy)
    maps[me] = mu_ref[me]
    for copy in first:
        copy.wait_recv()

    prefix = [maps[d] for d in range(n)]
    size = 1
    while size < n:
        for low in range(size, n, 2 * size):
            group = cat(prefix[low : low + size], 0)
            joined = later_of(group, prefix[low - 1])
            for d in range(size):
                prefix[low + d] = joined[64 * d : 64 * d + 64]
        size *= 2
    row_total[...] = prefix[n - 1]
    second = []
    for step, row in enumerate(rows):
        copy = pltpu.make_async_remote_copy(
            src_ref=row_total,
            dst_ref=row_totals.at[y],
            send_sem=s2.at[step],
            recv_sem=r2.at[step],
            device_id={"ctx": row * n + me},
            device_id_type=MESH,
        )
        copy.start()
        second.append(copy)
    row_totals[y] = row_total[...]
    for copy in second:
        copy.wait_recv()
    begin = start_ref[me]
    state = cat([begin, begin], 1)
    for row in range(nrow - 1):
        state = jnp.where(row < y, later_of(row_totals[row], state), state)
    after = later_of(cat(prefix[: n - 1], 0), state)
    lane = iota((32, 128), 1) < 64
    for d in range(n):
        full = state if d == 0 else after[64 * d - 64 : 64 * d]
        states[d] = jnp.where(lane, pltpu.roll(full[:32], 64, 1), full[32:])
    third = []
    for step, mate in enumerate(mates):
        copy = pltpu.make_async_remote_copy(
            src_ref=states.at[mate],
            dst_ref=got.at[me],
            send_sem=s3.at[step],
            recv_sem=r3.at[step],
            device_id={"ctx": base + mate},
            device_id_type=MESH,
        )
        copy.start()
        third.append(copy)
    got[me] = states[me]
    for copy in third:
        copy.wait_recv()
    out_ref[...] = got[...]
    for copy in first + second + third:
        copy.wait_send()


def starts_of(mu, start, nctx):
    n = mu.shape[0]
    nrow = nctx // n
    vmem = pl.BlockSpec(memory_space=pltpu.VMEM)
    dma = pltpu.SemaphoreType.DMA
    return pl.pallas_call(
        functools.partial(scan_kernel, nrow=nrow),
        in_specs=[vmem] * 2,
        out_specs=vmem,
        out_shape=jax.ShapeDtypeStruct((n, 32, 128), F32),
        scratch_shapes=[
            pltpu.VMEM((n, 64, 128), F32),
            pltpu.VMEM((64, 128), F32),
            pltpu.VMEM((nrow, 64, 128), F32),
            pltpu.VMEM((n, 32, 128), F32),
            pltpu.VMEM((n, 32, 128), F32),
            dma((n,)), dma((n,)), dma((nrow,)), dma((nrow,)), dma((n,)), dma((n,)),
        ],
        compiler_params=pltpu.CompilerParams(
            collective_id=1, has_side_effects=True, vmem_limit_bytes=32 * 1024 * 1024
        ),
    )(mu, start)


def read_kernel(reff, base, start, out, *, pairs):
    T = reff.shape[0]
    lane = iota((64, 128), 1) < 64
    row, col = iota((128, 128), 0), iota((128, 128), 1)
    mean64 = jnp.where(row // 64 == col // 64, 1.0 / 64, 0.0).astype(BF16)
    mean2 = cat([mean64, mean64], 0)
    for p in range(pairs):
        at = slice(128 * p, 128 * p + 128)
        a, b = start[2 * p], start[2 * p + 1]
        both_a = cat([a, pltpu.roll(a, 64, 1)], 0)
        both_b = cat([pltpu.roll(b, 64, 1), b], 0)
        state = cat([jnp.where(lane, both_a, 0.0), jnp.where(lane, 0.0, both_b)], 0)
        read = mm(reff[:, at], state) + base[:, at]
        centered = read - dot(cat(split(read), 1), mean2)
        var = dot(cat(split(centered * centered), 1), mean2)
        out[:, at] = (centered * lax.rsqrt(var + 0.00064)).astype(BF16)


def read_of(reff, base, starts, pairs=4):
    T, width = reff.shape
    w = 128 * pairs
    cols = lambda i: (0, i)
    return pl.pallas_call(
        functools.partial(read_kernel, pairs=pairs),
        grid=(width // w,),
        in_specs=[
            pl.BlockSpec((T, w), cols),
            pl.BlockSpec((T, w), cols),
            pl.BlockSpec((2 * pairs, 32, 128), lambda i: (i, 0, 0)),
        ],
        out_specs=pl.BlockSpec((T, w), cols),
        out_shape=jax.ShapeDtypeStruct((T, width), BF16),
        compiler_params=pltpu.CompilerParams(vmem_limit_bytes=32 * 1024 * 1024),
    )(reff, base, starts)


def solution(mesh):
    nctx, nhead = mesh.shape["ctx"], mesh.shape["head"]

    def on_device(x, mix, down, du, ru, db, rb, rec, key, val, start):
        hid = hidden_of(x, mix[None], down, nctx, nhead)
        mu, reff, base = chunk(hid, du, ru, db[None], rb[None], rec, key, val, pairs=4)
        starts = starts_of(mu, start, nctx)
        return read_of(reff, base, starts)

    P = jax.sharding.PartitionSpec
    both, wide = P("ctx", "head"), P("head")
    return jax.shard_map(
        on_device,
        mesh=mesh,
        in_specs=(both, wide, P("head", None), P(None, "head"), P(None, "head"), wide, wide)
        + (both,) * 3
        + (P("head", None, None),),
        out_specs=both,
        check_vma=False,
    )
```

```python
import functools
import jax
import jax.numpy as jnp
from jax import lax
from jax.experimental import pallas as pl
from jax.experimental.pallas import tpu as pltpu

F32 = jnp.float32
BF16 = jnp.bfloat16
NN = (((1,), (0,)), ((), ()))
NT = (((1,), (1,)), ((), ()))


def dot(a, b, dims=NN):
    return lax.dot_general(a, b, dims, preferred_element_type=F32)


def split(x):
    high = x.astype(BF16)
    return high, (x - high.astype(F32)).astype(BF16)


def cat(parts, axis):
    return jnp.concatenate(parts, axis=axis)


def mm3(a, b):
    ah, al = split(a)
    bh, bl = split(b)
    return dot(cat([ah, al], 1), cat([bh, bh], 0)) + dot(ah, bl)


def iota(shape, axis):
    return lax.broadcasted_iota(jnp.int32, shape, axis)


MESH = pl.DeviceIdType.MESH
PAIRS = 4


def half_roll(x):
    return pltpu.roll(x, 64, 1)


def later_of(map_later, earlier):
    wide = cat([earlier, jnp.zeros_like(earlier)], 0)
    lane = iota(map_later.shape, 1) < 64
    return mm3(map_later, wide) + jnp.where(lane, 0.0, map_later)


def pack_state(full):
    lane = iota((32, 128), 1) < 64
    return jnp.where(lane, half_roll(full[:32]), full[32:])


def unit_inverse(low, row, col):
    T = low[0].shape[0]
    eye = (row == col).astype(F32)
    block = row // 8 == col // 8
    d = [jnp.where(block, a, 0.0) for a in low]
    d2 = [mm3(a, a) for a in d]
    dd = [mm3(cat([a, b], 0), b) for a, b in zip(d, d2)]
    poly = [eye - a + b - c[:T] for a, b, c in zip(d, d2, dd)]
    inv = [a + mm3(a, c[T:]) for a, c in zip(poly, dd)]
    size = 8
    while size < T:
        blocks = T // size

        def rows_of(a, odd):
            return [a[size * i : size * i + size] for i in range(odd, blocks, 2)]

        below = cat(rows_of(row, 1), 0) // size - 1 == cat(rows_of(col, 1), 0) // size
        step = [
            mm3(jnp.where(below, cat(rows_of(a, 1), 0), 0.0), b) for a, b in zip(low, inv)
        ]
        new = []
        for a, b in zip(inv, step):
            parts = [b[size * (i // 2) : size * (i // 2) + size] for i in range(blocks)]
            odd = cat(rows_of(a, 1), 0)
            odd = odd - mm3(odd, cat(parts, 0))
            merged = []
            for i, even in enumerate(rows_of(a, 0)):
                merged += [even, odd[size * i : size * i + size]]
            new.append(cat(merged, 0))
        inv = new
        size *= 2
    return inv


def mixed_kernel(
    x_h, mix_h, down_h, du_h, ru_h, db_h, rb_h, rec_h, key_h, val_h, start_h,
    out,
    x_ref, mix_ref, down_ref, du, ru, db, rb, rec, key, val, start_ref, loads,
    tail, total, shares, hidden, sends, recvs,
    unit, mu, left_ref, solved_ref, reff, base_ref, starts,
    sib, first_maps, chip_maps, maps, row_total, row_totals, states, got, give,
    s0, r0, s1, r1, s2, r2, s3, r3, s4, r4,
    *, nctx, nhead,
):
    ctx, head = lax.axis_index("ctx"), lax.axis_index("head")
    T, width = x_ref.shape
    n = mu.shape[0] * mu.shape[1]
    chips = n // 2
    quarter = chips // 2
    nrow = nctx // n
    y, me = ctx // n, lax.rem(ctx, n)
    chip, core = me // 2, lax.rem(me, 2)
    other_core = 1 - core
    base = y * n
    my_slot = chip // 2 + quarter * lax.rem(chip, 2)
    my_head = core * chips + my_slot
    sibling = {"ctx": base + chip * 2 + other_core}

    fetch = []
    for i, (src, dst) in enumerate(
        [(x_h, x_ref), (mix_h, mix_ref), (down_h, down_ref), (key_h, key), (du_h, du), (ru_h, ru)]
        + [(db_h, db), (rb_h, rb), (rec_h, rec), (val_h, val), (start_h.at[my_head], start_ref)]
    ):
        copy = pltpu.make_async_copy(src, dst, loads.at[i])
        copy.start()
        fetch.append(copy)

    after, behind = lax.rem(ctx + 1, nctx), lax.rem(ctx + nctx - 1, nctx)
    mates = [lax.rem(head + step, nhead) for step in range(1, nhead)]
    far = sorted(range(1, chips), key=lambda d: -min(d, chips - d))
    others = [lax.rem(chip + step, chips) for step in far]
    rows = [lax.rem(y + step, nrow) for step in range(1, nrow)]
    barrier = pltpu.get_barrier_semaphore()
    for other in [after, behind]:
        pl.semaphore_signal(barrier, inc=1, device_id={"ctx": other}, device_id_type=MESH)
    for mate in mates:
        pl.semaphore_signal(barrier, inc=1, device_id={"head": mate}, device_id_type=MESH)
    pl.semaphore_signal(barrier, inc=1, device_id=sibling, device_id_type=MESH)
    for other in [base + 2 * o + core for o in others] + [r * n + me for r in rows]:
        pl.semaphore_signal(barrier, inc=1, device_id={"ctx": other}, device_id_type=MESH)
    pl.semaphore_wait(barrier, 2 + nhead - 1 + 1 + chips - 1 + nrow - 1)

    shift = pltpu.make_async_remote_copy(
        src_ref=x_h.at[pl.ds(T - 16, 16)],
        dst_ref=tail,
        send_sem=sends.at[0],
        recv_sem=recvs.at[0],
        device_id={"ctx": after},
        device_id_type=MESH,
    )
    shift.start()
    for i in range(3):
        fetch[i].wait()
    mix = mix_ref[...]
    xf = x_ref[...].astype(F32)
    before = pltpu.roll(xf, 1, 0)
    shifted = (xf + (before - xf) * mix).astype(BF16)
    total[...] = dot(shifted, down_ref[...])
    shift.wait_recv()
    xt = x_ref[0:16, :].astype(F32)
    edge = jnp.where(ctx > 0, tail[...].astype(F32)[15:16], 0.0)
    before = jnp.where(iota((16, width), 0) == 0, edge, pltpu.roll(xt, 1, 0))
    shifted = (xt + (before - xt) * mix).astype(BF16)
    total[0:16, :] = dot(shifted, down_ref[...])

    share = T // nhead
    mine = pl.ds(pl.multiple_of(head * share, share), share)
    scatter, spread = [], []
    for step, mate in enumerate(mates):
        copy = pltpu.make_async_remote_copy(
            src_ref=total.at[pl.ds(pl.multiple_of(mate * share, share), share)],
            dst_ref=shares.at[step],
            send_sem=sends.at[1 + step],
            recv_sem=recvs.at[1 + step],
            device_id={"head": mate},
            device_id_type=MESH,
        )
        copy.start()
        scatter.append(copy)

    row, col = iota((T, T), 0), iota((T, T), 1)
    tri = (row >= col).astype(BF16)
    half = (row // 64 == col // 64).astype(BF16)
    half2 = cat([half, half], 0)
    fetch[3].wait()
    for p in range(width // 128):
        kf = key[:, 128 * p : 128 * p + 128].astype(F32)
        square = dot(cat(split(kf * kf), 1), half2)
        unit[:, 128 * p : 128 * p + 128] = kf * lax.rsqrt(square + 1e-06)

    grand = total[mine, :]
    for step, copy in enumerate(scatter):
        copy.wait_recv()
        grand = grand + shares[step]
    hidden[mine, :] = cat([jnp.tanh(grand[:, :128]), grand[:, 128:]], 1).astype(BF16)
    for step, mate in enumerate(mates):
        copy = pltpu.make_async_remote_copy(
            src_ref=hidden.at[mine],
            dst_ref=hidden.at[mine],
            send_sem=sends.at[nhead + step],
            recv_sem=recvs.at[nhead + step],
            device_id={"head": mate},
            device_id_type=MESH,
        )
        copy.start()
        spread.append(copy)
    for i in range(4, len(fetch)):
        fetch[i].wait()
    shift.wait_send()
    for copy in scatter:
        copy.wait_send()
    for copy in spread:
        copy.wait()

    eye = (row == col).astype(F32)
    first = iota((T, 128), 1) < 64
    first2 = cat([first, first], 1)
    firsts = cat([first, first], 0)
    tri2 = cat([tri, tri], 1)
    strict, upto = row > col, row >= col
    P, H = range(PAIRS), range(2 * PAIRS)

    def swap_maps(h):
        part = pl.ds(h * quarter, quarter)
        return pltpu.make_async_remote_copy(
            src_ref=mu.at[other_core, part],
            dst_ref=sib.at[part],
            send_sem=s0.at[h],
            recv_sem=r0.at[h],
            device_id=sibling,
            device_id_type=MESH,
        )

    def send_map(h, k):
        place = lax.rem(chip // 2 + k, quarter)
        to = 2 * place + h
        return to, pltpu.make_async_remote_copy(
            src_ref=chip_maps.at[h * quarter + place],
            dst_ref=maps.at[chip],
            send_sem=s1.at[h, k],
            recv_sem=r1.at[chip],
            device_id={"ctx": base + 2 * to + core},
            device_id_type=MESH,
        )

    def forward(h):
        swap_maps(h).wait_recv()
        for i in range(quarter):
            slot = h * quarter + i
            own, theirs = mu[core, slot], sib[slot]
            earlier = jnp.where(core == 0, own, theirs)
            later = jnp.where(core == 0, theirs, own)
            first_maps[slot] = earlier
            chip_maps[slot] = later_of(later, earlier)
        for k in [2, 1, 3, 0]:
            to, copy = send_map(h, k)

            @pl.when(to != chip)
            def _():
                copy.start()

    def half_of_heads(g, carry):
        def columns(ref, p):
            start = (p // 2) * (width // 2) + g * (width // 4) + (p % 2) * 128
            return ref[:, pl.ds(pl.multiple_of(start, 128), 128)]

        hid = hidden[...]
        recv, keyv, valv, dirv = [[columns(a, p) for p in P] for a in (rec, key, val, unit)]
        logd = [
            -0.606531 * jax.nn.sigmoid(dot(hid[:, :128], columns(du, p)) + columns(db, p))
            for p in P
        ]
        rate = [jax.nn.sigmoid(dot(hid[:, 128:], columns(ru, p)) + columns(rb, p)) for p in P]
        cum = []
        for p in P:
            l1, l2 = split(logd[p])
            l3 = (logd[p] - l1.astype(F32) - l2.astype(F32)).astype(BF16)
            cum.append(dot(tri2, cat([l1, l2], 0)) + dot(tri, l3))
        mid = [cum[p][T // 2 - 1 : T // 2] for p in P]
        last = [cum[p][T - 1 :] for p in P]
        e_out = [jnp.exp(mid[p] - cum[p]) for p in P]
        dir_in = [dirv[p] * jnp.exp(cum[p] - logd[p] - mid[p]) for p in P]
        read_in = [recv[p].astype(F32) * jnp.exp(cum[p] - mid[p]) for p in P]
        key_out = [keyv[p].astype(F32) * e_out[p] for p in P]
        rem_out = [rate[p] * dirv[p] * e_out[p] for p in P]
        e_mid = [jnp.exp(mid[p]) for p in P]
        e_end = [jnp.exp(last[p] - mid[p]) for p in P]
        e_all = [jnp.exp(last[p]) for p in P]
        scores = []
        zero = jnp.zeros((2 * T, 128), BF16)
        for p in P:
            xh, xl = split(cat([dir_in[p], read_in[p]], 0))
            yh, yl = split(cat([key_out[p], rem_out[p]], 0))
            xr, yr = half_roll(xl), half_roll(yh)
            left = cat([jnp.where(firsts, xh, xr), jnp.where(firsts, xh, zero)], 1)
            scores.append(dot(left, cat([jnp.where(firsts, yh, yr), yl], 1), NT))
            left = cat([jnp.where(firsts, xr, xh), jnp.where(firsts, zero, xh)], 1)
            scores.append(dot(left, cat([jnp.where(firsts, yr, yh), yl], 1), NT))
        a_kk = [jnp.where(strict, scores[h][:T, :T], 0.0) for h in H]
        low = [jnp.where(strict, scores[h][:T, T:], 0.0) for h in H]
        for h in H:
            left_ref[g, h] = cat(
                [
                    jnp.where(upto, -scores[h][T:, T:], 0.0),
                    jnp.where(upto, scores[h][T:, :T], 0.0),
                ],
                1,
            )

        @pl.when(g == 1)
        def _():
            forward(0)

        inv = unit_inverse(low, row, col)
        kv = [dot(cat(split(a_kk[h]), 1), cat([valv[h // 2]] * 2, 0)) for h in H]
        right = [
            cat([dir_in[p] * e_mid[p], jnp.where(first, kv[2 * p], kv[2 * p + 1])], 1) for p in P
        ]
        sol = [mm3(inv[h], right[h // 2]) for h in H]
        low_lane = iota((64, 128), 1) < 64
        for p in P:
            solved = jnp.where(first2, sol[2 * p], sol[2 * p + 1])
            solved_ref[g, p] = solved
            values = cat([jnp.zeros((T, 128), BF16), valv[p]], 1)
            wh, wl = split(solved)
            lh, ll = split(cat([-rem_out[p] * e_end[p], key_out[p] * e_end[p]], 0).T)
            wide = cat([wh, values], 0)
            made = dot(lh, wide) + dot(ll, wide) + dot(lh[:, :T], wl)
            trans = made[:, :128] + eye * e_all[p]
            added = made[:, 128:]
            slot = g * quarter + 2 * (p % 2)
            mu[p // 2, slot] = jnp.where(low_lane, trans[:64], half_roll(added[:64]))
            mu[p // 2, slot + 1] = jnp.where(low_lane, half_roll(trans[64:]), added[64:])
            reff[g, p] = read_in[p] * e_mid[p]
        swap_maps(g).start()
        return carry

    lax.fori_loop(0, 2, half_of_heads, 0)

    def reads_of(i, carry):
        g, p = i // PAIRS, lax.rem(i, PAIRS)
        start = (p // 2) * (width // 2) + g * (width // 4) + lax.rem(p, 2) * 128
        solved = solved_ref[g, p]
        wh, wl = split(solved)
        values = val[:, pl.ds(pl.multiple_of(start, 128), 128)]
        wide = cat([wh, cat([jnp.zeros((T, 128), BF16), values], 1)], 0)
        lh, ll = split(cat([left_ref[g, 2 * p], left_ref[g, 2 * p + 1]], 0))
        made = dot(lh, wide) + dot(ll, wide) + dot(lh[:, :T], wl)
        reads = jnp.where(first2, made[:T], made[T:])
        reff[g, p] = reff[g, p] + reads[:, :128]
        base_ref[g, p] = reads[:, 128:]
        return carry

    lax.fori_loop(0, 3, reads_of, 0)
    forward(1)
    lax.fori_loop(3, 2 * PAIRS, reads_of, 0)

    maps[chip] = chip_maps[my_slot]
    for step in far:
        source = lax.rem(chip + step, chips)
        pltpu.make_async_remote_copy(
            src_ref=chip_maps.at[0],
            dst_ref=maps.at[source],
            send_sem=s1.at[0, 0],
            recv_sem=r1.at[source],
            device_id={"ctx": base + 2 * source + core},
            device_id_type=MESH,
        ).wait_recv()
    prefix = [maps[d] for d in range(chips)]
    size = 1
    while size < chips:
        for low in range(size, chips, 2 * size):
            joined = later_of(cat(prefix[low : low + size], 0), prefix[low - 1])
            for d in range(size):
                prefix[low + d] = joined[64 * d : 64 * d + 64]
        size *= 2
    row_total[...] = prefix[chips - 1]
    second = []
    for step, other in enumerate(rows):
        copy = pltpu.make_async_remote_copy(
            src_ref=row_total,
            dst_ref=row_totals.at[y],
            send_sem=s2.at[step],
            recv_sem=r2.at[step],
            device_id={"ctx": other * n + me},
            device_id_type=MESH,
        )
        copy.start()
        second.append(copy)
    row_totals[y] = row_total[...]
    begin = start_ref[...]
    state = cat([begin, begin], 1)
    for copy in second:
        copy.wait_recv()
    for r in range(nrow - 1):
        state = jnp.where(r < y, later_of(row_totals[r], state), state)
    after_state = later_of(cat(prefix[: chips - 1], 0), state)
    for d in range(chips):
        states[d] = pack_state(state if d == 0 else after_state[64 * d - 64 : 64 * d])
    third = []
    for step, other in enumerate(others):
        copy = pltpu.make_async_remote_copy(
            src_ref=states.at[other],
            dst_ref=got.at[my_slot],
            send_sem=s3.at[step],
            recv_sem=r3.at[step],
            device_id={"ctx": base + 2 * other + core},
            device_id_type=MESH,
        )
        copy.start()
        third.append(copy)
    got[my_slot] = states[chip]
    for copy in third:
        copy.wait_recv()

    for slot in range(chips):
        packed = got[slot]
        full = cat([half_roll(packed), packed], 0)
        next_packed = pack_state(later_of(first_maps[slot], full))
        give[slot] = jnp.where(core == 0, next_packed, packed)
        starts[core, slot] = jnp.where(core == 0, packed, next_packed)
    fourth = pltpu.make_async_remote_copy(
        src_ref=give,
        dst_ref=starts.at[core],
        send_sem=s4.at[0],
        recv_sem=r4.at[0],
        device_id=sibling,
        device_id_type=MESH,
    )
    fourth.start()

    lane = iota((64, 128), 1) < 64
    mean64 = (half.astype(F32) / 64).astype(BF16)
    mean2 = cat([mean64, mean64], 0)

    def finish(side):
        for q in range(chips // 2):
            g, p = q // 2, 2 * side + q % 2
            a, b = starts[side, 2 * q], starts[side, 2 * q + 1]
            both_a = cat([a, half_roll(a)], 0)
            both_b = cat([half_roll(b), b], 0)
            state = cat([jnp.where(lane, both_a, 0.0), jnp.where(lane, 0.0, both_b)], 0)
            read = mm3(reff[g, p], state) + base_ref[g, p]
            centered = read - dot(cat(split(read), 1), mean2)
            var = dot(cat(split(centered * centered), 1), mean2)
            normed = (centered * lax.rsqrt(var + 0.00064)).astype(BF16)
            start = side * (width // 2) + 128 * q
            out[:, pl.ds(pl.multiple_of(start, 128), 128)] = normed

    finish(core)
    fourth.wait()
    finish(other_core)

    for h in range(2):
        swap_maps(h).wait_send()
        for k in range(quarter):
            to, copy = send_map(h, k)

            @pl.when(to != chip)
            def _():
                copy.wait_send()

    for copy in second + third:
        copy.wait_send()


def mixed_of(x, mix, down, du, ru, db, rb, rec, key, val, start, nctx, nhead):
    T, width = x.shape
    n = start.shape[0]
    chips = n // 2
    nrow = nctx // n
    dma, vm = pltpu.SemaphoreType.DMA, pltpu.VMEM
    args = (x, mix, down, du, ru, db, rb, rec, key, val, start)
    return pl.pallas_call(
        functools.partial(mixed_kernel, nctx=nctx, nhead=nhead),
        in_specs=[pl.BlockSpec(memory_space=pl.ANY)] * len(args),
        out_specs=pl.BlockSpec(memory_space=pltpu.VMEM),
        out_shape=pltpu.VMEM((T, width), BF16),
        scratch_shapes=[vm(a.shape, a.dtype) for a in args[:-1]]
        + [vm((64, 64), F32), dma((len(args),))]
        + [
            vm((16, width), BF16),
            vm((T, 256), F32),
            vm((nhead - 1, T // nhead, 256), F32),
            vm((T, 256), BF16),
            dma((2 * nhead,)),
            dma((2 * nhead,)),
            vm((T, width), F32),
            vm((2, chips, 64, 128), F32),
            vm((2, 2 * PAIRS, T, 2 * T), F32),
            vm((2, PAIRS, T, 256), F32),
            vm((2, PAIRS, T, 128), F32),
            vm((2, PAIRS, T, 128), F32),
            vm((2, chips, 32, 128), F32),
            vm((chips, 64, 128), F32),
            vm((chips, 64, 128), F32),
            vm((chips, 64, 128), F32),
            vm((chips, 64, 128), F32),
            vm((64, 128), F32),
            vm((nrow, 64, 128), F32),
            vm((chips, 32, 128), F32),
            vm((chips, 32, 128), F32),
            vm((chips, 32, 128), F32),
        ]
        + [dma((2,)), dma((2,)), dma((2, chips // 2)), dma((chips,)), dma((nrow,)), dma((nrow,))]
        + [dma((chips,)), dma((chips,)), dma((1,)), dma((1,))],
        compiler_params=pltpu.CompilerParams(
            collective_id=0, has_side_effects=True, vmem_limit_bytes=40 * 1024 * 1024
        ),
    )(*[pltpu.with_memory_space_constraint(a, pltpu.HBM) for a in args])


def solution(mesh):
    nctx, nhead = mesh.shape["ctx"], mesh.shape["head"]

    def on_device(x, mix, down, du, ru, db, rb, rec, key, val, start):
        return mixed_of(
            x, mix[None], down, du, ru, db[None], rb[None], rec, key, val, start, nctx, nhead
        )

    P = jax.sharding.PartitionSpec
    both, wide = P("ctx", "head"), P("head")
    return jax.shard_map(
        on_device,
        mesh=mesh,
        in_specs=(both, wide, P("head", None), P(None, "head"), P(None, "head"), wide, wide)
        + (both,) * 3
        + (P("head", None, None),),
        out_specs=both,
        check_vma=False,
    )
```

```python
import functools
import jax
import jax.numpy as jnp
from jax import lax
from jax.experimental import pallas as pl
from jax.experimental.pallas import tpu as pltpu

F32 = jnp.float32
BF16 = jnp.bfloat16
NN = (((1,), (0,)), ((), ()))
NT = (((1,), (1,)), ((), ()))


def dot(a, b, dims=NN):
    return lax.dot_general(a, b, dims, preferred_element_type=F32)


def split(x):
    high = x.astype(BF16)
    return high, (x - high.astype(F32)).astype(BF16)


def cat(parts, axis):
    return jnp.concatenate(parts, axis=axis)


def mm3(a, b):
    ah, al = split(a)
    bh, bl = split(b)
    return dot(cat([ah, al], 1), cat([bh, bh], 0)) + dot(ah, bl)


def iota(shape, axis):
    return lax.broadcasted_iota(jnp.int32, shape, axis)


MESH = pl.DeviceIdType.MESH
PAIRS = 4


def half_roll(x):
    return pltpu.roll(x, 64, 1)


def later_all(laters, earliers):
    left = [split(a) for a in laters]
    right = [[cat([part, jnp.zeros_like(part)], 0) for part in split(b)] for b in earliers]
    main = [dot(cat([a, al], 1), cat([b, b], 0)) for (a, al), (b, _) in zip(left, right)]
    rest = [dot(a, bl) for (a, _), (_, bl) in zip(left, right)]
    lane = [iota(a.shape, 1) < 64 for a in laters]
    return [m + r + jnp.where(k, 0.0, a) for m, r, k, a in zip(main, rest, lane, laters)]


def later_of(map_later, earlier):
    return later_all([map_later], [earlier])[0]


def pack_state(full):
    lane = iota((32, 128), 1) < 64
    return jnp.where(lane, half_roll(full[:32]), full[32:])


def unit_inverse(low, row, col):
    T = low[0].shape[0]
    eye = (row == col).astype(F32)
    block = row // 8 == col // 8
    d = [jnp.where(block, a, 0.0) for a in low]
    d2 = [mm3(a, a) for a in d]
    dd = [mm3(cat([a, b], 0), b) for a, b in zip(d, d2)]
    poly = [eye - a + b - c[:T] for a, b, c in zip(d, d2, dd)]
    inv = [a + mm3(a, c[T:]) for a, c in zip(poly, dd)]
    size = 8
    while size < T:
        blocks = T // size

        def rows_of(a, odd):
            return [a[size * i : size * i + size] for i in range(odd, blocks, 2)]

        below = cat(rows_of(row, 1), 0) // size - 1 == cat(rows_of(col, 1), 0) // size
        step = [
            mm3(jnp.where(below, cat(rows_of(a, 1), 0), 0.0), b) for a, b in zip(low, inv)
        ]
        new = []
        for a, b in zip(inv, step):
            parts = [b[size * (i // 2) : size * (i // 2) + size] for i in range(blocks)]
            odd = cat(rows_of(a, 1), 0)
            odd = odd - mm3(odd, cat(parts, 0))
            merged = []
            for i, even in enumerate(rows_of(a, 0)):
                merged += [even, odd[size * i : size * i + size]]
            new.append(cat(merged, 0))
        inv = new
        size *= 2
    return inv


def mixed_kernel(
    x_h, mix_h, down_h, du_h, ru_h, db_h, rb_h, rec_h, key_h, val_h, start_h,
    out,
    x_ref, mix_ref, down_ref, du, ru, db, rb, rec, key, val, start_ref, loads,
    tail, total, shares, hidden, sends, recvs,
    edge_sum, edge_sums, grand_ref, edge_send, edge_recv,
    unit, mu, cent, outer, solved_ref, reff, base_ref, starts,
    sib, first_maps, chip_maps, maps, row_total, row_totals, states, got, give,
    s0, r0, s1, r1, s2, r2, s3, r3, s4, r4,
    *, nctx, nhead,
):
    ctx, head = lax.axis_index("ctx"), lax.axis_index("head")
    T, width = x_ref.shape
    n = mu.shape[0] * mu.shape[1]
    chips = n // 2
    quarter = chips // 2
    nrow = nctx // n
    y, me = ctx // n, lax.rem(ctx, n)
    chip, core = me // 2, lax.rem(me, 2)
    other_core = 1 - core
    base = y * n
    my_slot = chip // 2 + quarter * lax.rem(chip, 2)
    my_head = core * chips + my_slot
    sibling = {"ctx": base + chip * 2 + other_core}

    fetch = []
    for i, (src, dst) in enumerate(
        [(x_h, x_ref), (mix_h, mix_ref), (down_h, down_ref), (key_h, key), (du_h, du), (ru_h, ru)]
        + [(db_h, db), (rb_h, rb), (rec_h, rec), (val_h, val), (start_h.at[my_head], start_ref)]
    ):
        copy = pltpu.make_async_copy(src, dst, loads.at[i])
        copy.start()
        fetch.append(copy)

    row_totals[...] = jnp.zeros_like(row_totals)
    after, behind = lax.rem(ctx + 1, nctx), lax.rem(ctx + nctx - 1, nctx)
    mirror = 1 - 2 * core
    mates = [lax.rem(head + nhead + mirror * step, nhead) for step in (2, 1, 3)]
    far = sorted(range(1, chips), key=lambda d: -min(d, chips - d))
    others = [lax.rem(chip + chips + mirror * step, chips) for step in far]
    rows = [lax.rem(y + step, nrow) for step in range(1, nrow)]
    barrier = pltpu.get_barrier_semaphore()
    for other in [after, behind]:
        pl.semaphore_signal(barrier, inc=1, device_id={"ctx": other}, device_id_type=MESH)
    for mate in mates:
        pl.semaphore_signal(barrier, inc=1, device_id={"head": mate}, device_id_type=MESH)
    pl.semaphore_signal(barrier, inc=1, device_id=sibling, device_id_type=MESH)
    for other in [base + 2 * o + core for o in others] + [r * n + me for r in rows]:
        pl.semaphore_signal(barrier, inc=1, device_id={"ctx": other}, device_id_type=MESH)
    pl.semaphore_wait(barrier, 2 + nhead - 1 + 1 + chips - 1 + nrow - 1)

    shift = pltpu.make_async_remote_copy(
        src_ref=x_h.at[pl.ds(T - 16, 16)],
        dst_ref=tail,
        send_sem=sends.at[0],
        recv_sem=recvs.at[0],
        device_id={"ctx": after},
        device_id_type=MESH,
    )
    shift.start()
    for i in range(3):
        fetch[i].wait()
    mix = mix_ref[...]
    xf = x_ref[...].astype(F32)
    before = pltpu.roll(xf, 1, 0)
    shifted = (xf + (before - xf) * mix).astype(BF16)
    total[...] = dot(shifted, down_ref[...])
    share = T // nhead
    mine = pl.ds(pl.multiple_of(head * share, share), share)
    scatter, spread = [], []
    for step, mate in enumerate(mates):
        copy = pltpu.make_async_remote_copy(
            src_ref=total.at[pl.ds(pl.multiple_of(mate * share, share), share)],
            dst_ref=shares.at[step],
            send_sem=sends.at[1 + step],
            recv_sem=recvs.at[1 + step],
            device_id={"head": mate},
            device_id_type=MESH,
        )
        copy.start()
        scatter.append(copy)

    shift.wait_recv()
    xt = x_ref[0:16, :].astype(F32)
    edge = jnp.where(ctx > 0, tail[...].astype(F32)[15:16], 0.0)
    before = jnp.where(iota((16, width), 0) == 0, edge, pltpu.roll(xt, 1, 0))
    shifted = (xt + (before - xt) * mix).astype(BF16)
    edge_sum[...] = dot(shifted, down_ref[...])
    send_edge = pltpu.make_async_remote_copy(
        src_ref=edge_sum,
        dst_ref=edge_sums.at[head],
        send_sem=edge_send.at[0],
        recv_sem=edge_recv.at[head],
        device_id={"head": 0},
        device_id_type=MESH,
    )

    @pl.when(head != 0)
    def _():
        send_edge.start()

    row, col = iota((T, T), 0), iota((T, T), 1)
    tri = (row >= col).astype(BF16)
    half = (row // 64 == col // 64).astype(BF16)
    half2 = cat([half, half], 0)
    fetch[3].wait()
    for p in range(width // 128):
        kf = key[:, 128 * p : 128 * p + 128].astype(F32)
        square = dot(cat(split(kf * kf), 1), half2)
        unit[:, 128 * p : 128 * p + 128] = kf * lax.rsqrt(square + 1e-06)

    grand = total[mine, :]
    for step, copy in enumerate(scatter):
        copy.wait_recv()
        grand = grand + shares[step]
    grand_ref[...] = grand

    @pl.when(head == 0)
    def _():
        first_row = edge_sum[0:1, :]
        for h in range(1, nhead):
            pltpu.make_async_remote_copy(
                src_ref=edge_sum,
                dst_ref=edge_sums.at[h],
                send_sem=edge_send.at[0],
                recv_sem=edge_recv.at[h],
                device_id={"head": h},
                device_id_type=MESH,
            ).wait_recv()
            first_row = first_row + edge_sums[h, 0:1, :]
        grand_ref[0:1, :] = first_row

    grand = grand_ref[...]
    hidden[mine, :] = cat([jnp.tanh(grand[:, :128]), grand[:, 128:]], 1).astype(BF16)
    for step, mate in enumerate(mates):
        copy = pltpu.make_async_remote_copy(
            src_ref=hidden.at[mine],
            dst_ref=hidden.at[mine],
            send_sem=sends.at[nhead + step],
            recv_sem=recvs.at[nhead + step],
            device_id={"head": mate},
            device_id_type=MESH,
        )
        copy.start()
        spread.append(copy)
    for i in range(4, len(fetch)):
        fetch[i].wait()
    for copy in spread:
        copy.wait_recv()

    eye = (row == col).astype(F32)
    first = iota((T, 128), 1) < 64
    first2 = cat([first, first], 1)
    firsts = cat([first, first], 0)
    tri2 = cat([tri, tri], 1)
    strict, upto = row > col, row >= col
    P, H = range(PAIRS), range(2 * PAIRS)

    def swap_maps(h):
        part = pl.ds(h * quarter, quarter)
        return pltpu.make_async_remote_copy(
            src_ref=mu.at[other_core, part],
            dst_ref=sib.at[part],
            send_sem=s0.at[h],
            recv_sem=r0.at[h],
            device_id=sibling,
            device_id_type=MESH,
        )

    def send_map(h, k):
        place = lax.rem(chip // 2 + quarter + mirror * k, quarter)
        to = 2 * place + h
        return to, pltpu.make_async_remote_copy(
            src_ref=chip_maps.at[h * quarter + place],
            dst_ref=maps.at[chip],
            send_sem=s1.at[h, k],
            recv_sem=r1.at[chip],
            device_id={"ctx": base + 2 * to + core},
            device_id_type=MESH,
        )

    def forward(h):
        swap_maps(h).wait_recv()
        slots = [h * quarter + i for i in range(quarter)]
        own, theirs = [mu[core, i] for i in slots], [sib[i] for i in slots]
        earlier = [jnp.where(core == 0, a, b) for a, b in zip(own, theirs)]
        later = [jnp.where(core == 0, b, a) for a, b in zip(own, theirs)]
        joined = later_all(later, earlier)
        for i, slot in enumerate(slots):
            chip_maps[slot] = joined[i]
            first_maps[slot] = earlier[i]
        for k in [2, 1, 3, 0]:
            to, copy = send_map(h, k)

            @pl.when(to != chip)
            def _():
                copy.start()

    def masked_scores(x, yh, yl):
        xh, xl = split(x)
        xr, yr = half_roll(xl), half_roll(yh)
        zero = jnp.zeros_like(xh)
        a = cat([jnp.where(first, xh, xr), jnp.where(first, xh, zero)], 1)
        b = cat([jnp.where(first, xr, xh), jnp.where(first, zero, xh)], 1)
        return [
            dot(a, cat([jnp.where(firsts, yh, yr), yl], 1), NT),
            dot(b, cat([jnp.where(firsts, yr, yh), yl], 1), NT),
        ]

    def half_of_heads(g, carry):
        def columns(ref, p):
            start = (p // 2) * (width // 2) + g * (width // 4) + (p % 2) * 128
            return ref[:, pl.ds(pl.multiple_of(start, 128), 128)]

        hid = hidden[...]
        recv, keyv, valv, dirv = [[columns(a, p) for p in P] for a in (rec, key, val, unit)]
        logd = [
            -0.606531 * jax.nn.sigmoid(dot(hid[:, :128], columns(du, p)) + columns(db, p))
            for p in P
        ]
        rate = [jax.nn.sigmoid(dot(hid[:, 128:], columns(ru, p)) + columns(rb, p)) for p in P]
        cum = []
        for p in P:
            l1, l2 = split(logd[p])
            l3 = (logd[p] - l1.astype(F32) - l2.astype(F32)).astype(BF16)
            cum.append(dot(tri2, cat([l1, l2], 0)) + dot(tri, l3))
        mid = [cum[p][T // 2 - 1 : T // 2] for p in P]
        last = [cum[p][T - 1 :] for p in P]
        e_out = [jnp.exp(mid[p] - cum[p]) for p in P]
        dir_in = [dirv[p] * jnp.exp(cum[p] - logd[p] - mid[p]) for p in P]
        read_in = [recv[p].astype(F32) * jnp.exp(cum[p] - mid[p]) for p in P]
        key_out = [keyv[p].astype(F32) * e_out[p] for p in P]
        rem_out = [rate[p] * dirv[p] * e_out[p] for p in P]
        e_mid = [jnp.exp(mid[p]) for p in P]
        e_end = [jnp.exp(last[p] - mid[p]) for p in P]
        e_all = [jnp.exp(last[p]) for p in P]
        scores = []
        for p in P:
            scores += masked_scores(dir_in[p], *split(cat([key_out[p], rem_out[p]], 0)))
        a_kk = [jnp.where(strict, scores[h][:, :T], 0.0) for h in H]
        low = [jnp.where(strict, scores[h][:, T:], 0.0) for h in H]

        @pl.when(g == 1)
        def _():
            forward(0)

        inv = unit_inverse(low, row, col)
        kv = [dot(cat(split(a_kk[h]), 1), cat([valv[h // 2]] * 2, 0)) for h in H]
        right = [
            cat([dir_in[p] * e_mid[p], jnp.where(first, kv[2 * p], kv[2 * p + 1])], 1) for p in P
        ]
        sol = [mm3(inv[h], right[h // 2]) for h in H]
        low_lane = iota((64, 128), 1) < 64
        solved = [jnp.where(first2, sol[2 * p], sol[2 * p + 1]) for p in P]
        ends = [split(cat([-rem_out[p] * e_end[p], key_out[p] * e_end[p]], 0).T) for p in P]
        made = []
        for p in P:
            wh, wl = split(solved[p])
            lh, ll = ends[p]
            wide = cat([wh, cat([jnp.zeros((T, 128), BF16), valv[p]], 1)], 0)
            made.append(dot(lh, wide) + dot(ll, wide) + dot(lh[:, :T], wl))
        trans = [made[p][:, :128] + eye * e_all[p] for p in P]
        added = [made[p][:, 128:] for p in P]
        for p in P:
            slot = g * quarter + 2 * (p % 2)
            mu[p // 2, slot] = jnp.where(low_lane, trans[p][:64], half_roll(added[p][:64]))
            mu[p // 2, slot + 1] = jnp.where(low_lane, half_roll(trans[p][64:]), added[p][64:])
        swap_maps(g).start()
        for p in P:
            solved_ref[g, p] = solved[p]
            reff[g, p] = read_in[p] * e_mid[p]
            cent[g, p] = read_in[p]
            outer[g, p] = cat([key_out[p], rem_out[p]], 0)
        return carry

    lax.fori_loop(0, 2, half_of_heads, 0)

    def reads_of(i, carry):
        g, side = i // 2, lax.rem(i, 2)
        pairs = [2 * side, 2 * side + 1]
        start = side * (width // 2) + g * (width // 4)
        values = val[:, pl.ds(pl.multiple_of(start, 256), 256)]
        solved = [solved_ref[g, p] for p in pairs]
        inner = [(cent[g, p], outer[g, p]) for p in pairs]
        before = [reff[g, p] for p in pairs]
        scores = [masked_scores(x, *split(o)) for x, o in inner]
        left = [
            split(
                cat(
                    [
                        cat([jnp.where(upto, -a[:, T:], 0.0), jnp.where(upto, a[:, :T], 0.0)], 1)
                        for a in both
                    ],
                    0,
                )
            )
            for both in scores
        ]
        made = []
        for k in range(2):
            wh, wl = split(solved[k])
            zero = jnp.zeros((T, 128), BF16)
            wide = cat([wh, cat([zero, values[:, 128 * k : 128 * k + 128]], 1)], 0)
            lh, ll = left[k]
            made.append(dot(lh, wide) + dot(ll, wide) + dot(lh[:, :T], wl))
        reads = [jnp.where(first2, a[:T], a[T:]) for a in made]
        for k in range(2):
            reff[g, pairs[k]] = before[k] + reads[k][:, :128]
            base_ref[g, pairs[k]] = reads[k][:, 128:]
        return carry

    reads_of(0, 0)
    forward(1)
    lax.fori_loop(1, 4, reads_of, 0)

    maps[chip] = chip_maps[my_slot]
    for step in far:
        source = lax.rem(chip + step, chips)
        pltpu.make_async_remote_copy(
            src_ref=chip_maps.at[0],
            dst_ref=maps.at[source],
            send_sem=s1.at[0, 0],
            recv_sem=r1.at[source],
            device_id={"ctx": base + 2 * source + core},
            device_id_type=MESH,
        ).wait_recv()
    prefix = [maps[d] for d in range(chips)]
    size = 1
    while size < chips:
        lows = list(range(size, chips, 2 * size))
        joined = later_all(
            [cat(prefix[low : low + size], 0) for low in lows], [prefix[low - 1] for low in lows]
        )
        for low, group in zip(lows, joined):
            for d in range(size):
                prefix[low + d] = group[64 * d : 64 * d + 64]
        size *= 2
    row_total[...] = prefix[chips - 1]

    def send_total(r):
        return pltpu.make_async_remote_copy(
            src_ref=row_total,
            dst_ref=row_totals.at[y],
            send_sem=s2.at[r],
            recv_sem=r2.at[y],
            device_id={"ctx": r * n + me},
            device_id_type=MESH,
        )

    for r in range(1, nrow):

        @pl.when(r > y)
        def _():
            send_total(r).start()

    begin = start_ref[...]
    state = cat([begin, begin], 1)
    for r in range(nrow - 1):

        @pl.when(r < y)
        def _():
            pltpu.make_async_remote_copy(
                src_ref=row_total,
                dst_ref=row_totals.at[r],
                send_sem=s2.at[r],
                recv_sem=r2.at[r],
                device_id={"ctx": r * n + me},
                device_id_type=MESH,
            ).wait_recv()

    after_first, others_map = later_all(
        [row_totals[0], row_totals[2]], [state, row_totals[1]]
    )
    others_map = jnp.where(y == 3, others_map, row_totals[1])
    after_rows = later_of(others_map, after_first)
    state = jnp.where(y == 0, state, jnp.where(y == 1, after_first, after_rows))
    after_state = later_of(cat(prefix[: chips - 1], 0), state)
    packs = [pack_state(state)]
    packs += [pack_state(after_state[64 * d - 64 : 64 * d]) for d in range(1, chips)]
    for d in range(chips):
        states[d] = packs[d]
    third = []
    for step, other in enumerate(others):
        copy = pltpu.make_async_remote_copy(
            src_ref=states.at[other],
            dst_ref=got.at[my_slot],
            send_sem=s3.at[step],
            recv_sem=r3.at[step],
            device_id={"ctx": base + 2 * other + core},
            device_id_type=MESH,
        )
        copy.start()
        third.append(copy)
    got[my_slot] = states[chip]
    for copy in third:
        copy.wait_recv()

    packed = [got[slot] for slot in range(chips)]
    full = [cat([half_roll(a), a], 0) for a in packed]
    moved = later_all([first_maps[slot] for slot in range(chips)], full)
    next_packed = [pack_state(a) for a in moved]
    for slot in range(chips):
        give[slot] = jnp.where(core == 0, next_packed[slot], packed[slot])
    for slot in range(chips):
        starts[core, slot] = jnp.where(core == 0, packed[slot], next_packed[slot])
    fourth = pltpu.make_async_remote_copy(
        src_ref=give,
        dst_ref=starts.at[core],
        send_sem=s4.at[0],
        recv_sem=r4.at[0],
        device_id=sibling,
        device_id_type=MESH,
    )
    fourth.start()

    lane = iota((64, 128), 1) < 64
    mean64 = (half.astype(F32) / 64).astype(BF16)
    mean2 = cat([mean64, mean64], 0)

    def finish(side):
        Q = range(chips // 2)
        state = []
        for q in Q:
            a, b = starts[side, 2 * q], starts[side, 2 * q + 1]
            both_a = cat([a, half_roll(a)], 0)
            both_b = cat([half_roll(b), b], 0)
            state.append(
                cat([jnp.where(lane, both_a, 0.0), jnp.where(lane, 0.0, both_b)], 0)
            )
        place = [(q // 2, 2 * side + q % 2) for q in Q]
        read = [mm3(reff[place[q]], state[q]) + base_ref[place[q]] for q in Q]
        centered = [a - dot(cat(split(a), 1), mean2) for a in read]
        var = [dot(cat(split(a * a), 1), mean2) for a in centered]
        normed = [(a * lax.rsqrt(b + 0.00064)).astype(BF16) for a, b in zip(centered, var)]
        for q in Q:
            start = side * (width // 2) + 128 * q
            out[:, pl.ds(pl.multiple_of(start, 128), 128)] = normed[q]

    finish(core)
    fourth.wait_recv()
    finish(other_core)

    for h in range(2):
        swap_maps(h).wait_send()
        for k in range(quarter):
            to, copy = send_map(h, k)

            @pl.when(to != chip)
            def _():
                copy.wait_send()

    for r in range(1, nrow):

        @pl.when(r > y)
        def _():
            send_total(r).wait_send()

    for copy in [shift, fourth] + scatter + spread + third:
        copy.wait_send()

    @pl.when(head != 0)
    def _():
        send_edge.wait_send()


def mixed_of(x, mix, down, du, ru, db, rb, rec, key, val, start, nctx, nhead):
    T, width = x.shape
    n = start.shape[0]
    chips = n // 2
    nrow = nctx // n
    dma, vm = pltpu.SemaphoreType.DMA, pltpu.VMEM
    args = (x, mix, down, du, ru, db, rb, rec, key, val, start)
    return pl.pallas_call(
        functools.partial(mixed_kernel, nctx=nctx, nhead=nhead),
        in_specs=[pl.BlockSpec(memory_space=pl.ANY)] * len(args),
        out_specs=pl.BlockSpec(memory_space=pltpu.VMEM),
        out_shape=pltpu.VMEM((T, width), BF16),
        scratch_shapes=[vm(a.shape, a.dtype) for a in args[:-1]]
        + [vm((64, 64), F32), dma((len(args),))]
        + [
            vm((16, width), BF16),
            vm((T, 256), F32),
            vm((nhead - 1, T // nhead, 256), F32),
            vm((T, 256), BF16),
            dma((2 * nhead,)),
            dma((2 * nhead,)),
            vm((16, 256), F32),
            vm((nhead, 16, 256), F32),
            vm((T // nhead, 256), F32),
            dma((1,)),
            dma((nhead,)),
            vm((T, width), F32),
            vm((2, chips, 64, 128), F32),
            vm((2, PAIRS, T, 128), F32),
            vm((2, PAIRS, 2 * T, 128), F32),
            vm((2, PAIRS, T, 256), F32),
            vm((2, PAIRS, T, 128), F32),
            vm((2, PAIRS, T, 128), F32),
            vm((2, chips, 32, 128), F32),
            vm((chips, 64, 128), F32),
            vm((chips, 64, 128), F32),
            vm((chips, 64, 128), F32),
            vm((chips, 64, 128), F32),
            vm((64, 128), F32),
            vm((nrow, 64, 128), F32),
            vm((chips, 32, 128), F32),
            vm((chips, 32, 128), F32),
            vm((chips, 32, 128), F32),
        ]
        + [dma((2,)), dma((2,)), dma((2, chips // 2)), dma((chips,)), dma((nrow,)), dma((nrow,))]
        + [dma((chips,)), dma((chips,)), dma((1,)), dma((1,))],
        compiler_params=pltpu.CompilerParams(
            collective_id=0, has_side_effects=True, vmem_limit_bytes=40 * 1024 * 1024
        ),
    )(*[pltpu.with_memory_space_constraint(a, pltpu.HBM) for a in args])


def solution(mesh):
    nctx, nhead = mesh.shape["ctx"], mesh.shape["head"]

    def on_device(x, mix, down, du, ru, db, rb, rec, key, val, start):
        return mixed_of(
            x, mix[None], down, du, ru, db[None], rb[None], rec, key, val, start, nctx, nhead
        )

    P = jax.sharding.PartitionSpec
    both, wide = P("ctx", "head"), P("head")
    return jax.shard_map(
        on_device,
        mesh=mesh,
        in_specs=(both, wide, P("head", None), P(None, "head"), P(None, "head"), wide, wide)
        + (both,) * 3
        + (P("head", None, None),),
        out_specs=both,
        check_vma=False,
    )
```

```python
import functools
import jax
import jax.numpy as jnp
from jax import lax
from jax.experimental import pallas as pl
from jax.experimental.pallas import tpu as pltpu

F32 = jnp.float32
BF16 = jnp.bfloat16
NN = (((1,), (0,)), ((), ()))
NT = (((1,), (1,)), ((), ()))


def dot(a, b, dims=NN):
    return lax.dot_general(a, b, dims, preferred_element_type=F32)


def split(x):
    high = x.astype(BF16)
    return high, (x - high.astype(F32)).astype(BF16)


def cat(parts, axis):
    return jnp.concatenate(parts, axis=axis)


def mm3(a, b):
    ah, al = split(a)
    bh, bl = split(b)
    return dot(cat([ah, al], 1), cat([bh, bh], 0)) + dot(ah, bl)


def iota(shape, axis):
    return lax.broadcasted_iota(jnp.int32, shape, axis)


MESH = pl.DeviceIdType.MESH
PAIRS = 4


def half_roll(x):
    return pltpu.roll(x, 64, 1)


def later_all(laters, earliers):
    left = [split(a) for a in laters]
    right = [[cat([part, jnp.zeros_like(part)], 0) for part in split(b)] for b in earliers]
    main = [dot(cat([a, al], 1), cat([b, b], 0)) for (a, al), (b, _) in zip(left, right)]
    rest = [dot(a, bl) for (a, _), (_, bl) in zip(left, right)]
    lane = [iota(a.shape, 1) < 64 for a in laters]
    return [m + r + jnp.where(k, 0.0, a) for m, r, k, a in zip(main, rest, lane, laters)]


def later_of(map_later, earlier):
    return later_all([map_later], [earlier])[0]


def pack_state(full):
    lane = iota((32, 128), 1) < 64
    return jnp.where(lane, half_roll(full[:32]), full[32:])


def unit_inverse(low, row, col):
    T = low[0].shape[0]
    eye = (row == col).astype(F32)
    block = row // 8 == col // 8
    d = [jnp.where(block, a, 0.0) for a in low]
    d2 = [mm3(a, a) for a in d]
    dd = [mm3(cat([a, b], 0), b) for a, b in zip(d, d2)]
    poly = [eye - a + b - c[:T] for a, b, c in zip(d, d2, dd)]
    inv = [a + mm3(a, c[T:]) for a, c in zip(poly, dd)]
    size = 8
    while size < T:
        blocks = T // size

        def rows_of(a, odd):
            return [a[size * i : size * i + size] for i in range(odd, blocks, 2)]

        below = cat(rows_of(row, 1), 0) // size - 1 == cat(rows_of(col, 1), 0) // size
        step = [
            mm3(jnp.where(below, cat(rows_of(a, 1), 0), 0.0), b) for a, b in zip(low, inv)
        ]
        new = []
        for a, b in zip(inv, step):
            parts = [b[size * (i // 2) : size * (i // 2) + size] for i in range(blocks)]
            odd = cat(rows_of(a, 1), 0)
            odd = odd - mm3(odd, cat(parts, 0))
            merged = []
            for i, even in enumerate(rows_of(a, 0)):
                merged += [even, odd[size * i : size * i + size]]
            new.append(cat(merged, 0))
        inv = new
        size *= 2
    return inv


def mixed_kernel(
    x_h, mix_h, down_h, du_h, ru_h, db_h, rb_h, rec_h, key_h, val_h, start_h,
    out,
    x_ref, mix_ref, down_ref, du, ru, db, rb, rec, key, val, start_ref, loads,
    tail, total, shares, hidden, sends, recvs,
    edge_sum, edge_sums, ready, edge_send, edge_recv,
    unit, mu, cent, outer, solved_ref, reff, base_ref, starts,
    sib, first_maps, chip_maps, maps, row_total, row_totals, states, got, give,
    s0, r0, s1, r1, s2, r2, s3, r3, s4, r4,
    *, nctx, nhead,
):
    ctx, head = lax.axis_index("ctx"), lax.axis_index("head")
    T, width = x_ref.shape
    n = mu.shape[0] * mu.shape[1]
    chips = n // 2
    quarter = chips // 2
    nrow = nctx // n
    y, me = ctx // n, lax.rem(ctx, n)
    chip, core = me // 2, lax.rem(me, 2)
    other_core = 1 - core
    base = y * n
    my_slot = chip // 2 + quarter * lax.rem(chip, 2)
    my_head = core * chips + my_slot
    sibling = {"ctx": base + chip * 2 + other_core}

    fetch = []
    for i, (src, dst) in enumerate(
        [(x_h, x_ref), (mix_h, mix_ref), (down_h, down_ref), (key_h, key), (du_h, du), (ru_h, ru)]
        + [(db_h, db), (rb_h, rb), (rec_h, rec), (val_h, val), (start_h.at[my_head], start_ref)]
    ):
        fetch.append(pltpu.make_async_copy(src, dst, loads.at[i]))
    for copy in fetch[:4]:
        copy.start()

    row_totals[...] = jnp.zeros_like(row_totals)
    after, behind = lax.rem(ctx + 1, nctx), lax.rem(ctx + nctx - 1, nctx)
    mirror = 1 - 2 * core
    mates = [lax.rem(head + nhead + mirror * step, nhead) for step in (2, 1, 3)]
    far = sorted(range(1, chips), key=lambda d: -min(d, chips - d))
    others = [lax.rem(chip + chips + mirror * step, chips) for step in far]
    rows = [lax.rem(y + step, nrow) for step in range(1, nrow)]
    barrier = pltpu.get_barrier_semaphore()
    for other in [after, behind]:
        pl.semaphore_signal(barrier, inc=1, device_id={"ctx": other}, device_id_type=MESH)
    for mate in mates:
        pl.semaphore_signal(barrier, inc=1, device_id={"head": mate}, device_id_type=MESH)
    pl.semaphore_signal(barrier, inc=1, device_id=sibling, device_id_type=MESH)
    for other in [base + 2 * o + core for o in others] + [r * n + me for r in rows]:
        pl.semaphore_signal(barrier, inc=1, device_id={"ctx": other}, device_id_type=MESH)

    for i in range(3):
        fetch[i].wait()
    for copy in fetch[4:]:
        copy.start()
    mix = mix_ref[...]
    xf = x_ref[...].astype(F32)
    before = pltpu.roll(xf, 1, 0)
    shifted = (xf + (before - xf) * mix).astype(BF16)
    total[...] = dot(shifted, down_ref[...])
    pl.semaphore_wait(barrier, 2 + nhead - 1 + 1 + chips - 1 + nrow - 1)

    shift = pltpu.make_async_remote_copy(
        src_ref=x_h.at[pl.ds(T - 16, 16)],
        dst_ref=tail,
        send_sem=sends.at[0],
        recv_sem=recvs.at[0],
        device_id={"ctx": after},
        device_id_type=MESH,
    )
    shift.start()

    share = T // nhead
    mine = pl.ds(pl.multiple_of(head * share, share), share)
    scatter, spread = [], []
    for step, mate in enumerate(mates):
        copy = pltpu.make_async_remote_copy(
            src_ref=total.at[pl.ds(pl.multiple_of(mate * share, share), share)],
            dst_ref=shares.at[step],
            send_sem=sends.at[1 + step],
            recv_sem=recvs.at[1 + step],
            device_id={"head": mate},
            device_id_type=MESH,
        )
        copy.start()
        scatter.append(copy)

    shift.wait_recv()
    xt = x_ref[0:16, :].astype(F32)
    edge = jnp.where(ctx > 0, tail[...].astype(F32)[15:16], 0.0)
    before = jnp.where(iota((16, width), 0) == 0, edge, pltpu.roll(xt, 1, 0))
    shifted = (xt + (before - xt) * mix).astype(BF16)
    edge_sum[...] = dot(shifted, down_ref[...])
    edges = []
    for step, mate in enumerate(mates):
        copy = pltpu.make_async_remote_copy(
            src_ref=edge_sum,
            dst_ref=edge_sums.at[step],
            send_sem=edge_send.at[step],
            recv_sem=edge_recv.at[step],
            device_id={"head": mate},
            device_id_type=MESH,
        )
        copy.start()
        edges.append(copy)

    row, col = iota((T, T), 0), iota((T, T), 1)
    tri = (row >= col).astype(BF16)
    half = (row // 64 == col // 64).astype(BF16)
    half2 = cat([half, half], 0)
    fetch[3].wait()
    for p in range(width // 128):
        kf = key[:, 128 * p : 128 * p + 128].astype(F32)
        square = dot(cat(split(kf * kf), 1), half2)
        unit[:, 128 * p : 128 * p + 128] = kf * lax.rsqrt(square + 1e-06)

    grand = total[mine, :]
    for step, copy in enumerate(scatter):
        copy.wait_recv()
        grand = grand + shares[step]
    hidden[mine, :] = cat([jnp.tanh(grand[:, :128]), grand[:, 128:]], 1).astype(BF16)
    for step, mate in enumerate(mates):
        copy = pltpu.make_async_remote_copy(
            src_ref=hidden.at[mine],
            dst_ref=hidden.at[mine],
            send_sem=sends.at[nhead + step],
            recv_sem=recvs.at[nhead + step],
            device_id={"head": mate},
            device_id_type=MESH,
        )
        copy.start()
        spread.append(copy)
    for i in range(4, len(fetch)):
        fetch[i].wait()
    first_row = edge_sum[0:8, :]
    for step, copy in enumerate(edges):
        copy.wait_recv()
        first_row = first_row + edge_sums[step, 0:8, :]
    first_row = cat([jnp.tanh(first_row[:1, :128]), first_row[:1, 128:]], 1)
    for copy in spread:
        copy.wait_recv()
    ready[...] = jnp.where(
        iota((T, 256), 0) == 0, first_row, hidden[...].astype(F32)
    ).astype(BF16)

    eye = (row == col).astype(F32)
    first = iota((T, 128), 1) < 64
    first2 = cat([first, first], 1)
    firsts = cat([first, first], 0)
    tri2 = cat([tri, tri], 1)
    strict, upto = row > col, row >= col
    P, H = range(PAIRS), range(2 * PAIRS)

    def swap_maps(h):
        part = pl.ds(h * quarter, quarter)
        return pltpu.make_async_remote_copy(
            src_ref=mu.at[other_core, part],
            dst_ref=sib.at[part],
            send_sem=s0.at[h],
            recv_sem=r0.at[h],
            device_id=sibling,
            device_id_type=MESH,
        )

    def send_map(h, k):
        place = lax.rem(chip // 2 + quarter + mirror * k, quarter)
        to = 2 * place + h
        return to, pltpu.make_async_remote_copy(
            src_ref=chip_maps.at[h * quarter + place],
            dst_ref=maps.at[chip],
            send_sem=s1.at[h, k],
            recv_sem=r1.at[chip],
            device_id={"ctx": base + 2 * to + core},
            device_id_type=MESH,
        )

    def forward(h):
        swap_maps(h).wait_recv()
        slots = [h * quarter + i for i in range(quarter)]
        own, theirs = [mu[core, i] for i in slots], [sib[i] for i in slots]
        earlier = [jnp.where(core == 0, a, b) for a, b in zip(own, theirs)]
        later = [jnp.where(core == 0, b, a) for a, b in zip(own, theirs)]
        joined = later_all(later, earlier)
        for i, slot in enumerate(slots):
            chip_maps[slot] = joined[i]
            first_maps[slot] = earlier[i]
        for k in [2, 1, 3, 0]:
            to, copy = send_map(h, k)

            @pl.when(to != chip)
            def _():
                copy.start()

    def masked_scores(x, yh, yl):
        xh, xl = split(x)
        xr, yr = half_roll(xl), half_roll(yh)
        zero = jnp.zeros_like(xh)
        a = cat([jnp.where(first, xh, xr), jnp.where(first, xh, zero)], 1)
        b = cat([jnp.where(first, xr, xh), jnp.where(first, zero, xh)], 1)
        return [
            dot(a, cat([jnp.where(firsts, yh, yr), yl], 1), NT),
            dot(b, cat([jnp.where(firsts, yr, yh), yl], 1), NT),
        ]

    def half_of_heads(g, carry):
        def columns(ref, p):
            start = (p // 2) * (width // 2) + g * (width // 4) + (p % 2) * 128
            return ref[:, pl.ds(pl.multiple_of(start, 128), 128)]

        hid = ready[...]
        recv, keyv, valv, dirv = [[columns(a, p) for p in P] for a in (rec, key, val, unit)]
        logd = [
            -0.606531 * jax.nn.sigmoid(dot(hid[:, :128], columns(du, p)) + columns(db, p))
            for p in P
        ]
        rate = [jax.nn.sigmoid(dot(hid[:, 128:], columns(ru, p)) + columns(rb, p)) for p in P]
        cum = []
        for p in P:
            l1, l2 = split(logd[p])
            l3 = (logd[p] - l1.astype(F32) - l2.astype(F32)).astype(BF16)
            cum.append(dot(tri2, cat([l1, l2], 0)) + dot(tri, l3))
        mid = [cum[p][T // 2 - 1 : T // 2] for p in P]
        last = [cum[p][T - 1 :] for p in P]
        e_out = [jnp.exp(mid[p] - cum[p]) for p in P]
        dir_in = [dirv[p] * jnp.exp(cum[p] - logd[p] - mid[p]) for p in P]
        read_in = [recv[p].astype(F32) * jnp.exp(cum[p] - mid[p]) for p in P]
        key_out = [keyv[p].astype(F32) * e_out[p] for p in P]
        rem_out = [rate[p] * dirv[p] * e_out[p] for p in P]
        e_mid = [jnp.exp(mid[p]) for p in P]
        e_end = [jnp.exp(last[p] - mid[p]) for p in P]
        e_all = [jnp.exp(last[p]) for p in P]
        scores = []
        for p in P:
            scores += masked_scores(dir_in[p], *split(cat([key_out[p], rem_out[p]], 0)))
        a_kk = [jnp.where(strict, scores[h][:, :T], 0.0) for h in H]
        low = [jnp.where(strict, scores[h][:, T:], 0.0) for h in H]

        @pl.when(g == 1)
        def _():
            forward(0)

        inv = unit_inverse(low, row, col)
        kv = [dot(cat(split(a_kk[h]), 1), cat([valv[h // 2]] * 2, 0)) for h in H]
        right = [
            cat([dir_in[p] * e_mid[p], jnp.where(first, kv[2 * p], kv[2 * p + 1])], 1) for p in P
        ]
        sol = [mm3(inv[h], right[h // 2]) for h in H]
        low_lane = iota((64, 128), 1) < 64
        solved = [jnp.where(first2, sol[2 * p], sol[2 * p + 1]) for p in P]
        ends = [split(cat([-rem_out[p] * e_end[p], key_out[p] * e_end[p]], 0).T) for p in P]
        made = []
        for p in P:
            wh, wl = split(solved[p])
            lh, ll = ends[p]
            wide = cat([wh, cat([jnp.zeros((T, 128), BF16), valv[p]], 1)], 0)
            made.append(dot(lh, wide) + dot(ll, wide) + dot(lh[:, :T], wl))
        trans = [made[p][:, :128] + eye * e_all[p] for p in P]
        added = [made[p][:, 128:] for p in P]
        for p in P:
            slot = g * quarter + 2 * (p % 2)
            mu[p // 2, slot] = jnp.where(low_lane, trans[p][:64], half_roll(added[p][:64]))
            mu[p // 2, slot + 1] = jnp.where(low_lane, half_roll(trans[p][64:]), added[p][64:])
        swap_maps(g).start()
        for p in P:
            solved_ref[g, p] = solved[p]
            reff[g, p] = read_in[p] * e_mid[p]
            cent[g, p] = read_in[p]
            outer[g, p] = cat([key_out[p], rem_out[p]], 0)
        return carry

    lax.fori_loop(0, 2, half_of_heads, 0)

    def reads_of(i, carry):
        g, side = i // 2, lax.rem(i, 2)
        pairs = [2 * side, 2 * side + 1]
        start = side * (width // 2) + g * (width // 4)
        values = val[:, pl.ds(pl.multiple_of(start, 256), 256)]
        solved = [solved_ref[g, p] for p in pairs]
        inner = [(cent[g, p], outer[g, p]) for p in pairs]
        before = [reff[g, p] for p in pairs]
        scores = [masked_scores(x, *split(o)) for x, o in inner]
        left = [
            split(
                cat(
                    [
                        cat([jnp.where(upto, -a[:, T:], 0.0), jnp.where(upto, a[:, :T], 0.0)], 1)
                        for a in both
                    ],
                    0,
                )
            )
            for both in scores
        ]
        made = []
        for k in range(2):
            wh, wl = split(solved[k])
            zero = jnp.zeros((T, 128), BF16)
            wide = cat([wh, cat([zero, values[:, 128 * k : 128 * k + 128]], 1)], 0)
            lh, ll = left[k]
            made.append(dot(lh, wide) + dot(ll, wide) + dot(lh[:, :T], wl))
        reads = [jnp.where(first2, a[:T], a[T:]) for a in made]
        for k in range(2):
            reff[g, pairs[k]] = before[k] + reads[k][:, :128]
            base_ref[g, pairs[k]] = reads[k][:, 128:]
        return carry

    reads_of(0, 0)
    forward(1)
    lax.fori_loop(1, 4, reads_of, 0)

    maps[chip] = chip_maps[my_slot]
    for step in far:
        source = lax.rem(chip + step, chips)
        pltpu.make_async_remote_copy(
            src_ref=chip_maps.at[0],
            dst_ref=maps.at[source],
            send_sem=s1.at[0, 0],
            recv_sem=r1.at[source],
            device_id={"ctx": base + 2 * source + core},
            device_id_type=MESH,
        ).wait_recv()
    prefix = [maps[d] for d in range(chips)]
    size = 1
    while size < chips:
        lows = list(range(size, chips, 2 * size))
        joined = later_all(
            [cat(prefix[low : low + size], 0) for low in lows], [prefix[low - 1] for low in lows]
        )
        for low, group in zip(lows, joined):
            for d in range(size):
                prefix[low + d] = group[64 * d : 64 * d + 64]
        size *= 2
    row_total[...] = prefix[chips - 1]

    def send_total(r):
        return pltpu.make_async_remote_copy(
            src_ref=row_total,
            dst_ref=row_totals.at[y],
            send_sem=s2.at[r],
            recv_sem=r2.at[y],
            device_id={"ctx": r * n + me},
            device_id_type=MESH,
        )

    for r in range(1, nrow):

        @pl.when(r > y)
        def _():
            send_total(r).start()

    begin = start_ref[...]
    state = cat([begin, begin], 1)
    for r in range(nrow - 1):

        @pl.when(r < y)
        def _():
            pltpu.make_async_remote_copy(
                src_ref=row_total,
                dst_ref=row_totals.at[r],
                send_sem=s2.at[r],
                recv_sem=r2.at[r],
                device_id={"ctx": r * n + me},
                device_id_type=MESH,
            ).wait_recv()

    after_first, others_map = later_all(
        [row_totals[0], row_totals[2]], [state, row_totals[1]]
    )
    others_map = jnp.where(y == 3, others_map, row_totals[1])
    after_rows = later_of(others_map, after_first)
    state = jnp.where(y == 0, state, jnp.where(y == 1, after_first, after_rows))
    after_state = later_of(cat(prefix[: chips - 1], 0), state)
    packs = [pack_state(state)]
    packs += [pack_state(after_state[64 * d - 64 : 64 * d]) for d in range(1, chips)]
    for d in range(chips):
        states[d] = packs[d]
    third = []
    for step, other in enumerate(others):
        copy = pltpu.make_async_remote_copy(
            src_ref=states.at[other],
            dst_ref=got.at[my_slot],
            send_sem=s3.at[step],
            recv_sem=r3.at[my_slot],
            device_id={"ctx": base + 2 * other + core},
            device_id_type=MESH,
        )
        copy.start()
        third.append(copy)
    got[my_slot] = states[chip]

    def swap_states(h):
        part = pl.ds(h * quarter, quarter)
        return pltpu.make_async_remote_copy(
            src_ref=give.at[part],
            dst_ref=starts.at[core, part],
            send_sem=s4.at[h],
            recv_sem=r4.at[h],
            device_id=sibling,
            device_id_type=MESH,
        )

    def take(h):
        slots = range(h * quarter, h * quarter + quarter)
        for slot in slots:

            @pl.when(slot != my_slot)
            def _():
                pltpu.make_async_remote_copy(
                    src_ref=states.at[0],
                    dst_ref=got.at[slot],
                    send_sem=s3.at[0],
                    recv_sem=r3.at[slot],
                    device_id=sibling,
                    device_id_type=MESH,
                ).wait_recv()

        packed = [got[slot] for slot in slots]
        full = [cat([half_roll(a), a], 0) for a in packed]
        moved = later_all([first_maps[slot] for slot in slots], full)
        next_packed = [pack_state(a) for a in moved]
        for i, slot in enumerate(slots):
            give[slot] = jnp.where(core == 0, next_packed[i], packed[i])
        swap_states(h).start()
        for i, slot in enumerate(slots):
            starts[core, slot] = jnp.where(core == 0, packed[i], next_packed[i])

    lane = iota((64, 128), 1) < 64
    mean64 = (half.astype(F32) / 64).astype(BF16)
    mean2 = cat([mean64, mean64], 0)

    def finish(side, h):
        Q = range(2)
        state = []
        for q in Q:
            a, b = [starts[side, h * quarter + 2 * q + k] for k in range(2)]
            both_a = cat([a, half_roll(a)], 0)
            both_b = cat([half_roll(b), b], 0)
            state.append(
                cat([jnp.where(lane, both_a, 0.0), jnp.where(lane, 0.0, both_b)], 0)
            )
        place = [(h, 2 * side + q) for q in Q]
        read = [mm3(reff[place[q]], state[q]) + base_ref[place[q]] for q in Q]
        centered = [a - dot(cat(split(a), 1), mean2) for a in read]
        var = [dot(cat(split(a * a), 1), mean2) for a in centered]
        normed = [(a * lax.rsqrt(b + 0.00064)).astype(BF16) for a, b in zip(centered, var)]
        for q in Q:
            start = side * (width // 2) + h * (width // 4) + 128 * q
            out[:, pl.ds(pl.multiple_of(start, 128), 128)] = normed[q]

    for h in range(2):
        take(h)
        finish(core, h)
        swap_states(h).wait_recv()
        finish(other_core, h)

    for h in range(2):
        swap_maps(h).wait_send()
        for k in range(quarter):
            to, copy = send_map(h, k)

            @pl.when(to != chip)
            def _():
                copy.wait_send()

    for r in range(1, nrow):

        @pl.when(r > y)
        def _():
            send_total(r).wait_send()

    for copy in [shift, swap_states(0), swap_states(1)] + scatter + edges + spread + third:
        copy.wait_send()


def mixed_of(x, mix, down, du, ru, db, rb, rec, key, val, start, nctx, nhead):
    T, width = x.shape
    n = start.shape[0]
    chips = n // 2
    nrow = nctx // n
    dma, vm = pltpu.SemaphoreType.DMA, pltpu.VMEM
    args = (x, mix, down, du, ru, db, rb, rec, key, val, start)
    return pl.pallas_call(
        functools.partial(mixed_kernel, nctx=nctx, nhead=nhead),
        in_specs=[pl.BlockSpec(memory_space=pl.ANY)] * len(args),
        out_specs=pl.BlockSpec(memory_space=pltpu.VMEM),
        out_shape=pltpu.VMEM((T, width), BF16),
        scratch_shapes=[vm(a.shape, a.dtype) for a in args[:-1]]
        + [vm((64, 64), F32), dma((len(args),))]
        + [
            vm((16, width), BF16),
            vm((T, 256), F32),
            vm((nhead - 1, T // nhead, 256), F32),
            vm((T, 256), BF16),
            dma((2 * nhead,)),
            dma((2 * nhead,)),
            vm((16, 256), F32),
            vm((nhead - 1, 16, 256), F32),
            vm((T, 256), BF16),
            dma((nhead - 1,)),
            dma((nhead - 1,)),
            vm((T, width), F32),
            vm((2, chips, 64, 128), F32),
            vm((2, PAIRS, T, 128), F32),
            vm((2, PAIRS, 2 * T, 128), F32),
            vm((2, PAIRS, T, 256), F32),
            vm((2, PAIRS, T, 128), F32),
            vm((2, PAIRS, T, 128), F32),
            vm((2, chips, 32, 128), F32),
            vm((chips, 64, 128), F32),
            vm((chips, 64, 128), F32),
            vm((chips, 64, 128), F32),
            vm((chips, 64, 128), F32),
            vm((64, 128), F32),
            vm((nrow, 64, 128), F32),
            vm((chips, 32, 128), F32),
            vm((chips, 32, 128), F32),
            vm((chips, 32, 128), F32),
        ]
        + [dma((2,)), dma((2,)), dma((2, chips // 2)), dma((chips,)), dma((nrow,)), dma((nrow,))]
        + [dma((chips,)), dma((chips,)), dma((2,)), dma((2,))],
        compiler_params=pltpu.CompilerParams(
            collective_id=0, has_side_effects=True, vmem_limit_bytes=40 * 1024 * 1024
        ),
    )(*[pltpu.with_memory_space_constraint(a, pltpu.HBM) for a in args])


def solution(mesh):
    nctx, nhead = mesh.shape["ctx"], mesh.shape["head"]

    def on_device(x, mix, down, du, ru, db, rb, rec, key, val, start):
        return mixed_of(
            x, mix[None], down, du, ru, db[None], rb[None], rec, key, val, start, nctx, nhead
        )

    P = jax.sharding.PartitionSpec
    both, wide = P("ctx", "head"), P("head")
    return jax.shard_map(
        on_device,
        mesh=mesh,
        in_specs=(both, wide, P("head", None), P(None, "head"), P(None, "head"), wide, wide)
        + (both,) * 3
        + (P("head", None, None),),
        out_specs=both,
        check_vma=False,
    )
```

```python
import functools
import jax
import jax.numpy as jnp
from jax import lax
from jax.experimental import pallas as pl
from jax.experimental.pallas import tpu as pltpu

F32 = jnp.float32
BF16 = jnp.bfloat16
NN = (((1,), (0,)), ((), ()))
NT = (((1,), (1,)), ((), ()))


def dot(a, b, dims=NN):
    return lax.dot_general(a, b, dims, preferred_element_type=F32)


def split(x):
    high = x.astype(BF16)
    return high, (x - high.astype(F32)).astype(BF16)


def cat(parts, axis):
    return jnp.concatenate(parts, axis=axis)


def mm3(a, b):
    ah, al = split(a)
    bh, bl = split(b)
    return dot(cat([ah, al], 1), cat([bh, bh], 0)) + dot(ah, bl)


def iota(shape, axis):
    return lax.broadcasted_iota(jnp.int32, shape, axis)


MESH = pl.DeviceIdType.MESH
PAIRS = 4


def half_roll(x):
    return pltpu.roll(x, 64, 1)


def later_all(laters, earliers):
    left = [split(a) for a in laters]
    right = [[cat([part, jnp.zeros_like(part)], 0) for part in split(b)] for b in earliers]
    main = [dot(cat([a, al], 1), cat([b, b], 0)) for (a, al), (b, _) in zip(left, right)]
    rest = [dot(a, bl) for (a, _), (_, bl) in zip(left, right)]
    lane = [iota(a.shape, 1) < 64 for a in laters]
    return [m + r + jnp.where(k, 0.0, a) for m, r, k, a in zip(main, rest, lane, laters)]


def later_of(map_later, earlier):
    return later_all([map_later], [earlier])[0]


def pack_state(full):
    lane = iota((32, 128), 1) < 64
    return jnp.where(lane, half_roll(full[:32]), full[32:])


def unit_inverse(low, row, col):
    T = low[0].shape[0]
    eye = (row == col).astype(F32)
    block = row // 8 == col // 8
    d = [jnp.where(block, a, 0.0) for a in low]
    d2 = [mm3(a, a) for a in d]
    dd = [mm3(cat([a, b], 0), b) for a, b in zip(d, d2)]
    poly = [eye - a + b - c[:T] for a, b, c in zip(d, d2, dd)]
    inv = [a + mm3(a, c[T:]) for a, c in zip(poly, dd)]
    size = 8
    while size < T:
        blocks = T // size

        def rows_of(a, odd):
            return [a[size * i : size * i + size] for i in range(odd, blocks, 2)]

        below = cat(rows_of(row, 1), 0) // size - 1 == cat(rows_of(col, 1), 0) // size
        step = [
            mm3(jnp.where(below, cat(rows_of(a, 1), 0), 0.0), b) for a, b in zip(low, inv)
        ]
        new = []
        for a, b in zip(inv, step):
            parts = [b[size * (i // 2) : size * (i // 2) + size] for i in range(blocks)]
            odd = cat(rows_of(a, 1), 0)
            odd = odd - mm3(odd, cat(parts, 0))
            merged = []
            for i, even in enumerate(rows_of(a, 0)):
                merged += [even, odd[size * i : size * i + size]]
            new.append(cat(merged, 0))
        inv = new
        size *= 2
    return inv


def mixed_kernel(
    x_h, mix_h, down_h, du_h, ru_h, db_h, rb_h, rec_h, key_h, val_h, start_h,
    out,
    x_ref, mix_ref, down_ref, du, ru, db, rb, rec, key, val, start_ref, loads,
    tail, total, shares, hidden, sends, recvs,
    edge_sum, edge_sums, ready, edge_send, edge_recv,
    unit, mu, cent, outer, solved_ref, reff, base_ref, starts,
    sib, first_maps, chip_maps, maps, row_total, row_totals, states, got, give,
    s0, r0, s1, r1, s2, r2, s3, r3, s4, r4,
    *, nctx, nhead,
):
    ctx, head = lax.axis_index("ctx"), lax.axis_index("head")
    T, width = x_ref.shape
    n = mu.shape[0] * mu.shape[1]
    chips = n // 2
    quarter = chips // 2
    nrow = nctx // n
    y, me = ctx // n, lax.rem(ctx, n)
    chip, core = me // 2, lax.rem(me, 2)
    other_core = 1 - core
    base = y * n
    my_slot = chip // 2 + quarter * lax.rem(chip, 2)
    my_head = core * chips + my_slot
    sibling = {"ctx": base + chip * 2 + other_core}

    fetch = []
    for i, (src, dst) in enumerate(
        [(x_h, x_ref), (mix_h, mix_ref), (down_h, down_ref), (key_h, key), (du_h, du), (ru_h, ru)]
        + [(db_h, db), (rb_h, rb), (rec_h, rec), (val_h, val), (start_h.at[my_head], start_ref)]
    ):
        fetch.append(pltpu.make_async_copy(src, dst, loads.at[i]))

    row_totals[...] = jnp.zeros_like(row_totals)
    after, behind = lax.rem(ctx + 1, nctx), lax.rem(ctx + nctx - 1, nctx)
    mirror = 1 - 2 * core
    mates = [lax.rem(head + nhead + mirror * step, nhead) for step in (2, 1, 3)]
    far = sorted(range(1, chips), key=lambda d: -min(d, chips - d))
    others = [lax.rem(chip + chips + mirror * step, chips) for step in far]
    rows = [lax.rem(y + step, nrow) for step in range(1, nrow)]
    barrier = pltpu.get_barrier_semaphore()
    for other in [base + 2 * o + core for o in others] + [r * n + me for r in rows]:
        pl.semaphore_signal(barrier, inc=1, device_id={"ctx": other}, device_id_type=MESH)
    for mate in mates:
        pl.semaphore_signal(barrier, inc=1, device_id={"head": mate}, device_id_type=MESH)
    for other in [after, behind]:
        pl.semaphore_signal(barrier, inc=1, device_id={"ctx": other}, device_id_type=MESH)
    pl.semaphore_signal(barrier, inc=1, device_id=sibling, device_id_type=MESH)
    for copy in fetch[:4]:
        copy.start()

    for i in range(3):
        fetch[i].wait()
    for copy in fetch[4:]:
        copy.start()
    mix = mix_ref[...]
    xf = x_ref[...].astype(F32)
    before = pltpu.roll(xf, 1, 0)
    shifted = (xf + (before - xf) * mix).astype(BF16)
    total[...] = dot(shifted, down_ref[...])

    row, col = iota((T, T), 0), iota((T, T), 1)
    tri = (row >= col).astype(BF16)
    half = (row // 64 == col // 64).astype(BF16)
    half2 = cat([half, half], 0)
    fetch[3].wait()
    for p in range(width // 128):
        kf = key[:, 128 * p : 128 * p + 128].astype(F32)
        square = dot(cat(split(kf * kf), 1), half2)
        unit[:, 128 * p : 128 * p + 128] = kf * lax.rsqrt(square + 1e-06)
    pl.semaphore_wait(barrier, 2 + nhead - 1 + 1 + chips - 1 + nrow - 1)

    shift = pltpu.make_async_remote_copy(
        src_ref=x_h.at[pl.ds(T - 16, 16)],
        dst_ref=tail,
        send_sem=sends.at[0],
        recv_sem=recvs.at[0],
        device_id={"ctx": after},
        device_id_type=MESH,
    )
    shift.start()

    share = T // nhead
    mine = pl.ds(pl.multiple_of(head * share, share), share)
    scatter, spread = [], []
    for step, mate in enumerate(mates):
        copy = pltpu.make_async_remote_copy(
            src_ref=total.at[pl.ds(pl.multiple_of(mate * share, share), share)],
            dst_ref=shares.at[step],
            send_sem=sends.at[1 + step],
            recv_sem=recvs.at[1 + step],
            device_id={"head": mate},
            device_id_type=MESH,
        )
        copy.start()
        scatter.append(copy)

    shift.wait_recv()
    xt = x_ref[0:16, :].astype(F32)
    edge = jnp.where(ctx > 0, tail[...].astype(F32)[15:16], 0.0)
    before = jnp.where(iota((16, width), 0) == 0, edge, pltpu.roll(xt, 1, 0))
    shifted = (xt + (before - xt) * mix).astype(BF16)
    edge_sum[...] = dot(shifted, down_ref[...])
    edges = []
    for step, mate in enumerate(mates):
        copy = pltpu.make_async_remote_copy(
            src_ref=edge_sum,
            dst_ref=edge_sums.at[step],
            send_sem=edge_send.at[step],
            recv_sem=edge_recv.at[step],
            device_id={"head": mate},
            device_id_type=MESH,
        )
        copy.start()
        edges.append(copy)

    grand = total[mine, :]
    for step, copy in enumerate(scatter):
        copy.wait_recv()
        grand = grand + shares[step]
    hidden[mine, :] = cat([jnp.tanh(grand[:, :128]), grand[:, 128:]], 1).astype(BF16)
    for step, mate in enumerate(mates):
        copy = pltpu.make_async_remote_copy(
            src_ref=hidden.at[mine],
            dst_ref=hidden.at[mine],
            send_sem=sends.at[nhead + step],
            recv_sem=recvs.at[nhead + step],
            device_id={"head": mate},
            device_id_type=MESH,
        )
        copy.start()
        spread.append(copy)
    for i in range(4, len(fetch)):
        fetch[i].wait()
    first_row = edge_sum[0:8, :]
    for step, copy in enumerate(edges):
        copy.wait_recv()
        first_row = first_row + edge_sums[step, 0:8, :]
    first_row = cat([jnp.tanh(first_row[:1, :128]), first_row[:1, 128:]], 1)
    for copy in spread:
        copy.wait_recv()
    ready[...] = jnp.where(
        iota((T, 256), 0) == 0, first_row, hidden[...].astype(F32)
    ).astype(BF16)

    eye = (row == col).astype(F32)
    first = iota((T, 128), 1) < 64
    first2 = cat([first, first], 1)
    firsts = cat([first, first], 0)
    tri2 = cat([tri, tri], 1)
    strict, upto = row > col, row >= col
    P, H = range(PAIRS), range(2 * PAIRS)

    def swap_maps(h):
        part = pl.ds(h * quarter, quarter)
        return pltpu.make_async_remote_copy(
            src_ref=mu.at[other_core, part],
            dst_ref=sib.at[part],
            send_sem=s0.at[h],
            recv_sem=r0.at[h],
            device_id=sibling,
            device_id_type=MESH,
        )

    def send_map(h, k):
        place = lax.rem(chip // 2 + quarter + mirror * k, quarter)
        to = 2 * place + h
        return to, pltpu.make_async_remote_copy(
            src_ref=chip_maps.at[h * quarter + place],
            dst_ref=maps.at[chip],
            send_sem=s1.at[h, k],
            recv_sem=r1.at[chip],
            device_id={"ctx": base + 2 * to + core},
            device_id_type=MESH,
        )

    def forward(h):
        swap_maps(h).wait_recv()
        slots = [h * quarter + i for i in range(quarter)]
        own, theirs = [mu[core, i] for i in slots], [sib[i] for i in slots]
        earlier = [jnp.where(core == 0, a, b) for a, b in zip(own, theirs)]
        later = [jnp.where(core == 0, b, a) for a, b in zip(own, theirs)]
        joined = later_all(later, earlier)
        for i, slot in enumerate(slots):
            chip_maps[slot] = joined[i]
            first_maps[slot] = earlier[i]
        for k in [2, 1, 3, 0]:
            to, copy = send_map(h, k)

            @pl.when(to != chip)
            def _():
                copy.start()

    def masked_scores(x, yh, yl):
        xh, xl = split(x)
        xr, yr = half_roll(xl), half_roll(yh)
        zero = jnp.zeros_like(xh)
        a = cat([jnp.where(first, xh, xr), jnp.where(first, xh, zero)], 1)
        b = cat([jnp.where(first, xr, xh), jnp.where(first, zero, xh)], 1)
        return [
            dot(a, cat([jnp.where(firsts, yh, yr), yl], 1), NT),
            dot(b, cat([jnp.where(firsts, yr, yh), yl], 1), NT),
        ]

    def half_of_heads(g, carry):
        def columns(ref, p):
            start = (p // 2) * (width // 2) + g * (width // 4) + (p % 2) * 128
            return ref[:, pl.ds(pl.multiple_of(start, 128), 128)]

        hid = ready[...]
        recv, keyv, valv, dirv = [[columns(a, p) for p in P] for a in (rec, key, val, unit)]
        logd = [
            -0.606531 * jax.nn.sigmoid(dot(hid[:, :128], columns(du, p)) + columns(db, p))
            for p in P
        ]
        rate = [jax.nn.sigmoid(dot(hid[:, 128:], columns(ru, p)) + columns(rb, p)) for p in P]
        cum = []
        for p in P:
            l1, l2 = split(logd[p])
            l3 = (logd[p] - l1.astype(F32) - l2.astype(F32)).astype(BF16)
            cum.append(dot(tri2, cat([l1, l2], 0)) + dot(tri, l3))
        mid = [cum[p][T // 2 - 1 : T // 2] for p in P]
        last = [cum[p][T - 1 :] for p in P]
        e_out = [jnp.exp(mid[p] - cum[p]) for p in P]
        dir_in = [dirv[p] * jnp.exp(cum[p] - logd[p] - mid[p]) for p in P]
        read_in = [recv[p].astype(F32) * jnp.exp(cum[p] - mid[p]) for p in P]
        key_out = [keyv[p].astype(F32) * e_out[p] for p in P]
        rem_out = [rate[p] * dirv[p] * e_out[p] for p in P]
        e_mid = [jnp.exp(mid[p]) for p in P]
        e_end = [jnp.exp(last[p] - mid[p]) for p in P]
        e_all = [jnp.exp(last[p]) for p in P]
        scores = []
        for p in P:
            scores += masked_scores(dir_in[p], *split(cat([key_out[p], rem_out[p]], 0)))
        a_kk = [jnp.where(strict, scores[h][:, :T], 0.0) for h in H]
        low = [jnp.where(strict, scores[h][:, T:], 0.0) for h in H]

        @pl.when(g == 1)
        def _():
            forward(0)

        inv = unit_inverse(low, row, col)
        kv = [dot(cat(split(a_kk[h]), 1), cat([valv[h // 2]] * 2, 0)) for h in H]
        right = [
            cat([dir_in[p] * e_mid[p], jnp.where(first, kv[2 * p], kv[2 * p + 1])], 1) for p in P
        ]
        sol = [mm3(inv[h], right[h // 2]) for h in H]
        low_lane = iota((64, 128), 1) < 64
        solved = [jnp.where(first2, sol[2 * p], sol[2 * p + 1]) for p in P]
        ends = [split(cat([-rem_out[p] * e_end[p], key_out[p] * e_end[p]], 0).T) for p in P]
        made = []
        for p in P:
            wh, wl = split(solved[p])
            lh, ll = ends[p]
            wide = cat([wh, cat([jnp.zeros((T, 128), BF16), valv[p]], 1)], 0)
            made.append(dot(lh, wide) + dot(ll, wide) + dot(lh[:, :T], wl))
        trans = [made[p][:, :128] + eye * e_all[p] for p in P]
        added = [made[p][:, 128:] for p in P]
        for p in P:
            slot = g * quarter + 2 * (p % 2)
            mu[p // 2, slot] = jnp.where(low_lane, trans[p][:64], half_roll(added[p][:64]))
            mu[p // 2, slot + 1] = jnp.where(low_lane, half_roll(trans[p][64:]), added[p][64:])
        swap_maps(g).start()
        for p in P:
            solved_ref[g, p] = solved[p]
            reff[g, p] = read_in[p] * e_mid[p]
            cent[g, p] = read_in[p]
            outer[g, p] = cat([key_out[p], rem_out[p]], 0)
        return carry

    lax.fori_loop(0, 2, half_of_heads, 0)

    def reads_of(i, carry):
        g, side = i // 2, lax.rem(i, 2)
        pairs = [2 * side, 2 * side + 1]
        start = side * (width // 2) + g * (width // 4)
        values = val[:, pl.ds(pl.multiple_of(start, 256), 256)]
        solved = [solved_ref[g, p] for p in pairs]
        inner = [(cent[g, p], outer[g, p]) for p in pairs]
        before = [reff[g, p] for p in pairs]
        scores = [masked_scores(x, *split(o)) for x, o in inner]
        left = [
            split(
                cat(
                    [
                        cat([jnp.where(upto, -a[:, T:], 0.0), jnp.where(upto, a[:, :T], 0.0)], 1)
                        for a in both
                    ],
                    0,
                )
            )
            for both in scores
        ]
        made = []
        for k in range(2):
            wh, wl = split(solved[k])
            zero = jnp.zeros((T, 128), BF16)
            wide = cat([wh, cat([zero, values[:, 128 * k : 128 * k + 128]], 1)], 0)
            lh, ll = left[k]
            made.append(dot(lh, wide) + dot(ll, wide) + dot(lh[:, :T], wl))
        reads = [jnp.where(first2, a[:T], a[T:]) for a in made]
        for k in range(2):
            reff[g, pairs[k]] = before[k] + reads[k][:, :128]
            base_ref[g, pairs[k]] = reads[k][:, 128:]
        return carry

    forward(1)
    lax.fori_loop(0, 4, reads_of, 0)

    maps[chip] = chip_maps[my_slot]
    for step in far:
        source = lax.rem(chip + step, chips)
        pltpu.make_async_remote_copy(
            src_ref=chip_maps.at[0],
            dst_ref=maps.at[source],
            send_sem=s1.at[0, 0],
            recv_sem=r1.at[source],
            device_id={"ctx": base + 2 * source + core},
            device_id_type=MESH,
        ).wait_recv()
    prefix = [maps[d] for d in range(chips)]
    size = 1
    while size < chips:
        lows = list(range(size, chips, 2 * size))
        joined = later_all(
            [cat(prefix[low : low + size], 0) for low in lows], [prefix[low - 1] for low in lows]
        )
        for low, group in zip(lows, joined):
            for d in range(size):
                prefix[low + d] = group[64 * d : 64 * d + 64]
        size *= 2
    row_total[...] = prefix[chips - 1]

    def send_total(r):
        return pltpu.make_async_remote_copy(
            src_ref=row_total,
            dst_ref=row_totals.at[y],
            send_sem=s2.at[r],
            recv_sem=r2.at[y],
            device_id={"ctx": r * n + me},
            device_id_type=MESH,
        )

    for r in range(1, nrow):

        @pl.when(r > y)
        def _():
            send_total(r).start()

    begin = start_ref[...]
    state = cat([begin, begin], 1)
    for r in range(nrow - 1):

        @pl.when(r < y)
        def _():
            pltpu.make_async_remote_copy(
                src_ref=row_total,
                dst_ref=row_totals.at[r],
                send_sem=s2.at[r],
                recv_sem=r2.at[r],
                device_id={"ctx": r * n + me},
                device_id_type=MESH,
            ).wait_recv()

    after_first, others_map = later_all(
        [row_totals[0], row_totals[2]], [state, row_totals[1]]
    )
    others_map = jnp.where(y == 3, others_map, row_totals[1])
    after_rows = later_of(others_map, after_first)
    state = jnp.where(y == 0, state, jnp.where(y == 1, after_first, after_rows))
    after_state = later_of(cat(prefix[: chips - 1], 0), state)
    packs = [pack_state(state)]
    packs += [pack_state(after_state[64 * d - 64 : 64 * d]) for d in range(1, chips)]
    for d in range(chips):
        states[d] = packs[d]
    third = []
    for step, other in enumerate(others):
        copy = pltpu.make_async_remote_copy(
            src_ref=states.at[other],
            dst_ref=got.at[my_slot],
            send_sem=s3.at[step],
            recv_sem=r3.at[my_slot],
            device_id={"ctx": base + 2 * other + core},
            device_id_type=MESH,
        )
        copy.start()
        third.append(copy)
    got[my_slot] = states[chip]

    def swap_states(h):
        part = pl.ds(h * quarter, quarter)
        return pltpu.make_async_remote_copy(
            src_ref=give.at[part],
            dst_ref=starts.at[core, part],
            send_sem=s4.at[h],
            recv_sem=r4.at[h],
            device_id=sibling,
            device_id_type=MESH,
        )

    def take(h):
        slots = range(h * quarter, h * quarter + quarter)
        for slot in slots:

            @pl.when(slot != my_slot)
            def _():
                pltpu.make_async_remote_copy(
                    src_ref=states.at[0],
                    dst_ref=got.at[slot],
                    send_sem=s3.at[0],
                    recv_sem=r3.at[slot],
                    device_id=sibling,
                    device_id_type=MESH,
                ).wait_recv()

        packed = [got[slot] for slot in slots]
        full = [cat([half_roll(a), a], 0) for a in packed]
        moved = later_all([first_maps[slot] for slot in slots], full)
        next_packed = [pack_state(a) for a in moved]
        for i, slot in enumerate(slots):
            give[slot] = jnp.where(core == 0, next_packed[i], packed[i])
        swap_states(h).start()
        for i, slot in enumerate(slots):
            starts[core, slot] = jnp.where(core == 0, packed[i], next_packed[i])

    lane = iota((64, 128), 1) < 64
    mean64 = (half.astype(F32) / 64).astype(BF16)
    mean2 = cat([mean64, mean64], 0)

    def finish(side, h):
        Q = range(2)
        state = []
        for q in Q:
            a, b = [starts[side, h * quarter + 2 * q + k] for k in range(2)]
            both_a = cat([a, half_roll(a)], 0)
            both_b = cat([half_roll(b), b], 0)
            state.append(
                cat([jnp.where(lane, both_a, 0.0), jnp.where(lane, 0.0, both_b)], 0)
            )
        place = [(h, 2 * side + q) for q in Q]
        read = [mm3(reff[place[q]], state[q]) + base_ref[place[q]] for q in Q]
        centered = [a - dot(cat(split(a), 1), mean2) for a in read]
        var = [dot(cat(split(a * a), 1), mean2) for a in centered]
        normed = [(a * lax.rsqrt(b + 0.00064)).astype(BF16) for a, b in zip(centered, var)]
        for q in Q:
            start = side * (width // 2) + h * (width // 4) + 128 * q
            out[:, pl.ds(pl.multiple_of(start, 128), 128)] = normed[q]

    for h in range(2):
        take(h)
        finish(core, h)
        swap_states(h).wait_recv()
        finish(other_core, h)

    for h in range(2):
        swap_maps(h).wait_send()
        for k in range(quarter):
            to, copy = send_map(h, k)

            @pl.when(to != chip)
            def _():
                copy.wait_send()

    for r in range(1, nrow):

        @pl.when(r > y)
        def _():
            send_total(r).wait_send()

    for copy in [shift, swap_states(0), swap_states(1)] + scatter + edges + spread + third:
        copy.wait_send()


def mixed_of(x, mix, down, du, ru, db, rb, rec, key, val, start, nctx, nhead):
    T, width = x.shape
    n = start.shape[0]
    chips = n // 2
    nrow = nctx // n
    dma, vm = pltpu.SemaphoreType.DMA, pltpu.VMEM
    args = (x, mix, down, du, ru, db, rb, rec, key, val, start)
    return pl.pallas_call(
        functools.partial(mixed_kernel, nctx=nctx, nhead=nhead),
        in_specs=[pl.BlockSpec(memory_space=pl.ANY)] * len(args),
        out_specs=pl.BlockSpec(memory_space=pltpu.VMEM),
        out_shape=pltpu.VMEM((T, width), BF16),
        scratch_shapes=[vm(a.shape, a.dtype) for a in args[:-1]]
        + [vm((64, 64), F32), dma((len(args),))]
        + [
            vm((16, width), BF16),
            vm((T, 256), F32),
            vm((nhead - 1, T // nhead, 256), F32),
            vm((T, 256), BF16),
            dma((2 * nhead,)),
            dma((2 * nhead,)),
            vm((16, 256), F32),
            vm((nhead - 1, 16, 256), F32),
            vm((T, 256), BF16),
            dma((nhead - 1,)),
            dma((nhead - 1,)),
            vm((T, width), F32),
            vm((2, chips, 64, 128), F32),
            vm((2, PAIRS, T, 128), F32),
            vm((2, PAIRS, 2 * T, 128), F32),
            vm((2, PAIRS, T, 256), F32),
            vm((2, PAIRS, T, 128), F32),
            vm((2, PAIRS, T, 128), F32),
            vm((2, chips, 32, 128), F32),
            vm((chips, 64, 128), F32),
            vm((chips, 64, 128), F32),
            vm((chips, 64, 128), F32),
            vm((chips, 64, 128), F32),
            vm((64, 128), F32),
            vm((nrow, 64, 128), F32),
            vm((chips, 32, 128), F32),
            vm((chips, 32, 128), F32),
            vm((chips, 32, 128), F32),
        ]
        + [dma((2,)), dma((2,)), dma((2, chips // 2)), dma((chips,)), dma((nrow,)), dma((nrow,))]
        + [dma((chips,)), dma((chips,)), dma((2,)), dma((2,))],
        compiler_params=pltpu.CompilerParams(
            collective_id=0, has_side_effects=True, vmem_limit_bytes=40 * 1024 * 1024
        ),
    )(*[pltpu.with_memory_space_constraint(a, pltpu.HBM) for a in args])


def solution(mesh):
    nctx, nhead = mesh.shape["ctx"], mesh.shape["head"]

    def on_device(x, mix, down, du, ru, db, rb, rec, key, val, start):
        return mixed_of(
            x, mix[None], down, du, ru, db[None], rb[None], rec, key, val, start, nctx, nhead
        )

    P = jax.sharding.PartitionSpec
    both, wide = P("ctx", "head"), P("head")
    return jax.shard_map(
        on_device,
        mesh=mesh,
        in_specs=(both, wide, P("head", None), P(None, "head"), P(None, "head"), wide, wide)
        + (both,) * 3
        + (P("head", None, None),),
        out_specs=both,
        check_vma=False,
    )
```

```python
import functools
import jax
import jax.numpy as jnp
from jax import lax
from jax.experimental import pallas as pl
from jax.experimental.pallas import tpu as pltpu

F32 = jnp.float32
BF16 = jnp.bfloat16
NN = (((1,), (0,)), ((), ()))
NT = (((1,), (1,)), ((), ()))


def dot(a, b, dims=NN):
    return lax.dot_general(a, b, dims, preferred_element_type=F32)


def split(x):
    high = x.astype(BF16)
    return high, (x - high.astype(F32)).astype(BF16)


def cat(parts, axis):
    return jnp.concatenate(parts, axis=axis)


def mm3(a, b):
    ah, al = split(a)
    bh, bl = split(b)
    return dot(cat([ah, al], 1), cat([bh, bh], 0)) + dot(ah, bl)


def iota(shape, axis):
    return lax.broadcasted_iota(jnp.int32, shape, axis)


MESH = pl.DeviceIdType.MESH
PAIRS = 4


def half_roll(x):
    return pltpu.roll(x, 64, 1)


def later_all(laters, earliers):
    left = [split(a) for a in laters]
    right = [[cat([part, jnp.zeros_like(part)], 0) for part in split(b)] for b in earliers]
    main = [dot(cat([a, al], 1), cat([b, b], 0)) for (a, al), (b, _) in zip(left, right)]
    rest = [dot(a, bl) for (a, _), (_, bl) in zip(left, right)]
    lane = [iota(a.shape, 1) < 64 for a in laters]
    return [m + r + jnp.where(k, 0.0, a) for m, r, k, a in zip(main, rest, lane, laters)]


def later_of(map_later, earlier):
    return later_all([map_later], [earlier])[0]


def pack_state(full):
    lane = iota((32, 128), 1) < 64
    return jnp.where(lane, half_roll(full[:32]), full[32:])


def unit_inverse(low, row, col):
    T = low[0].shape[0]
    eye = (row == col).astype(F32)
    block = row // 8 == col // 8
    d = [jnp.where(block, a, 0.0) for a in low]
    d2 = [mm3(a, a) for a in d]
    dd = [mm3(cat([a, b], 0), b) for a, b in zip(d, d2)]
    poly = [eye - a + b - c[:T] for a, b, c in zip(d, d2, dd)]
    inv = [a + mm3(a, c[T:]) for a, c in zip(poly, dd)]
    size = 8
    while size < T:
        blocks = T // size

        def rows_of(a, odd):
            return [a[size * i : size * i + size] for i in range(odd, blocks, 2)]

        below = cat(rows_of(row, 1), 0) // size - 1 == cat(rows_of(col, 1), 0) // size
        step = [
            mm3(jnp.where(below, cat(rows_of(a, 1), 0), 0.0), b) for a, b in zip(low, inv)
        ]
        new = []
        for a, b in zip(inv, step):
            parts = [b[size * (i // 2) : size * (i // 2) + size] for i in range(blocks)]
            odd = cat(rows_of(a, 1), 0)
            odd = odd - mm3(odd, cat(parts, 0))
            merged = []
            for i, even in enumerate(rows_of(a, 0)):
                merged += [even, odd[size * i : size * i + size]]
            new.append(cat(merged, 0))
        inv = new
        size *= 2
    return inv


def mixed_kernel(
    x_h, mix_h, down_h, du_h, ru_h, db_h, rb_h, rec_h, key_h, val_h, start_h,
    out,
    x_ref, mix_ref, down_ref, du, ru, db, rb, rec, key, val, start_ref, loads,
    tail, total, shares, hidden, sends, recvs,
    edge_sum, edge_sums, ready, edge_send, edge_recv,
    unit, mu, cent, outer, solved_ref, reff, base_ref, starts,
    sib, first_maps, chip_maps, maps, row_total, row_totals, states, got, give,
    s0, r0, s1, r1, s2, r2, s3, r3, s4, r4,
    *, nctx, nhead,
):
    ctx, head = lax.axis_index("ctx"), lax.axis_index("head")
    T, width = x_ref.shape
    n = mu.shape[0] * mu.shape[1]
    chips = n // 2
    quarter = chips // 2
    nrow = nctx // n
    y, me = ctx // n, lax.rem(ctx, n)
    chip, core = me // 2, lax.rem(me, 2)
    other_core = 1 - core
    base = y * n
    my_slot = chip // 2 + quarter * lax.rem(chip, 2)
    my_head = core * chips + my_slot
    sibling = {"ctx": base + chip * 2 + other_core}

    fetch = []
    for i, (src, dst) in enumerate(
        [(x_h, x_ref), (mix_h, mix_ref), (down_h, down_ref), (key_h, key), (du_h, du), (ru_h, ru)]
        + [(db_h, db), (rb_h, rb), (rec_h, rec), (val_h, val), (start_h.at[my_head], start_ref)]
    ):
        fetch.append(pltpu.make_async_copy(src, dst, loads.at[i]))

    row_totals[...] = jnp.zeros_like(row_totals)
    after, behind = lax.rem(ctx + 1, nctx), lax.rem(ctx + nctx - 1, nctx)
    mirror = 1 - 2 * core
    mates = [lax.rem(head + nhead + mirror * step, nhead) for step in (2, 1, 3)]
    far = sorted(range(1, chips), key=lambda d: -min(d, chips - d))
    others = [lax.rem(chip + chips + mirror * step, chips) for step in far]
    rows = [lax.rem(y + step, nrow) for step in range(1, nrow)]
    barrier = pltpu.get_barrier_semaphore()
    for other in [base + 2 * o + core for o in others] + [r * n + me for r in rows]:
        pl.semaphore_signal(barrier, inc=1, device_id={"ctx": other}, device_id_type=MESH)
    for mate in mates:
        pl.semaphore_signal(barrier, inc=1, device_id={"head": mate}, device_id_type=MESH)
    for other in [after, behind]:
        pl.semaphore_signal(barrier, inc=1, device_id={"ctx": other}, device_id_type=MESH)
    pl.semaphore_signal(barrier, inc=1, device_id=sibling, device_id_type=MESH)
    for copy in fetch[:4]:
        copy.start()

    for i in range(3):
        fetch[i].wait()
    for copy in fetch[4:]:
        copy.start()
    mix = mix_ref[...]
    xf = x_ref[...].astype(F32)
    before = pltpu.roll(xf, 1, 0)
    shifted = (xf + (before - xf) * mix).astype(BF16)
    total[...] = dot(shifted, down_ref[...])

    row, col = iota((T, T), 0), iota((T, T), 1)
    tri = (row >= col).astype(BF16)
    half = (row // 64 == col // 64).astype(BF16)
    half2 = cat([half, half], 0)
    fetch[3].wait()
    for p in range(width // 128):
        kf = key[:, 128 * p : 128 * p + 128].astype(F32)
        square = dot(cat(split(kf * kf), 1), half2)
        unit[:, 128 * p : 128 * p + 128] = kf * lax.rsqrt(square + 1e-06)
    pl.semaphore_wait(barrier, 2 + nhead - 1 + 1 + chips - 1 + nrow - 1)

    shift = pltpu.make_async_remote_copy(
        src_ref=x_h.at[pl.ds(T - 16, 16)],
        dst_ref=tail,
        send_sem=sends.at[0],
        recv_sem=recvs.at[0],
        device_id={"ctx": after},
        device_id_type=MESH,
    )
    shift.start()

    share = T // nhead
    mine = pl.ds(pl.multiple_of(head * share, share), share)
    scatter, spread = [], []
    for step, mate in enumerate(mates):
        copy = pltpu.make_async_remote_copy(
            src_ref=total.at[pl.ds(pl.multiple_of(mate * share, share), share)],
            dst_ref=shares.at[step],
            send_sem=sends.at[1 + step],
            recv_sem=recvs.at[1 + step],
            device_id={"head": mate},
            device_id_type=MESH,
        )
        copy.start()
        scatter.append(copy)

    shift.wait_recv()
    xt = x_ref[0:16, :].astype(F32)
    edge = jnp.where(ctx > 0, tail[...].astype(F32)[15:16], 0.0)
    before = jnp.where(iota((16, width), 0) == 0, edge, pltpu.roll(xt, 1, 0))
    shifted = (xt + (before - xt) * mix).astype(BF16)
    edge_sum[...] = dot(shifted, down_ref[...])
    edges = []
    for step, mate in enumerate(mates):
        copy = pltpu.make_async_remote_copy(
            src_ref=edge_sum,
            dst_ref=edge_sums.at[step],
            send_sem=edge_send.at[step],
            recv_sem=edge_recv.at[step],
            device_id={"head": mate},
            device_id_type=MESH,
        )
        copy.start()
        edges.append(copy)

    grand = total[mine, :]
    for step, copy in enumerate(scatter):
        copy.wait_recv()
        grand = grand + shares[step]
    hidden[mine, :] = cat([jnp.tanh(grand[:, :128]), grand[:, 128:]], 1).astype(BF16)
    for step, mate in enumerate(mates):
        copy = pltpu.make_async_remote_copy(
            src_ref=hidden.at[mine],
            dst_ref=hidden.at[mine],
            send_sem=sends.at[nhead + step],
            recv_sem=recvs.at[nhead + step],
            device_id={"head": mate},
            device_id_type=MESH,
        )
        copy.start()
        spread.append(copy)
    for i in range(4, len(fetch)):
        fetch[i].wait()
    first_row = edge_sum[0:8, :]
    for step, copy in enumerate(edges):
        copy.wait_recv()
        first_row = first_row + edge_sums[step, 0:8, :]
    first_row = cat([jnp.tanh(first_row[:1, :128]), first_row[:1, 128:]], 1)
    for copy in spread:
        copy.wait_recv()
    ready[...] = jnp.where(
        iota((T, 256), 0) == 0, first_row, hidden[...].astype(F32)
    ).astype(BF16)

    eye = (row == col).astype(F32)
    first = iota((T, 128), 1) < 64
    first2 = cat([first, first], 1)
    firsts = cat([first, first], 0)
    tri2 = cat([tri, tri], 1)
    strict, upto = row > col, row >= col
    P, H = range(PAIRS), range(2 * PAIRS)

    def swap_maps(h):
        part = pl.ds(h * quarter, quarter)
        return pltpu.make_async_remote_copy(
            src_ref=mu.at[other_core, part],
            dst_ref=sib.at[part],
            send_sem=s0.at[h],
            recv_sem=r0.at[h],
            device_id=sibling,
            device_id_type=MESH,
        )

    def send_map(h, k):
        place = lax.rem(chip // 2 + quarter + mirror * k, quarter)
        to = 2 * place + h
        return to, pltpu.make_async_remote_copy(
            src_ref=chip_maps.at[h * quarter + place],
            dst_ref=maps.at[chip],
            send_sem=s1.at[h, k],
            recv_sem=r1.at[chip],
            device_id={"ctx": base + 2 * to + core},
            device_id_type=MESH,
        )

    def forward(h):
        swap_maps(h).wait_recv()
        slots = [h * quarter + i for i in range(quarter)]
        own, theirs = [mu[core, i] for i in slots], [sib[i] for i in slots]
        earlier = [jnp.where(core == 0, a, b) for a, b in zip(own, theirs)]
        later = [jnp.where(core == 0, b, a) for a, b in zip(own, theirs)]
        joined = later_all(later, earlier)
        for i, slot in enumerate(slots):
            chip_maps[slot] = joined[i]
            first_maps[slot] = earlier[i]
        for k in [2, 1, 3, 0]:
            to, copy = send_map(h, k)

            @pl.when(to != chip)
            def _():
                copy.start()

    def masked_scores(x, yh, yl):
        xh, xl = split(x)
        xr, yr = half_roll(xl), half_roll(yh)
        zero = jnp.zeros_like(xh)
        a = cat([jnp.where(first, xh, xr), jnp.where(first, xh, zero)], 1)
        b = cat([jnp.where(first, xr, xh), jnp.where(first, zero, xh)], 1)
        return [
            dot(a, cat([jnp.where(firsts, yh, yr), yl], 1), NT),
            dot(b, cat([jnp.where(firsts, yr, yh), yl], 1), NT),
        ]

    def half_of_heads(g, carry):
        def columns(ref, p):
            start = (p // 2) * (width // 2) + g * (width // 4) + (p % 2) * 128
            return ref[:, pl.ds(pl.multiple_of(start, 128), 128)]

        hid = ready[...]
        recv, keyv, valv, dirv = [[columns(a, p) for p in P] for a in (rec, key, val, unit)]
        logd = [
            -0.606531 * jax.nn.sigmoid(dot(hid[:, :128], columns(du, p)) + columns(db, p))
            for p in P
        ]
        rate = [jax.nn.sigmoid(dot(hid[:, 128:], columns(ru, p)) + columns(rb, p)) for p in P]
        cum = []
        for p in P:
            l1, l2 = split(logd[p])
            l3 = (logd[p] - l1.astype(F32) - l2.astype(F32)).astype(BF16)
            cum.append(dot(tri2, cat([l1, l2], 0)) + dot(tri, l3))
        mid = [cum[p][T // 2 - 1 : T // 2] for p in P]
        last = [cum[p][T - 1 :] for p in P]
        e_out = [jnp.exp(mid[p] - cum[p]) for p in P]
        dir_in = [dirv[p] * jnp.exp(cum[p] - logd[p] - mid[p]) for p in P]
        read_in = [recv[p].astype(F32) * jnp.exp(cum[p] - mid[p]) for p in P]
        key_out = [keyv[p].astype(F32) * e_out[p] for p in P]
        rem_out = [rate[p] * dirv[p] * e_out[p] for p in P]
        e_mid = [jnp.exp(mid[p]) for p in P]
        e_end = [jnp.exp(last[p] - mid[p]) for p in P]
        e_all = [jnp.exp(last[p]) for p in P]
        scores = []
        for p in P:
            scores += masked_scores(dir_in[p], *split(cat([key_out[p], rem_out[p]], 0)))
        a_kk = [jnp.where(strict, scores[h][:, :T], 0.0) for h in H]
        low = [jnp.where(strict, scores[h][:, T:], 0.0) for h in H]

        @pl.when(g == 1)
        def _():
            forward(0)

        inv = unit_inverse(low, row, col)
        kv = [dot(cat(split(a_kk[h]), 1), cat([valv[h // 2]] * 2, 0)) for h in H]
        right = [
            cat([dir_in[p] * e_mid[p], jnp.where(first, kv[2 * p], kv[2 * p + 1])], 1) for p in P
        ]
        sol = [mm3(inv[h], right[h // 2]) for h in H]
        low_lane = iota((64, 128), 1) < 64
        solved = [jnp.where(first2, sol[2 * p], sol[2 * p + 1]) for p in P]
        ends = [split(cat([-rem_out[p] * e_end[p], key_out[p] * e_end[p]], 0).T) for p in P]
        made = []
        for p in P:
            wh, wl = split(solved[p])
            lh, ll = ends[p]
            wide = cat([wh, cat([jnp.zeros((T, 128), BF16), valv[p]], 1)], 0)
            made.append(dot(lh, wide) + dot(ll, wide) + dot(lh[:, :T], wl))
        trans = [made[p][:, :128] + eye * e_all[p] for p in P]
        added = [made[p][:, 128:] for p in P]
        for p in P:
            slot = g * quarter + 2 * (p % 2)
            mu[p // 2, slot] = jnp.where(low_lane, trans[p][:64], half_roll(added[p][:64]))
            mu[p // 2, slot + 1] = jnp.where(low_lane, half_roll(trans[p][64:]), added[p][64:])
        swap_maps(g).start()
        for p in P:
            solved_ref[g, p] = solved[p]
            reff[g, p] = read_in[p] * e_mid[p]
            cent[g, p] = read_in[p]
            outer[g, p] = cat([key_out[p], rem_out[p]], 0)
        return carry

    lax.fori_loop(0, 2, half_of_heads, 0)

    def reads_of(i, carry):
        g, side = i // 2, lax.rem(i, 2)
        pairs = [2 * side, 2 * side + 1]
        start = side * (width // 2) + g * (width // 4)
        values = val[:, pl.ds(pl.multiple_of(start, 256), 256)]
        solved = [solved_ref[g, p] for p in pairs]
        inner = [(cent[g, p], outer[g, p]) for p in pairs]
        before = [reff[g, p] for p in pairs]
        scores = [masked_scores(x, *split(o)) for x, o in inner]
        left = [
            split(
                cat(
                    [
                        cat([jnp.where(upto, -a[:, T:], 0.0), jnp.where(upto, a[:, :T], 0.0)], 1)
                        for a in both
                    ],
                    0,
                )
            )
            for both in scores
        ]
        made = []
        for k in range(2):
            wh, wl = split(solved[k])
            zero = jnp.zeros((T, 128), BF16)
            wide = cat([wh, cat([zero, values[:, 128 * k : 128 * k + 128]], 1)], 0)
            lh, ll = left[k]
            made.append(dot(lh, wide) + dot(ll, wide) + dot(lh[:, :T], wl))
        reads = [jnp.where(first2, a[:T], a[T:]) for a in made]
        for k in range(2):
            reff[g, pairs[k]] = before[k] + reads[k][:, :128]
            base_ref[g, pairs[k]] = reads[k][:, 128:]
        return carry

    forward(1)
    lax.fori_loop(0, 4, reads_of, 0)

    maps[chip] = chip_maps[my_slot]
    for step in far:
        source = lax.rem(chip + step, chips)
        pltpu.make_async_remote_copy(
            src_ref=chip_maps.at[0],
            dst_ref=maps.at[source],
            send_sem=s1.at[0, 0],
            recv_sem=r1.at[source],
            device_id={"ctx": base + 2 * source + core},
            device_id_type=MESH,
        ).wait_recv()
    prefix = [maps[d] for d in range(chips)]
    size = 1
    while size < chips:
        lows = list(range(size, chips, 2 * size))
        joined = later_all(
            [cat(prefix[low : low + size], 0) for low in lows], [prefix[low - 1] for low in lows]
        )
        for low, group in zip(lows, joined):
            for d in range(size):
                prefix[low + d] = group[64 * d : 64 * d + 64]
        size *= 2
    row_total[...] = prefix[chips - 1]

    def send_total(r):
        return pltpu.make_async_remote_copy(
            src_ref=row_total,
            dst_ref=row_totals.at[y],
            send_sem=s2.at[r],
            recv_sem=r2.at[y],
            device_id={"ctx": r * n + me},
            device_id_type=MESH,
        )

    for r in range(1, nrow):

        @pl.when(r > y)
        def _():
            send_total(r).start()

    begin = start_ref[...]
    state = cat([begin, begin], 1)
    for r in range(nrow - 1):

        @pl.when(r < y)
        def _():
            pltpu.make_async_remote_copy(
                src_ref=row_total,
                dst_ref=row_totals.at[r],
                send_sem=s2.at[r],
                recv_sem=r2.at[r],
                device_id={"ctx": r * n + me},
                device_id_type=MESH,
            ).wait_recv()

    after_first, others_map = later_all(
        [row_totals[0], row_totals[2]], [state, row_totals[1]]
    )
    others_map = jnp.where(y == 3, others_map, row_totals[1])
    after_rows = later_of(others_map, after_first)
    state = jnp.where(y == 0, state, jnp.where(y == 1, after_first, after_rows))
    after_state = later_of(cat(prefix[: chips - 1], 0), state)
    packs = [pack_state(state)]
    packs += [pack_state(after_state[64 * d - 64 : 64 * d]) for d in range(1, chips)]
    for d in range(chips):
        states[d] = packs[d]
    third = []
    for step, other in enumerate(others):
        copy = pltpu.make_async_remote_copy(
            src_ref=states.at[other],
            dst_ref=got.at[my_slot],
            send_sem=s3.at[step],
            recv_sem=r3.at[my_slot],
            device_id={"ctx": base + 2 * other + core},
            device_id_type=MESH,
        )
        copy.start()
        third.append(copy)
    got[my_slot] = states[chip]

    def swap_states(h):
        part = pl.ds(h * quarter, quarter)
        return pltpu.make_async_remote_copy(
            src_ref=give.at[part],
            dst_ref=starts.at[core, part],
            send_sem=s4.at[h],
            recv_sem=r4.at[h],
            device_id=sibling,
            device_id_type=MESH,
        )

    def take(h):
        slots = [h * quarter + i for i in range(quarter)]
        for slot in slots:

            @pl.when(slot != my_slot)
            def _():
                pltpu.make_async_remote_copy(
                    src_ref=states.at[0],
                    dst_ref=got.at[slot],
                    send_sem=s3.at[0],
                    recv_sem=r3.at[slot],
                    device_id=sibling,
                    device_id_type=MESH,
                ).wait_recv()

        packed = [got[slot] for slot in slots]
        full = [cat([half_roll(a), a], 0) for a in packed]
        moved = later_all([first_maps[slot] for slot in slots], full)
        next_packed = [pack_state(a) for a in moved]
        for i, slot in enumerate(slots):
            give[slot] = jnp.where(core == 0, next_packed[i], packed[i])
        swap_states(h).start()
        for i, slot in enumerate(slots):
            starts[core, slot] = jnp.where(core == 0, packed[i], next_packed[i])

    lane = iota((64, 128), 1) < 64
    mean64 = (half.astype(F32) / 64).astype(BF16)
    mean2 = cat([mean64, mean64], 0)

    def finish(side, h):
        Q = range(2)
        state = []
        for q in Q:
            a, b = [starts[side, h * quarter + 2 * q + k] for k in range(2)]
            both_a = cat([a, half_roll(a)], 0)
            both_b = cat([half_roll(b), b], 0)
            state.append(
                cat([jnp.where(lane, both_a, 0.0), jnp.where(lane, 0.0, both_b)], 0)
            )
        place = [(h, 2 * side + q) for q in Q]
        read = [mm3(reff[place[q]], state[q]) + base_ref[place[q]] for q in Q]
        centered = [a - dot(cat(split(a), 1), mean2) for a in read]
        var = [dot(cat(split(a * a), 1), mean2) for a in centered]
        normed = [(a * lax.rsqrt(b + 0.00064)).astype(BF16) for a, b in zip(centered, var)]
        for q in Q:
            start = side * (width // 2) + h * (width // 4) + 128 * q
            out[:, pl.ds(pl.multiple_of(start, 128), 128)] = normed[q]

    def settle(h, carry):
        take(h)
        finish(core, h)
        swap_states(h).wait_recv()
        finish(other_core, h)
        return carry

    lax.fori_loop(0, 2, settle, 0)

    for h in range(2):
        swap_maps(h).wait_send()
        for k in range(quarter):
            to, copy = send_map(h, k)

            @pl.when(to != chip)
            def _():
                copy.wait_send()

    for r in range(1, nrow):

        @pl.when(r > y)
        def _():
            send_total(r).wait_send()

    for copy in [shift, swap_states(0), swap_states(1)] + scatter + edges + spread + third:
        copy.wait_send()


def mixed_of(x, mix, down, du, ru, db, rb, rec, key, val, start, nctx, nhead):
    T, width = x.shape
    n = start.shape[0]
    chips = n // 2
    nrow = nctx // n
    dma, vm = pltpu.SemaphoreType.DMA, pltpu.VMEM
    args = (x, mix, down, du, ru, db, rb, rec, key, val, start)
    return pl.pallas_call(
        functools.partial(mixed_kernel, nctx=nctx, nhead=nhead),
        in_specs=[pl.BlockSpec(memory_space=pl.ANY)] * len(args),
        out_specs=pl.BlockSpec(memory_space=pltpu.VMEM),
        out_shape=pltpu.VMEM((T, width), BF16),
        scratch_shapes=[vm(a.shape, a.dtype) for a in args[:-1]]
        + [vm((64, 64), F32), dma((len(args),))]
        + [
            vm((16, width), BF16),
            vm((T, 256), F32),
            vm((nhead - 1, T // nhead, 256), F32),
            vm((T, 256), BF16),
            dma((2 * nhead,)),
            dma((2 * nhead,)),
            vm((16, 256), F32),
            vm((nhead - 1, 16, 256), F32),
            vm((T, 256), BF16),
            dma((nhead - 1,)),
            dma((nhead - 1,)),
            vm((T, width), F32),
            vm((2, chips, 64, 128), F32),
            vm((2, PAIRS, T, 128), F32),
            vm((2, PAIRS, 2 * T, 128), F32),
            vm((2, PAIRS, T, 256), F32),
            vm((2, PAIRS, T, 128), F32),
            vm((2, PAIRS, T, 128), F32),
            vm((2, chips, 32, 128), F32),
            vm((chips, 64, 128), F32),
            vm((chips, 64, 128), F32),
            vm((chips, 64, 128), F32),
            vm((chips, 64, 128), F32),
            vm((64, 128), F32),
            vm((nrow, 64, 128), F32),
            vm((chips, 32, 128), F32),
            vm((chips, 32, 128), F32),
            vm((chips, 32, 128), F32),
        ]
        + [dma((2,)), dma((2,)), dma((2, chips // 2)), dma((chips,)), dma((nrow,)), dma((nrow,))]
        + [dma((chips,)), dma((chips,)), dma((2,)), dma((2,))],
        compiler_params=pltpu.CompilerParams(
            collective_id=0, has_side_effects=True, vmem_limit_bytes=40 * 1024 * 1024
        ),
    )(*[pltpu.with_memory_space_constraint(a, pltpu.HBM) for a in args])


def solution(mesh):
    nctx, nhead = mesh.shape["ctx"], mesh.shape["head"]

    def on_device(x, mix, down, du, ru, db, rb, rec, key, val, start):
        return mixed_of(
            x, mix[None], down, du, ru, db[None], rb[None], rec, key, val, start, nctx, nhead
        )

    P = jax.sharding.PartitionSpec
    both, wide = P("ctx", "head"), P("head")
    return jax.shard_map(
        on_device,
        mesh=mesh,
        in_specs=(both, wide, P("head", None), P(None, "head"), P(None, "head"), wide, wide)
        + (both,) * 3
        + (P("head", None, None),),
        out_specs=both,
        check_vma=False,
    )
```

```python
import functools
import jax
import jax.numpy as jnp
from jax import lax
from jax.experimental import pallas as pl
from jax.experimental.pallas import tpu as pltpu

F32 = jnp.float32
BF16 = jnp.bfloat16
NN = (((1,), (0,)), ((), ()))
NT = (((1,), (1,)), ((), ()))


def dot(a, b, dims=NN):
    return lax.dot_general(a, b, dims, preferred_element_type=F32)


def split(x):
    high = x.astype(BF16)
    return high, (x - high.astype(F32)).astype(BF16)


def cat(parts, axis):
    return jnp.concatenate(parts, axis=axis)


def mm3(a, b):
    ah, al = split(a)
    bh, bl = split(b)
    return dot(cat([ah, al], 1), cat([bh, bh], 0)) + dot(ah, bl)


def iota(shape, axis):
    return lax.broadcasted_iota(jnp.int32, shape, axis)


MESH = pl.DeviceIdType.MESH
PAIRS = 4


def half_roll(x):
    return pltpu.roll(x, 64, 1)


def later_all(laters, earliers):
    left = [split(a) for a in laters]
    right = [[cat([part, jnp.zeros_like(part)], 0) for part in split(b)] for b in earliers]
    main = [dot(cat([a, al], 1), cat([b, b], 0)) for (a, al), (b, _) in zip(left, right)]
    rest = [dot(a, bl) for (a, _), (_, bl) in zip(left, right)]
    lane = [iota(a.shape, 1) < 64 for a in laters]
    return [m + r + jnp.where(k, 0.0, a) for m, r, k, a in zip(main, rest, lane, laters)]


def later_of(map_later, earlier):
    return later_all([map_later], [earlier])[0]


def pack_state(full):
    lane = iota((32, 128), 1) < 64
    return jnp.where(lane, half_roll(full[:32]), full[32:])


def unit_inverse(low, row, col):
    T = low[0].shape[0]
    eye = (row == col).astype(F32)
    block = row // 8 == col // 8
    d = [jnp.where(block, a, 0.0) for a in low]
    d2 = [mm3(a, a) for a in d]
    dd = [mm3(cat([a, b], 0), b) for a, b in zip(d, d2)]
    poly = [eye - a + b - c[:T] for a, b, c in zip(d, d2, dd)]
    inv = [a + mm3(a, c[T:]) for a, c in zip(poly, dd)]
    size = 8
    while size < T:
        blocks = T // size

        def rows_of(a, odd):
            return [a[size * i : size * i + size] for i in range(odd, blocks, 2)]

        below = cat(rows_of(row, 1), 0) // size - 1 == cat(rows_of(col, 1), 0) // size
        step = [
            mm3(jnp.where(below, cat(rows_of(a, 1), 0), 0.0), b) for a, b in zip(low, inv)
        ]
        new = []
        for a, b in zip(inv, step):
            parts = [b[size * (i // 2) : size * (i // 2) + size] for i in range(blocks)]
            odd = cat(rows_of(a, 1), 0)
            odd = odd - mm3(odd, cat(parts, 0))
            merged = []
            for i, even in enumerate(rows_of(a, 0)):
                merged += [even, odd[size * i : size * i + size]]
            new.append(cat(merged, 0))
        inv = new
        size *= 2
    return inv


def mixed_kernel(
    x_h, mix_h, down_h, du_h, ru_h, db_h, rb_h, rec_h, key_h, val_h, start_h,
    out,
    x_ref, mix_ref, down_ref, du, ru, db, rb, rec, key, val, start_ref, loads,
    tail, total, shares, hidden, sends, recvs,
    edge_sum, edge_sums, ready, edge_send, edge_recv, val_high, val_low,
    unit, mu, cent, outer, solved_ref, reff, base_ref, starts,
    sib, first_maps, chip_maps, maps, row_total, row_totals, states, got, give,
    s0, r0, s1, r1, s2, r2, s3, r3, s4, r4,
    *, nctx, nhead,
):
    ctx, head = lax.axis_index("ctx"), lax.axis_index("head")
    T, width = x_ref.shape
    n = mu.shape[0] * mu.shape[1]
    chips = n // 2
    quarter = chips // 2
    nrow = nctx // n
    y, me = ctx // n, lax.rem(ctx, n)
    chip, core = me // 2, lax.rem(me, 2)
    other_core = 1 - core
    base = y * n
    my_slot = chip // 2 + quarter * lax.rem(chip, 2)
    my_head = core * chips + my_slot
    sibling = {"ctx": base + chip * 2 + other_core}

    fetch = []
    for i, (src, dst) in enumerate(
        [(x_h, x_ref), (mix_h, mix_ref), (down_h, down_ref), (key_h, key), (du_h, du), (ru_h, ru)]
        + [(db_h, db), (rb_h, rb), (rec_h, rec), (val_h, val), (start_h.at[my_head], start_ref)]
    ):
        fetch.append(pltpu.make_async_copy(src, dst, loads.at[i]))

    row_totals[...] = jnp.zeros_like(row_totals)
    after, behind = lax.rem(ctx + 1, nctx), lax.rem(ctx + nctx - 1, nctx)
    mirror = 1 - 2 * core
    mates = [lax.rem(head + nhead + mirror * step, nhead) for step in (2, 1, 3)]
    far = sorted(range(1, chips), key=lambda d: -min(d, chips - d))
    others = [lax.rem(chip + chips + mirror * step, chips) for step in far]
    rows = [lax.rem(y + step, nrow) for step in range(1, nrow)]
    barrier = pltpu.get_barrier_semaphore()
    for other in [base + 2 * o + core for o in others] + [r * n + me for r in rows]:
        pl.semaphore_signal(barrier, inc=1, device_id={"ctx": other}, device_id_type=MESH)
    for mate in mates:
        pl.semaphore_signal(barrier, inc=1, device_id={"head": mate}, device_id_type=MESH)
    for other in [after, behind]:
        pl.semaphore_signal(barrier, inc=1, device_id={"ctx": other}, device_id_type=MESH)
    pl.semaphore_signal(barrier, inc=1, device_id=sibling, device_id_type=MESH)
    for copy in fetch[:4]:
        copy.start()

    for i in range(3):
        fetch[i].wait()
    for copy in fetch[4:]:
        copy.start()
    mix = mix_ref[...]
    xf = x_ref[...].astype(F32)
    before = pltpu.roll(xf, 1, 0)
    shifted = (xf + (before - xf) * mix).astype(BF16)
    total[...] = dot(shifted, down_ref[...])

    row, col = iota((T, T), 0), iota((T, T), 1)
    tri = (row >= col).astype(BF16)
    half = (row // 64 == col // 64).astype(BF16)
    half2 = cat([half, half], 0)
    fetch[3].wait()
    for p in range(width // 128):
        kf = key[:, 128 * p : 128 * p + 128].astype(F32)
        square = dot(cat(split(kf * kf), 1), half2)
        unit[:, 128 * p : 128 * p + 128] = kf * lax.rsqrt(square + 1e-06)
    pl.semaphore_wait(barrier, 2 + nhead - 1 + 1 + chips - 1 + nrow - 1)

    shift = pltpu.make_async_remote_copy(
        src_ref=x_h.at[pl.ds(T - 16, 16)],
        dst_ref=tail,
        send_sem=sends.at[0],
        recv_sem=recvs.at[0],
        device_id={"ctx": after},
        device_id_type=MESH,
    )
    shift.start()

    share = T // nhead
    mine = pl.ds(pl.multiple_of(head * share, share), share)
    scatter, spread = [], []
    for step, mate in enumerate(mates):
        copy = pltpu.make_async_remote_copy(
            src_ref=total.at[pl.ds(pl.multiple_of(mate * share, share), share)],
            dst_ref=shares.at[step],
            send_sem=sends.at[1 + step],
            recv_sem=recvs.at[1 + step],
            device_id={"head": mate},
            device_id_type=MESH,
        )
        copy.start()
        scatter.append(copy)

    shift.wait_recv()
    xt = x_ref[0:16, :].astype(F32)
    edge = jnp.where(ctx > 0, tail[...].astype(F32)[15:16], 0.0)
    before = jnp.where(iota((16, width), 0) == 0, edge, pltpu.roll(xt, 1, 0))
    shifted = (xt + (before - xt) * mix).astype(BF16)
    edge_sum[...] = dot(shifted, down_ref[...])
    edges = []
    for step, mate in enumerate(mates):
        copy = pltpu.make_async_remote_copy(
            src_ref=edge_sum.at[pl.ds(0, 8)],
            dst_ref=edge_sums.at[step],
            send_sem=edge_send.at[step],
            recv_sem=edge_recv.at[step],
            device_id={"head": mate},
            device_id_type=MESH,
        )
        copy.start()
        edges.append(copy)

    grand = total[mine, :]
    for step, copy in enumerate(scatter):
        copy.wait_recv()
        grand = grand + shares[step]
    hidden[mine, :] = cat([jnp.tanh(grand[:, :128]), grand[:, 128:]], 1).astype(BF16)
    for step, mate in enumerate(mates):
        copy = pltpu.make_async_remote_copy(
            src_ref=hidden.at[mine],
            dst_ref=hidden.at[mine],
            send_sem=sends.at[nhead + step],
            recv_sem=recvs.at[nhead + step],
            device_id={"head": mate},
            device_id_type=MESH,
        )
        copy.start()
        spread.append(copy)
    for i in range(4, len(fetch)):
        fetch[i].wait()
    mean64 = (half.astype(F32) / 64).astype(BF16)
    for p in range(width // 128):
        cols = slice(128 * p, 128 * p + 128)
        values = val[:, cols]
        vh, vl = split(values.astype(F32) - dot(values, mean64))
        val_high[:, cols] = vh
        val_low[:, cols] = vl
    first_row = edge_sum[0:8, :]
    for step, copy in enumerate(edges):
        copy.wait_recv()
        first_row = first_row + edge_sums[step]
    first_row = cat([jnp.tanh(first_row[:1, :128]), first_row[:1, 128:]], 1)
    for copy in spread:
        copy.wait_recv()
    ready[...] = jnp.where(
        iota((T, 256), 0) == 0, first_row, hidden[...].astype(F32)
    ).astype(BF16)

    eye = (row == col).astype(F32)
    first = iota((T, 128), 1) < 64
    first2 = cat([first, first], 1)
    firsts = cat([first, first], 0)
    tri2 = cat([tri, tri], 1)
    strict, upto = row > col, row >= col
    P, H = range(PAIRS), range(2 * PAIRS)

    def swap_maps(h):
        part = pl.ds(h * quarter, quarter)
        return pltpu.make_async_remote_copy(
            src_ref=mu.at[other_core, part],
            dst_ref=sib.at[part],
            send_sem=s0.at[h],
            recv_sem=r0.at[h],
            device_id=sibling,
            device_id_type=MESH,
        )

    def send_map(h, k):
        place = lax.rem(chip // 2 + quarter + mirror * k, quarter)
        to = 2 * place + h
        return to, pltpu.make_async_remote_copy(
            src_ref=chip_maps.at[h * quarter + place],
            dst_ref=maps.at[chip],
            send_sem=s1.at[h, k],
            recv_sem=r1.at[chip],
            device_id={"ctx": base + 2 * to + core},
            device_id_type=MESH,
        )

    def forward(h):
        swap_maps(h).wait_recv()
        slots = [h * quarter + i for i in range(quarter)]
        own, theirs = [mu[core, i] for i in slots], [sib[i] for i in slots]
        earlier = [jnp.where(core == 0, a, b) for a, b in zip(own, theirs)]
        later = [jnp.where(core == 0, b, a) for a, b in zip(own, theirs)]
        joined = later_all(later, earlier)
        for i, slot in enumerate(slots):
            chip_maps[slot] = joined[i]
            first_maps[slot] = earlier[i]
        for k in [2, 1, 3, 0]:
            to, copy = send_map(h, k)

            @pl.when(to != chip)
            def _():
                copy.start()

    def masked_scores(x, yh, yl):
        xh, xl = split(x)
        xr, yr = half_roll(xl), half_roll(yh)
        zero = jnp.zeros_like(xh)
        a = cat([jnp.where(first, xh, xr), jnp.where(first, xh, zero)], 1)
        b = cat([jnp.where(first, xr, xh), jnp.where(first, zero, xh)], 1)
        return [
            dot(a, cat([jnp.where(firsts, yh, yr), yl], 1), NT),
            dot(b, cat([jnp.where(firsts, yr, yh), yl], 1), NT),
        ]

    def half_of_heads(g, carry):
        def columns(ref, p):
            start = (p // 2) * (width // 2) + g * (width // 4) + (p % 2) * 128
            return ref[:, pl.ds(pl.multiple_of(start, 128), 128)]

        hid = ready[...]
        recv, keyv, dirv = [[columns(a, p) for p in P] for a in (rec, key, unit)]
        val_h, val_l = [[columns(a, p) for p in P] for a in (val_high, val_low)]
        logd = [
            -0.606531 * jax.nn.sigmoid(dot(hid[:, :128], columns(du, p)) + columns(db, p))
            for p in P
        ]
        rate = [jax.nn.sigmoid(dot(hid[:, 128:], columns(ru, p)) + columns(rb, p)) for p in P]
        cum = []
        for p in P:
            l1, l2 = split(logd[p])
            l3 = (logd[p] - l1.astype(F32) - l2.astype(F32)).astype(BF16)
            cum.append(dot(tri2, cat([l1, l2], 0)) + dot(tri, l3))
        mid = [cum[p][T // 2 - 1 : T // 2] for p in P]
        last = [cum[p][T - 1 :] for p in P]
        e_out = [jnp.exp(mid[p] - cum[p]) for p in P]
        dir_in = [dirv[p] * jnp.exp(cum[p] - logd[p] - mid[p]) for p in P]
        read_in = [recv[p].astype(F32) * jnp.exp(cum[p] - mid[p]) for p in P]
        key_out = [keyv[p].astype(F32) * e_out[p] for p in P]
        rem_out = [rate[p] * dirv[p] * e_out[p] for p in P]
        e_mid = [jnp.exp(mid[p]) for p in P]
        e_end = [jnp.exp(last[p] - mid[p]) for p in P]
        e_all = [jnp.exp(last[p]) for p in P]
        scores = []
        for p in P:
            scores += masked_scores(dir_in[p], *split(cat([key_out[p], rem_out[p]], 0)))
        a_kk = [jnp.where(strict, scores[h][:, :T], 0.0) for h in H]
        low = [jnp.where(strict, scores[h][:, T:], 0.0) for h in H]

        @pl.when(g == 1)
        def _():
            forward(0)

        inv = unit_inverse(low, row, col)
        kk = [split(a) for a in a_kk]
        kv = [
            dot(cat(kk[h], 1), cat([val_h[h // 2]] * 2, 0)) + dot(kk[h][0], val_l[h // 2])
            for h in H
        ]
        right = [
            cat([dir_in[p] * e_mid[p], jnp.where(first, kv[2 * p], kv[2 * p + 1])], 1) for p in P
        ]
        sol = [mm3(inv[h], right[h // 2]) for h in H]
        low_lane = iota((64, 128), 1) < 64
        solved = [jnp.where(first2, sol[2 * p], sol[2 * p + 1]) for p in P]
        ends = [split(cat([-rem_out[p] * e_end[p], key_out[p] * e_end[p]], 0).T) for p in P]
        made = []
        for p in P:
            wh, wl = split(solved[p])
            lh, ll = ends[p]
            zero = jnp.zeros((T, 128), BF16)
            wide = cat([wh, cat([zero, val_h[p]], 1)], 0)
            rest = cat([wl, cat([zero, val_l[p]], 1)], 0)
            made.append(dot(lh, wide) + dot(ll, wide) + dot(lh, rest))
        trans = [made[p][:, :128] + eye * e_all[p] for p in P]
        added = [made[p][:, 128:] for p in P]
        for p in P:
            slot = g * quarter + 2 * (p % 2)
            mu[p // 2, slot] = jnp.where(low_lane, trans[p][:64], half_roll(added[p][:64]))
            mu[p // 2, slot + 1] = jnp.where(low_lane, half_roll(trans[p][64:]), added[p][64:])
        swap_maps(g).start()
        for p in P:
            solved_ref[g, p] = solved[p]
            reff[g, p] = read_in[p] * e_mid[p]
            cent[g, p] = read_in[p]
            outer[g, p] = cat([key_out[p], rem_out[p]], 0)
        return carry

    lax.fori_loop(0, 2, half_of_heads, 0)

    def reads_of(i, carry):
        g, side = i // 2, lax.rem(i, 2)
        pairs = [2 * side, 2 * side + 1]
        start = side * (width // 2) + g * (width // 4)
        cols = pl.ds(pl.multiple_of(start, 256), 256)
        high, low_part = val_high[:, cols], val_low[:, cols]
        solved = [solved_ref[g, p] for p in pairs]
        inner = [(cent[g, p], outer[g, p]) for p in pairs]
        before = [reff[g, p] for p in pairs]
        scores = [masked_scores(x, *split(o)) for x, o in inner]
        left = [
            split(
                cat(
                    [
                        cat([jnp.where(upto, -a[:, T:], 0.0), jnp.where(upto, a[:, :T], 0.0)], 1)
                        for a in both
                    ],
                    0,
                )
            )
            for both in scores
        ]
        made = []
        for k in range(2):
            wh, wl = split(solved[k])
            zero = jnp.zeros((T, 128), BF16)
            side_cols = slice(128 * k, 128 * k + 128)
            wide = cat([wh, cat([zero, high[:, side_cols]], 1)], 0)
            rest = cat([wl, cat([zero, low_part[:, side_cols]], 1)], 0)
            lh, ll = left[k]
            made.append(dot(lh, wide) + dot(ll, wide) + dot(lh, rest))
        reads = [jnp.where(first2, a[:T], a[T:]) for a in made]
        for k in range(2):
            reff[g, pairs[k]] = before[k] + reads[k][:, :128]
            base_ref[g, pairs[k]] = reads[k][:, 128:]
        return carry

    forward(1)
    lax.fori_loop(0, 4, reads_of, 0)

    maps[chip] = chip_maps[my_slot]
    for step in far:
        source = lax.rem(chip + step, chips)
        pltpu.make_async_remote_copy(
            src_ref=chip_maps.at[0],
            dst_ref=maps.at[source],
            send_sem=s1.at[0, 0],
            recv_sem=r1.at[source],
            device_id={"ctx": base + 2 * source + core},
            device_id_type=MESH,
        ).wait_recv()
    prefix = [maps[d] for d in range(chips)]
    size = 1
    while size < chips:
        lows = list(range(size, chips, 2 * size))
        joined = later_all(
            [cat(prefix[low : low + size], 0) for low in lows], [prefix[low - 1] for low in lows]
        )
        for low, group in zip(lows, joined):
            for d in range(size):
                prefix[low + d] = group[64 * d : 64 * d + 64]
        size *= 2
    row_total[...] = prefix[chips - 1]

    def send_total(r):
        return pltpu.make_async_remote_copy(
            src_ref=row_total,
            dst_ref=row_totals.at[y],
            send_sem=s2.at[r],
            recv_sem=r2.at[y],
            device_id={"ctx": r * n + me},
            device_id_type=MESH,
        )

    for r in range(1, nrow):

        @pl.when(r > y)
        def _():
            send_total(r).start()

    begin = start_ref[...]
    begin = begin - jnp.mean(begin, axis=1, keepdims=True)
    state = cat([begin, begin], 1)
    for r in range(nrow - 1):

        @pl.when(r < y)
        def _():
            pltpu.make_async_remote_copy(
                src_ref=row_total,
                dst_ref=row_totals.at[r],
                send_sem=s2.at[r],
                recv_sem=r2.at[r],
                device_id={"ctx": r * n + me},
                device_id_type=MESH,
            ).wait_recv()

    after_first, others_map = later_all(
        [row_totals[0], row_totals[2]], [state, row_totals[1]]
    )
    others_map = jnp.where(y == 3, others_map, row_totals[1])
    after_rows = later_of(others_map, after_first)
    state = jnp.where(y == 0, state, jnp.where(y == 1, after_first, after_rows))
    after_state = later_of(cat(prefix[: chips - 1], 0), state)
    packs = [pack_state(state)]
    packs += [pack_state(after_state[64 * d - 64 : 64 * d]) for d in range(1, chips)]
    for d in range(chips):
        states[d] = packs[d]
    third = []
    for step, other in enumerate(others):
        copy = pltpu.make_async_remote_copy(
            src_ref=states.at[other],
            dst_ref=got.at[my_slot],
            send_sem=s3.at[step],
            recv_sem=r3.at[my_slot],
            device_id={"ctx": base + 2 * other + core},
            device_id_type=MESH,
        )
        copy.start()
        third.append(copy)
    got[my_slot] = states[chip]

    def swap_states(h):
        part = pl.ds(h * quarter, quarter)
        return pltpu.make_async_remote_copy(
            src_ref=give.at[part],
            dst_ref=starts.at[core, part],
            send_sem=s4.at[h],
            recv_sem=r4.at[h],
            device_id=sibling,
            device_id_type=MESH,
        )

    def take(h):
        slots = [h * quarter + i for i in range(quarter)]
        for slot in slots:

            @pl.when(slot != my_slot)
            def _():
                pltpu.make_async_remote_copy(
                    src_ref=states.at[0],
                    dst_ref=got.at[slot],
                    send_sem=s3.at[0],
                    recv_sem=r3.at[slot],
                    device_id=sibling,
                    device_id_type=MESH,
                ).wait_recv()

        packed = [got[slot] for slot in slots]
        full = [cat([half_roll(a), a], 0) for a in packed]
        moved = later_all([first_maps[slot] for slot in slots], full)
        next_packed = [pack_state(a) for a in moved]
        for i, slot in enumerate(slots):
            give[slot] = jnp.where(core == 0, next_packed[i], packed[i])
        swap_states(h).start()
        for i, slot in enumerate(slots):
            starts[core, slot] = jnp.where(core == 0, packed[i], next_packed[i])

    lane = iota((64, 128), 1) < 64
    mean2 = cat([mean64, mean64], 0)

    def finish(side, h):
        Q = range(2)
        state = []
        for q in Q:
            a, b = [starts[side, h * quarter + 2 * q + k] for k in range(2)]
            both_a = cat([a, half_roll(a)], 0)
            both_b = cat([half_roll(b), b], 0)
            state.append(
                cat([jnp.where(lane, both_a, 0.0), jnp.where(lane, 0.0, both_b)], 0)
            )
        place = [(h, 2 * side + q) for q in Q]
        centered = [mm3(reff[place[q]], state[q]) + base_ref[place[q]] for q in Q]
        var = [dot(cat(split(a * a), 1), mean2) for a in centered]
        normed = [(a * lax.rsqrt(b + 0.00064)).astype(BF16) for a, b in zip(centered, var)]
        for q in Q:
            start = side * (width // 2) + h * (width // 4) + 128 * q
            out[:, pl.ds(pl.multiple_of(start, 128), 128)] = normed[q]

    def settle(h, carry):
        take(h)
        finish(core, h)
        swap_states(h).wait_recv()
        finish(other_core, h)
        return carry

    lax.fori_loop(0, 2, settle, 0)

    for h in range(2):
        swap_maps(h).wait_send()
        for k in range(quarter):
            to, copy = send_map(h, k)

            @pl.when(to != chip)
            def _():
                copy.wait_send()

    for r in range(1, nrow):

        @pl.when(r > y)
        def _():
            send_total(r).wait_send()

    for copy in [shift, swap_states(0), swap_states(1)] + scatter + edges + spread + third:
        copy.wait_send()


def mixed_of(x, mix, down, du, ru, db, rb, rec, key, val, start, nctx, nhead):
    T, width = x.shape
    n = start.shape[0]
    chips = n // 2
    nrow = nctx // n
    dma, vm = pltpu.SemaphoreType.DMA, pltpu.VMEM
    args = (x, mix, down, du, ru, db, rb, rec, key, val, start)
    return pl.pallas_call(
        functools.partial(mixed_kernel, nctx=nctx, nhead=nhead),
        in_specs=[pl.BlockSpec(memory_space=pl.ANY)] * len(args),
        out_specs=pl.BlockSpec(memory_space=pltpu.VMEM),
        out_shape=pltpu.VMEM((T, width), BF16),
        scratch_shapes=[vm(a.shape, a.dtype) for a in args[:-1]]
        + [vm((64, 64), F32), dma((len(args),))]
        + [
            vm((16, width), BF16),
            vm((T, 256), F32),
            vm((nhead - 1, T // nhead, 256), F32),
            vm((T, 256), BF16),
            dma((2 * nhead,)),
            dma((2 * nhead,)),
            vm((16, 256), F32),
            vm((nhead - 1, 8, 256), F32),
            vm((T, 256), BF16),
            dma((nhead - 1,)),
            dma((nhead - 1,)),
            vm((T, width), BF16),
            vm((T, width), BF16),
            vm((T, width), F32),
            vm((2, chips, 64, 128), F32),
            vm((2, PAIRS, T, 128), F32),
            vm((2, PAIRS, 2 * T, 128), F32),
            vm((2, PAIRS, T, 256), F32),
            vm((2, PAIRS, T, 128), F32),
            vm((2, PAIRS, T, 128), F32),
            vm((2, chips, 32, 128), F32),
            vm((chips, 64, 128), F32),
            vm((chips, 64, 128), F32),
            vm((chips, 64, 128), F32),
            vm((chips, 64, 128), F32),
            vm((64, 128), F32),
            vm((nrow, 64, 128), F32),
            vm((chips, 32, 128), F32),
            vm((chips, 32, 128), F32),
            vm((chips, 32, 128), F32),
        ]
        + [dma((2,)), dma((2,)), dma((2, chips // 2)), dma((chips,)), dma((nrow,)), dma((nrow,))]
        + [dma((chips,)), dma((chips,)), dma((2,)), dma((2,))],
        compiler_params=pltpu.CompilerParams(
            collective_id=0, has_side_effects=True, vmem_limit_bytes=40 * 1024 * 1024
        ),
    )(*[pltpu.with_memory_space_constraint(a, pltpu.HBM) for a in args])


def solution(mesh):
    nctx, nhead = mesh.shape["ctx"], mesh.shape["head"]

    def on_device(x, mix, down, du, ru, db, rb, rec, key, val, start):
        return mixed_of(
            x, mix[None], down, du, ru, db[None], rb[None], rec, key, val, start, nctx, nhead
        )

    P = jax.sharding.PartitionSpec
    both, wide = P("ctx", "head"), P("head")
    return jax.shard_map(
        on_device,
        mesh=mesh,
        in_specs=(both, wide, P("head", None), P(None, "head"), P(None, "head"), wide, wide)
        + (both,) * 3
        + (P("head", None, None),),
        out_specs=both,
        check_vma=False,
    )
```

```python
import functools
import jax
import jax.numpy as jnp
from jax import lax
from jax.experimental import pallas as pl
from jax.experimental.pallas import tpu as pltpu

F32 = jnp.float32
BF16 = jnp.bfloat16
NN = (((1,), (0,)), ((), ()))
NT = (((1,), (1,)), ((), ()))


def dot(a, b, dims=NN):
    return lax.dot_general(a, b, dims, preferred_element_type=F32)


def split(x):
    high = x.astype(BF16)
    return high, (x - high.astype(F32)).astype(BF16)


def cat(parts, axis):
    return jnp.concatenate(parts, axis=axis)


def mm3(a, b):
    ah, al = split(a)
    bh, bl = split(b)
    return dot(cat([ah, al], 1), cat([bh, bh], 0)) + dot(ah, bl)


def iota(shape, axis):
    return lax.broadcasted_iota(jnp.int32, shape, axis)


MESH = pl.DeviceIdType.MESH
PAIRS = 4


def half_roll(x):
    return pltpu.roll(x, 64, 1)


def later_all(laters, earliers):
    left = [split(a) for a in laters]
    right = [[cat([part, jnp.zeros_like(part)], 0) for part in split(b)] for b in earliers]
    main = [dot(cat([a, al], 1), cat([b, b], 0)) for (a, al), (b, _) in zip(left, right)]
    rest = [dot(a, bl) for (a, _), (_, bl) in zip(left, right)]
    lane = [iota(a.shape, 1) < 64 for a in laters]
    return [m + r + jnp.where(k, 0.0, a) for m, r, k, a in zip(main, rest, lane, laters)]


def later_of(map_later, earlier):
    return later_all([map_later], [earlier])[0]


def pack_state(full):
    lane = iota((32, 128), 1) < 64
    return jnp.where(lane, half_roll(full[:32]), full[32:])


def unit_inverse(low, row, col):
    T = low[0].shape[0]
    eye = (row == col).astype(F32)
    block = row // 8 == col // 8
    d = [jnp.where(block, a, 0.0) for a in low]
    d2 = [mm3(a, a) for a in d]
    dd = [mm3(cat([a, b], 0), b) for a, b in zip(d, d2)]
    poly = [eye - a + b - c[:T] for a, b, c in zip(d, d2, dd)]
    inv = [a + mm3(a, c[T:]) for a, c in zip(poly, dd)]
    size = 8
    while size < T:
        blocks = T // size

        def rows_of(a, odd):
            return [a[size * i : size * i + size] for i in range(odd, blocks, 2)]

        below = cat(rows_of(row, 1), 0) // size - 1 == cat(rows_of(col, 1), 0) // size
        step = [
            mm3(jnp.where(below, cat(rows_of(a, 1), 0), 0.0), b) for a, b in zip(low, inv)
        ]
        new = []
        for a, b in zip(inv, step):
            parts = [b[size * (i // 2) : size * (i // 2) + size] for i in range(blocks)]
            odd = cat(rows_of(a, 1), 0)
            odd = odd - mm3(odd, cat(parts, 0))
            merged = []
            for i, even in enumerate(rows_of(a, 0)):
                merged += [even, odd[size * i : size * i + size]]
            new.append(cat(merged, 0))
        inv = new
        size *= 2
    return inv


def mixed_kernel(
    x_h, mix_h, down_h, du_h, ru_h, db_h, rb_h, rec_h, key_h, val_h, start_h,
    out,
    x_ref, mix_ref, down_ref, du, ru, db, rb, rec, key, val, start_ref, loads,
    tail, total, shares, hidden, sends, recvs,
    edge_sum, edge_sums, ready, edge_send, edge_recv,
    unit, mu, cent, outer, solved_ref, reff, base_ref, starts,
    sib, first_maps, chip_maps, maps, row_total, row_totals, states, got, give,
    s0, r0, s1, r1, s2, r2, s3, r3, s4, r4,
    *, nctx, nhead,
):
    ctx, head = lax.axis_index("ctx"), lax.axis_index("head")
    T, width = x_ref.shape
    n = mu.shape[0] * mu.shape[1]
    chips = n // 2
    quarter = chips // 2
    nrow = nctx // n
    y, me = ctx // n, lax.rem(ctx, n)
    chip, core = me // 2, lax.rem(me, 2)
    other_core = 1 - core
    base = y * n
    my_slot = chip // 2 + quarter * lax.rem(chip, 2)
    my_head = core * chips + my_slot
    sibling = {"ctx": base + chip * 2 + other_core}

    fetch = []
    for i, (src, dst) in enumerate(
        [(x_h, x_ref), (mix_h, mix_ref), (down_h, down_ref), (key_h, key), (du_h, du), (ru_h, ru)]
        + [(db_h, db), (rb_h, rb), (rec_h, rec), (val_h, val), (start_h.at[my_head], start_ref)]
    ):
        fetch.append(pltpu.make_async_copy(src, dst, loads.at[i]))

    row_totals[...] = jnp.zeros_like(row_totals)
    after, behind = lax.rem(ctx + 1, nctx), lax.rem(ctx + nctx - 1, nctx)
    mirror = 1 - 2 * core
    mates = [lax.rem(head + nhead + mirror * step, nhead) for step in (2, 1, 3)]
    far = sorted(range(1, chips), key=lambda d: -min(d, chips - d))
    others = [lax.rem(chip + chips + mirror * step, chips) for step in far]
    rows = [lax.rem(y + step, nrow) for step in range(1, nrow)]
    barrier = pltpu.get_barrier_semaphore()
    for other in [base + 2 * o + core for o in others] + [r * n + me for r in rows]:
        pl.semaphore_signal(barrier, inc=1, device_id={"ctx": other}, device_id_type=MESH)
    for mate in mates:
        pl.semaphore_signal(barrier, inc=1, device_id={"head": mate}, device_id_type=MESH)
    for other in [after, behind]:
        pl.semaphore_signal(barrier, inc=1, device_id={"ctx": other}, device_id_type=MESH)
    pl.semaphore_signal(barrier, inc=1, device_id=sibling, device_id_type=MESH)
    for copy in fetch[:4]:
        copy.start()

    for i in range(3):
        fetch[i].wait()
    for copy in fetch[4:]:
        copy.start()
    mix = mix_ref[...]
    xf = x_ref[...].astype(F32)
    before = pltpu.roll(xf, 1, 0)
    shifted = (xf + (before - xf) * mix).astype(BF16)
    total[...] = dot(shifted, down_ref[...])

    row, col = iota((T, T), 0), iota((T, T), 1)
    tri = (row >= col).astype(BF16)
    half = (row // 64 == col // 64).astype(BF16)
    half2 = cat([half, half], 0)
    fetch[3].wait()
    for p in range(width // 128):
        kf = key[:, 128 * p : 128 * p + 128].astype(F32)
        square = dot(cat(split(kf * kf), 1), half2)
        unit[:, 128 * p : 128 * p + 128] = kf * lax.rsqrt(square + 1e-06)
    pl.semaphore_wait(barrier, 2 + nhead - 1 + 1 + chips - 1 + nrow - 1)

    shift = pltpu.make_async_remote_copy(
        src_ref=x_h.at[pl.ds(T - 16, 16)],
        dst_ref=tail,
        send_sem=sends.at[0],
        recv_sem=recvs.at[0],
        device_id={"ctx": after},
        device_id_type=MESH,
    )
    shift.start()

    share = T // nhead
    mine = pl.ds(pl.multiple_of(head * share, share), share)
    scatter, spread = [], []
    for step, mate in enumerate(mates):
        copy = pltpu.make_async_remote_copy(
            src_ref=total.at[pl.ds(pl.multiple_of(mate * share, share), share)],
            dst_ref=shares.at[step],
            send_sem=sends.at[1 + step],
            recv_sem=recvs.at[1 + step],
            device_id={"head": mate},
            device_id_type=MESH,
        )
        copy.start()
        scatter.append(copy)

    shift.wait_recv()
    xt = x_ref[0:16, :].astype(F32)
    edge = jnp.where(ctx > 0, tail[...].astype(F32)[15:16], 0.0)
    before = jnp.where(iota((16, width), 0) == 0, edge, pltpu.roll(xt, 1, 0))
    shifted = (xt + (before - xt) * mix).astype(BF16)
    edge_sum[...] = dot(shifted, down_ref[...])
    edges = []
    for step, mate in enumerate(mates):
        copy = pltpu.make_async_remote_copy(
            src_ref=edge_sum.at[pl.ds(0, 8)],
            dst_ref=edge_sums.at[step],
            send_sem=edge_send.at[step],
            recv_sem=edge_recv.at[step],
            device_id={"head": mate},
            device_id_type=MESH,
        )
        copy.start()
        edges.append(copy)

    grand = total[mine, :]
    for step, copy in enumerate(scatter):
        copy.wait_recv()
        grand = grand + shares[step]
    hidden[mine, :] = cat([jnp.tanh(grand[:, :128]), grand[:, 128:]], 1).astype(BF16)
    for step, mate in enumerate(mates):
        copy = pltpu.make_async_remote_copy(
            src_ref=hidden.at[mine],
            dst_ref=hidden.at[mine],
            send_sem=sends.at[nhead + step],
            recv_sem=recvs.at[nhead + step],
            device_id={"head": mate},
            device_id_type=MESH,
        )
        copy.start()
        spread.append(copy)
    for i in range(4, len(fetch)):
        fetch[i].wait()
    first_row = edge_sum[0:8, :]
    for step, copy in enumerate(edges):
        copy.wait_recv()
        first_row = first_row + edge_sums[step]
    first_row = cat([jnp.tanh(first_row[:1, :128]), first_row[:1, 128:]], 1)
    for copy in spread:
        copy.wait_recv()
    ready[...] = jnp.where(
        iota((T, 256), 0) == 0, first_row, hidden[...].astype(F32)
    ).astype(BF16)

    eye = (row == col).astype(F32)
    first = iota((T, 128), 1) < 64
    first2 = cat([first, first], 1)
    firsts = cat([first, first], 0)
    tri2 = cat([tri, tri], 1)
    strict, upto = row > col, row >= col
    P, H = range(PAIRS), range(2 * PAIRS)

    def swap_maps(h):
        part = pl.ds(h * quarter, quarter)
        return pltpu.make_async_remote_copy(
            src_ref=mu.at[other_core, part],
            dst_ref=sib.at[part],
            send_sem=s0.at[h],
            recv_sem=r0.at[h],
            device_id=sibling,
            device_id_type=MESH,
        )

    def send_map(h, k):
        place = lax.rem(chip // 2 + quarter + mirror * k, quarter)
        to = 2 * place + h
        return to, pltpu.make_async_remote_copy(
            src_ref=chip_maps.at[h * quarter + place],
            dst_ref=maps.at[chip],
            send_sem=s1.at[h, k],
            recv_sem=r1.at[chip],
            device_id={"ctx": base + 2 * to + core},
            device_id_type=MESH,
        )

    def forward(h):
        swap_maps(h).wait_recv()
        slots = [h * quarter + i for i in range(quarter)]
        own, theirs = [mu[core, i] for i in slots], [sib[i] for i in slots]
        earlier = [jnp.where(core == 0, a, b) for a, b in zip(own, theirs)]
        later = [jnp.where(core == 0, b, a) for a, b in zip(own, theirs)]
        joined = later_all(later, earlier)
        for i, slot in enumerate(slots):
            chip_maps[slot] = joined[i]
            first_maps[slot] = earlier[i]
        for k in [2, 1, 3, 0]:
            to, copy = send_map(h, k)

            @pl.when(to != chip)
            def _():
                copy.start()

    def masked_scores(x, yh, yl):
        xh, xl = split(x)
        xr, yr = half_roll(xl), half_roll(yh)
        zero = jnp.zeros_like(xh)
        a = cat([jnp.where(first, xh, xr), jnp.where(first, xh, zero)], 1)
        b = cat([jnp.where(first, xr, xh), jnp.where(first, zero, xh)], 1)
        return [
            dot(a, cat([jnp.where(firsts, yh, yr), yl], 1), NT),
            dot(b, cat([jnp.where(firsts, yr, yh), yl], 1), NT),
        ]

    def half_of_heads(g, carry):
        def columns(ref, p):
            start = (p // 2) * (width // 2) + g * (width // 4) + (p % 2) * 128
            return ref[:, pl.ds(pl.multiple_of(start, 128), 128)]

        hid = ready[...]
        recv, keyv, valv, dirv = [[columns(a, p) for p in P] for a in (rec, key, val, unit)]
        logd = [
            -0.606531 * jax.nn.sigmoid(dot(hid[:, :128], columns(du, p)) + columns(db, p))
            for p in P
        ]
        rate = [jax.nn.sigmoid(dot(hid[:, 128:], columns(ru, p)) + columns(rb, p)) for p in P]
        cum = []
        for p in P:
            l1, l2 = split(logd[p])
            l3 = (logd[p] - l1.astype(F32) - l2.astype(F32)).astype(BF16)
            cum.append(dot(tri2, cat([l1, l2], 0)) + dot(tri, l3))
        mid = [cum[p][T // 2 - 1 : T // 2] for p in P]
        last = [cum[p][T - 1 :] for p in P]
        e_out = [jnp.exp(mid[p] - cum[p]) for p in P]
        dir_in = [dirv[p] * jnp.exp(cum[p] - logd[p] - mid[p]) for p in P]
        read_in = [recv[p].astype(F32) * jnp.exp(cum[p] - mid[p]) for p in P]
        key_out = [keyv[p].astype(F32) * e_out[p] for p in P]
        rem_out = [rate[p] * dirv[p] * e_out[p] for p in P]
        e_mid = [jnp.exp(mid[p]) for p in P]
        e_end = [jnp.exp(last[p] - mid[p]) for p in P]
        e_all = [jnp.exp(last[p]) for p in P]
        scores = []
        for p in P:
            scores += masked_scores(dir_in[p], *split(cat([key_out[p], rem_out[p]], 0)))
        a_kk = [jnp.where(strict, scores[h][:, :T], 0.0) for h in H]
        low = [jnp.where(strict, scores[h][:, T:], 0.0) for h in H]

        inv = unit_inverse(low, row, col)
        kv = [dot(cat(split(a_kk[h]), 1), cat([valv[h // 2]] * 2, 0)) for h in H]
        right = [
            cat([dir_in[p] * e_mid[p], jnp.where(first, kv[2 * p], kv[2 * p + 1])], 1) for p in P
        ]
        sol = [mm3(inv[h], right[h // 2]) for h in H]
        @pl.when(g == 1)
        def _():
            forward(0)

        low_lane = iota((64, 128), 1) < 64
        solved = [jnp.where(first2, sol[2 * p], sol[2 * p + 1]) for p in P]
        ends = [split(cat([-rem_out[p] * e_end[p], key_out[p] * e_end[p]], 0).T) for p in P]
        made = []
        for p in P:
            wh, wl = split(solved[p])
            lh, ll = ends[p]
            wide = cat([wh, cat([jnp.zeros((T, 128), BF16), valv[p]], 1)], 0)
            made.append(dot(lh, wide) + dot(ll, wide) + dot(lh[:, :T], wl))
        trans = [made[p][:, :128] + eye * e_all[p] for p in P]
        added = [made[p][:, 128:] for p in P]
        for p in P:
            slot = g * quarter + 2 * (p % 2)
            mu[p // 2, slot] = jnp.where(low_lane, trans[p][:64], half_roll(added[p][:64]))
            mu[p // 2, slot + 1] = jnp.where(low_lane, half_roll(trans[p][64:]), added[p][64:])
        swap_maps(g).start()
        for p in P:
            solved_ref[g, p] = solved[p]
            reff[g, p] = read_in[p] * e_mid[p]
            cent[g, p] = read_in[p]
            outer[g, p] = cat([key_out[p], rem_out[p]], 0)
        return carry

    lax.fori_loop(0, 2, half_of_heads, 0)

    def reads_of(i, carry):
        g, side = i // 2, lax.rem(i, 2)
        pairs = [2 * side, 2 * side + 1]
        start = side * (width // 2) + g * (width // 4)
        values = val[:, pl.ds(pl.multiple_of(start, 256), 256)]
        solved = [solved_ref[g, p] for p in pairs]
        inner = [(cent[g, p], outer[g, p]) for p in pairs]
        before = [reff[g, p] for p in pairs]
        scores = [masked_scores(x, *split(o)) for x, o in inner]
        left = [
            split(
                cat(
                    [
                        cat([jnp.where(upto, -a[:, T:], 0.0), jnp.where(upto, a[:, :T], 0.0)], 1)
                        for a in both
                    ],
                    0,
                )
            )
            for both in scores
        ]
        made = []
        for k in range(2):
            wh, wl = split(solved[k])
            zero = jnp.zeros((T, 128), BF16)
            wide = cat([wh, cat([zero, values[:, 128 * k : 128 * k + 128]], 1)], 0)
            lh, ll = left[k]
            made.append(dot(lh, wide) + dot(ll, wide) + dot(lh[:, :T], wl))
        reads = [jnp.where(first2, a[:T], a[T:]) for a in made]
        for k in range(2):
            reff[g, pairs[k]] = before[k] + reads[k][:, :128]
            base_ref[g, pairs[k]] = reads[k][:, 128:]
        return carry

    forward(1)
    lax.fori_loop(0, 4, reads_of, 0)

    maps[chip] = chip_maps[my_slot]
    for step in far:
        source = lax.rem(chip + step, chips)
        pltpu.make_async_remote_copy(
            src_ref=chip_maps.at[0],
            dst_ref=maps.at[source],
            send_sem=s1.at[0, 0],
            recv_sem=r1.at[source],
            device_id={"ctx": base + 2 * source + core},
            device_id_type=MESH,
        ).wait_recv()
    prefix = [maps[d] for d in range(chips)]
    size = 1
    while size < chips:
        lows = list(range(size, chips, 2 * size))
        joined = later_all(
            [cat(prefix[low : low + size], 0) for low in lows], [prefix[low - 1] for low in lows]
        )
        for low, group in zip(lows, joined):
            for d in range(size):
                prefix[low + d] = group[64 * d : 64 * d + 64]
        size *= 2
    row_total[...] = prefix[chips - 1]

    def send_total(r):
        return pltpu.make_async_remote_copy(
            src_ref=row_total,
            dst_ref=row_totals.at[y],
            send_sem=s2.at[r],
            recv_sem=r2.at[y],
            device_id={"ctx": r * n + me},
            device_id_type=MESH,
        )

    for r in range(1, nrow):

        @pl.when(r > y)
        def _():
            send_total(r).start()

    begin = start_ref[...]
    state = cat([begin, begin], 1)
    for r in range(nrow - 1):

        @pl.when(r < y)
        def _():
            pltpu.make_async_remote_copy(
                src_ref=row_total,
                dst_ref=row_totals.at[r],
                send_sem=s2.at[r],
                recv_sem=r2.at[r],
                device_id={"ctx": r * n + me},
                device_id_type=MESH,
            ).wait_recv()

    after_first, others_map = later_all(
        [row_totals[0], row_totals[2]], [state, row_totals[1]]
    )
    others_map = jnp.where(y == 3, others_map, row_totals[1])
    after_rows = later_of(others_map, after_first)
    state = jnp.where(y == 0, state, jnp.where(y == 1, after_first, after_rows))
    after_state = later_of(cat(prefix[: chips - 1], 0), state)
    packs = [pack_state(state)]
    packs += [pack_state(after_state[64 * d - 64 : 64 * d]) for d in range(1, chips)]
    for d in range(chips):
        states[d] = packs[d]
    third = []
    for step, other in enumerate(others):
        copy = pltpu.make_async_remote_copy(
            src_ref=states.at[other],
            dst_ref=got.at[my_slot],
            send_sem=s3.at[step],
            recv_sem=r3.at[my_slot],
            device_id={"ctx": base + 2 * other + core},
            device_id_type=MESH,
        )
        copy.start()
        third.append(copy)
    got[my_slot] = states[chip]

    def swap_states(h):
        part = pl.ds(h * quarter, quarter)
        return pltpu.make_async_remote_copy(
            src_ref=give.at[part],
            dst_ref=starts.at[core, part],
            send_sem=s4.at[h],
            recv_sem=r4.at[h],
            device_id=sibling,
            device_id_type=MESH,
        )

    def take(h):
        slots = [h * quarter + i for i in range(quarter)]
        for slot in slots:

            @pl.when(slot != my_slot)
            def _():
                pltpu.make_async_remote_copy(
                    src_ref=states.at[0],
                    dst_ref=got.at[slot],
                    send_sem=s3.at[0],
                    recv_sem=r3.at[slot],
                    device_id=sibling,
                    device_id_type=MESH,
                ).wait_recv()

        packed = [got[slot] for slot in slots]
        full = [cat([half_roll(a), a], 0) for a in packed]
        moved = later_all([first_maps[slot] for slot in slots], full)
        next_packed = [pack_state(a) for a in moved]
        for i, slot in enumerate(slots):
            give[slot] = jnp.where(core == 0, next_packed[i], packed[i])
        swap_states(h).start()
        for i, slot in enumerate(slots):
            starts[core, slot] = jnp.where(core == 0, packed[i], next_packed[i])

    lane = iota((64, 128), 1) < 64
    mean64 = (half.astype(F32) / 64).astype(BF16)
    mean2 = cat([mean64, mean64], 0)

    def finish(side, h):
        Q = range(2)
        state = []
        for q in Q:
            a, b = [starts[side, h * quarter + 2 * q + k] for k in range(2)]
            both_a = cat([a, half_roll(a)], 0)
            both_b = cat([half_roll(b), b], 0)
            state.append(
                cat([jnp.where(lane, both_a, 0.0), jnp.where(lane, 0.0, both_b)], 0)
            )
        place = [(h, 2 * side + q) for q in Q]
        read = [mm3(reff[place[q]], state[q]) + base_ref[place[q]] for q in Q]
        centered = [a - dot(cat(split(a), 1), mean2) for a in read]
        var = [dot(cat(split(a * a), 1), mean2) for a in centered]
        normed = [(a * lax.rsqrt(b + 0.00064)).astype(BF16) for a, b in zip(centered, var)]
        for q in Q:
            start = side * (width // 2) + h * (width // 4) + 128 * q
            out[:, pl.ds(pl.multiple_of(start, 128), 128)] = normed[q]

    def settle(h, carry):
        take(h)
        finish(core, h)
        swap_states(h).wait_recv()
        finish(other_core, h)
        return carry

    lax.fori_loop(0, 2, settle, 0)

    for h in range(2):
        swap_maps(h).wait_send()
        for k in range(quarter):
            to, copy = send_map(h, k)

            @pl.when(to != chip)
            def _():
                copy.wait_send()

    for r in range(1, nrow):

        @pl.when(r > y)
        def _():
            send_total(r).wait_send()

    for copy in [shift, swap_states(0), swap_states(1)] + scatter + edges + spread + third:
        copy.wait_send()


def mixed_of(x, mix, down, du, ru, db, rb, rec, key, val, start, nctx, nhead):
    T, width = x.shape
    n = start.shape[0]
    chips = n // 2
    nrow = nctx // n
    dma, vm = pltpu.SemaphoreType.DMA, pltpu.VMEM
    args = (x, mix, down, du, ru, db, rb, rec, key, val, start)
    return pl.pallas_call(
        functools.partial(mixed_kernel, nctx=nctx, nhead=nhead),
        in_specs=[pl.BlockSpec(memory_space=pl.ANY)] * len(args),
        out_specs=pl.BlockSpec(memory_space=pltpu.VMEM),
        out_shape=pltpu.VMEM((T, width), BF16),
        scratch_shapes=[vm(a.shape, a.dtype) for a in args[:-1]]
        + [vm((64, 64), F32), dma((len(args),))]
        + [
            vm((16, width), BF16),
            vm((T, 256), F32),
            vm((nhead - 1, T // nhead, 256), F32),
            vm((T, 256), BF16),
            dma((2 * nhead,)),
            dma((2 * nhead,)),
            vm((16, 256), F32),
            vm((nhead - 1, 8, 256), F32),
            vm((T, 256), BF16),
            dma((nhead - 1,)),
            dma((nhead - 1,)),
            vm((T, width), F32),
            vm((2, chips, 64, 128), F32),
            vm((2, PAIRS, T, 128), F32),
            vm((2, PAIRS, 2 * T, 128), F32),
            vm((2, PAIRS, T, 256), F32),
            vm((2, PAIRS, T, 128), F32),
            vm((2, PAIRS, T, 128), F32),
            vm((2, chips, 32, 128), F32),
            vm((chips, 64, 128), F32),
            vm((chips, 64, 128), F32),
            vm((chips, 64, 128), F32),
            vm((chips, 64, 128), F32),
            vm((64, 128), F32),
            vm((nrow, 64, 128), F32),
            vm((chips, 32, 128), F32),
            vm((chips, 32, 128), F32),
            vm((chips, 32, 128), F32),
        ]
        + [dma((2,)), dma((2,)), dma((2, chips // 2)), dma((chips,)), dma((nrow,)), dma((nrow,))]
        + [dma((chips,)), dma((chips,)), dma((2,)), dma((2,))],
        compiler_params=pltpu.CompilerParams(
            collective_id=0, has_side_effects=True, vmem_limit_bytes=40 * 1024 * 1024
        ),
    )(*[pltpu.with_memory_space_constraint(a, pltpu.HBM) for a in args])


def solution(mesh):
    nctx, nhead = mesh.shape["ctx"], mesh.shape["head"]

    def on_device(x, mix, down, du, ru, db, rb, rec, key, val, start):
        return mixed_of(
            x, mix[None], down, du, ru, db[None], rb[None], rec, key, val, start, nctx, nhead
        )

    P = jax.sharding.PartitionSpec
    both, wide = P("ctx", "head"), P("head")
    return jax.shard_map(
        on_device,
        mesh=mesh,
        in_specs=(both, wide, P("head", None), P(None, "head"), P(None, "head"), wide, wide)
        + (both,) * 3
        + (P("head", None, None),),
        out_specs=both,
        check_vma=False,
    )
```
